512 devices in a mesh: net: 64 (over z, x_lo, core), hyd: 8 (over x_hi, y).
Axes of the slice: x: 4 (x_hi: 2, x_lo: 2; x = x_hi * 2 + x_lo), y: 4, z: 16, core: 2. Of those that a mesh axis runs over, the one named last changes fastest.
Arguments:
- diagonal: float32 [32768], P('net'), may hold values from 0.1 to 1
- edge_ends: int32 [40960, 2], P('net'), may hold values from 0 to 511, as said below
- edge_cond: float32 [40960], P('net'), may hold values from 0.3 to 3
- bnd_nodes: int32 [64, 2, 64], P('net'), may hold values from 0 to 511
- bnd_cond: float32 [64, 2, 64], P('net'), may hold values from 0 to 3, as said below
- hyd_ids: int32 [2048], P('hyd'), may hold values from 0 to 32767
- warm_start: float32 [32768, 2048], P('net', 'hyd'), may hold values from -6 to 6
- scen_picks: int32 [1024, 4], replicated, may hold values from 0 to 2047
- scen_flows: float32 [1024, 4], replicated, may hold values from 0.5 to 2
Outputs:
- responses: float32 [32768, 2048], P('net', 'hyd')
- heads: float32 [1024, 32768], P('hyd', 'net')
The draws below stay inside these ranges and needn't reach their ends.
Inputs may be any that keep to these rules, and one draw needn't show every extreme that they name: `edge_ends`: in each partition's block of 640 rows the first 511 rows join all the partition's nodes in one path; no row joins a node to itself. `bnd_cond`: entry [p, 1, k] equals entry [p + 1, 0, k]; row 0 of the first partition and row 1 of the last are zero, all other entries positive.
All inputs are finite; a program needn't handle non-finite values.
Results may differ from the reference program's by a relative error of at most 0.0003.
Values sent between devices are 32-bit elements; how exact they have to be, the bound alone decides.
A program may use at most 64 MiB of HBM per device.

```python
import math
import jax
import jax.numpy as jnp
from jax import lax

NODE_DEV = 512
BND = 64
BLK = 256
PICK = 4
ITERS = 2
EDGE_DEV = 640
NODES = 32768
HYD = 2048
SCEN = 1024
N_NET = 64


def draw_edge_ends(key, part):
    partitions = NODES // NODE_DEV
    extra = NODE_DEV // 4 + 1

    def one_partition(index):
        sub = jax.random.fold_in(key, index)
        key_perm = jax.random.fold_in(sub, 11)
        key_start = jax.random.fold_in(sub, 12)
        key_offset = jax.random.fold_in(sub, 13)
        order = jax.random.permutation(key_perm, NODE_DEV).astype(jnp.int32)
        path = jnp.stack([order[:-1], order[1:]], axis=1)
        starts = jax.random.randint(key_start, (extra,), 0, NODE_DEV).astype(jnp.int32)
        shifts = jax.random.randint(key_offset, (extra,), 1, NODE_DEV).astype(jnp.int32)
        ends = (starts + shifts) % NODE_DEV
        return jnp.concatenate([path, jnp.stack([starts, ends], axis=1)], axis=0)
    every = jax.vmap(one_partition)(jnp.arange(partitions, dtype=jnp.int32))
    return every.reshape(partitions * EDGE_DEV, 2)


def draw_bnd_cond(key, part):
    partitions = NODES // NODE_DEV
    conduct = jnp.exp(jax.random.uniform(key, (partitions, BND), jnp.float32, jnp.log(0.3), jnp.log(3.0)))
    keep = (jnp.arange(partitions) < partitions - 1).astype(jnp.float32)
    upper = conduct * keep[:, None]
    lower = jnp.concatenate([jnp.zeros((1, BND), jnp.float32), upper[:-1]], axis=0)
    return jnp.stack([lower, upper], axis=1)


def draw_warm_start(key, part):
    position = jnp.arange(NODES, dtype=jnp.float32) / NODES
    rising = jnp.exp(jnp.log(3.0) * position)[:, None]
    key_main = jax.random.fold_in(key, 21)
    values = 0.5 * jax.random.normal(key_main, (NODES, HYD), jnp.float32) * rising
    return jnp.clip(values, -6.0, 6.0)


def set_ends(array, rng, least, largest):
    index_at = [jax.random.randint(jax.random.fold_in(rng, axis), (), 0, length) for axis, length in enumerate(array.shape)]
    main_axis = array.shape.index(max(array.shape))
    beside = index_at[:main_axis] + [(index_at[main_axis] + 1) % array.shape[main_axis]] + index_at[main_axis + 1:]
    return array.at[tuple(index_at)].set(least).at[tuple(beside)].set(largest)


def block_scale(rng, extent, shards, least, high):
    factor_of, own = 1.0, jax.random.fold_in(rng, 6)
    for axis_at, blocks in shards:
        heights = jnp.exp(jax.random.uniform(jax.random.fold_in(own, axis_at), (blocks,), jnp.float32, least / len(shards), high / len(shards)))
        factor_of = factor_of * jnp.repeat(heights, extent[axis_at] // blocks).reshape([-1 if axis == axis_at else 1 for axis in range(len(extent))])
    return factor_of


def setup_inputs(seed: int = 0) -> dict:
    key_list = jax.random.split(jax.random.key(seed), 10)
    diagonal = jnp.clip(jnp.exp(math.log(1.0) - 2.3025851 * jax.random.uniform(key_list[0], (NODES,), jnp.float32) ** block_scale(key_list[0], (NODES,), ((0, 64),), -0.2, 0.2)), 0.1, 1.0)
    edge_ends = draw_edge_ends(jax.random.fold_in(key_list[9], 71), 0)
    edge_cond = jnp.clip(jnp.exp(math.log(3.0) - 2.3025851 * jax.random.uniform(key_list[2], (N_NET * EDGE_DEV,), jnp.float32) ** block_scale(key_list[2], (N_NET * EDGE_DEV,), ((0, 64),), -0.2, 0.2)), 0.3, 3.0)
    bnd_nodes = set_ends(jax.random.randint(key_list[3], (N_NET, 2, BND), 0, NODE_DEV), jax.random.fold_in(key_list[3], 1), 0, NODE_DEV - 1).astype(jnp.int32)
    bnd_cond = draw_bnd_cond(jax.random.fold_in(key_list[9], 71), 0)
    hyd_ids = set_ends(jax.random.randint(key_list[5], (HYD,), 0, NODES), jax.random.fold_in(key_list[5], 1), 0, NODES - 1).astype(jnp.int32)
    warm_start = draw_warm_start(jax.random.fold_in(key_list[9], 71), 0)
    scen_picks = set_ends(jax.random.randint(key_list[7], (SCEN, PICK), 0, HYD), jax.random.fold_in(key_list[7], 1), 0, HYD - 1).astype(jnp.int32)
    scen_flows = jnp.clip(jnp.exp(jax.random.uniform(key_list[8], (SCEN, PICK), jnp.float32, math.log(0.5), math.log(2.0))), 0.5, 2.0)
    return dict(diagonal=diagonal, edge_ends=edge_ends, edge_cond=edge_cond, bnd_nodes=bnd_nodes, bnd_cond=bnd_cond, hyd_ids=hyd_ids, warm_start=warm_start, scen_picks=scen_picks, scen_flows=scen_flows)


def apply_matrix(values, diagonal, edge_ends, edge_cond, bnd_nodes, bnd_cond):
    count = values.shape[0]
    partitions = count // NODE_DEV
    offsets = jnp.arange(partitions, dtype=jnp.int32) * NODE_DEV
    edge_base = jnp.repeat(offsets, EDGE_DEV)
    source = edge_ends[:, 0] + edge_base
    target = edge_ends[:, 1] + edge_base
    flux = edge_cond[:, None] * (values[source] - values[target])
    result = diagonal[:, None] * values
    result = result + jax.ops.segment_sum(flux, source, count) - jax.ops.segment_sum(flux, target, count)
    upper = (bnd_nodes[:-1, 1, :] + offsets[:-1, None]).reshape(-1)
    lower = (bnd_nodes[1:, 0, :] + offsets[1:, None]).reshape(-1)
    bnd_flux = bnd_cond[:-1, 1, :].reshape(-1)[:, None] * (values[upper] - values[lower])
    result = result.at[upper].add(bnd_flux)
    result = result.at[lower].add(-bnd_flux)
    return result

def gram_of(first_m, second_m):
    return lax.dot_general(first_m, second_m, (((0,), (0,)), ((), ())), precision=lax.Precision.HIGHEST)

def times_of(first_m, second_m):
    return jnp.dot(first_m, second_m, precision=lax.Precision.HIGHEST)

def solve_spd(matrix, rhs_m):
    factor = jnp.linalg.cholesky(matrix)
    return jax.scipy.linalg.cho_solve((factor, True), rhs_m)

def reference(diagonal, edge_ends, edge_cond, bnd_nodes, bnd_cond, hyd_ids, warm_start, scen_picks, scen_flows):
    nodes = warm_start.shape[0]
    node_iota = jnp.arange(nodes, dtype=jnp.int32)

    def operator(values):
        return apply_matrix(values, diagonal, edge_ends, edge_cond, bnd_nodes, bnd_cond)

    def solve_block(block):
        start = (block * BLK).astype(jnp.int32)
        iterate = lax.dynamic_slice_in_dim(warm_start, start, BLK, 1)
        ids_block = lax.dynamic_slice_in_dim(hyd_ids, start, BLK, 0)
        demand = (node_iota[:, None] == ids_block[None, :]).astype(jnp.float32)
        residual = demand - operator(iterate)
        direction = residual
        res_gram = gram_of(residual, residual)
        for sweep in range(ITERS):
            image = operator(direction)
            dir_gram = gram_of(direction, image)
            alpha_m = solve_spd(dir_gram, res_gram)
            iterate = iterate + times_of(direction, alpha_m)
            residual = residual - times_of(image, alpha_m)
            if sweep + 1 < ITERS:
                new_gram = gram_of(residual, residual)
                beta_m = solve_spd(res_gram, new_gram)
                direction = residual + times_of(direction, beta_m)
                res_gram = new_gram
        return iterate
    blocks = lax.map(solve_block, jnp.arange(HYD // BLK, dtype=jnp.int32))
    responses = jnp.transpose(blocks, (1, 0, 2)).reshape(nodes, HYD)
    hyd_iota = jnp.arange(HYD, dtype=jnp.int32)
    scenario = jnp.zeros((HYD, SCEN), jnp.float32)
    for slot in range(PICK):
        scenario = scenario + scen_flows[:, slot][None, :] * (hyd_iota[:, None] == scen_picks[:, slot][None, :]).astype(jnp.float32)
    heads = lax.dot_general(scenario, responses, (((0,), (1,)), ((), ())), precision=lax.Precision.HIGHEST)
    return (responses, heads)
```

```python
import functools

import jax
import jax.numpy as jnp
from jax import lax
from jax.experimental import pallas as pl
from jax.experimental.pallas import tpu as pltpu
from jax.sharding import PartitionSpec as P

MESH = pl.DeviceIdType.MESH
F32 = jnp.float32
BF16 = jnp.bfloat16
NN = (((1,), (0,)), ((), ()))
TN = (((0,), (0,)), ((), ()))
NT = (((1,), (1,)), ((), ()))
PICK = 4


def pieces(value, count):
    out = []
    for step in range(count):
        part = value.astype(BF16)
        out.append(part)
        if step + 1 < count:
            value = value - part.astype(F32)
    return out


def dot_pieces(first, second, dims):
    depth = max(len(first), len(second))
    total = None
    for level in reversed(range(depth)):
        for i, left in enumerate(first):
            j = level - i
            if 0 <= j < len(second):
                term = lax.dot_general(left, second[j], dims, preferred_element_type=F32)
                total = term if total is None else total + term
    return total


def dot_full(first, second, dims=NN):
    return lax.dot_general(
        first, second, dims, precision=lax.Precision.HIGHEST, preferred_element_type=F32
    )


def dot_one(first, second):
    return lax.dot_general(
        first.astype(BF16), second.astype(BF16), NN, preferred_element_type=F32
    )


def moments_kernel(
    nz,
    diag_ref,
    ends_ref,
    cond_ref,
    bn_ref,
    bc_ref,
    hid_ref,
    x_ref,
    r_ref,
    q_ref,
    t_out,
    d_out,
    a_ref,
    halo_src,
    halo_dst,
    t_buf,
    d_buf,
    core_t,
    core_d,
    acc_t,
    acc_d,
    zr_t,
    zr_d,
    xs,
    xr,
    halo_ss,
    halo_rs,
    core_ss,
    core_rs,
    zr_ss,
    zr_rs,
    x_ss,
    x_rs,
    ag_ss,
    ag_rs,
    fin_ss,
    fin_rs,
):
    nodes, cols = x_ref.shape
    edges = cond_ref.shape[1]
    rim = bn_ref.shape[1]
    n_net = 4 * nz
    net = lax.axis_index("net")
    z = net // 4
    x_lo = lax.rem(net // 2, 2)
    core = lax.rem(net, 2)
    up, down = lax.rem(net + 1, n_net), lax.rem(net + n_net - 1, n_net)
    core_mate = net + 1 - 2 * core
    x_mate = net + 2 - 4 * x_lo

    def z_mate(step):
        return lax.rem(net + 4 * step, n_net)

    barrier = pltpu.get_barrier_semaphore()
    order = sorted(range(1, nz), key=lambda s: -min(s, nz - s))
    mates = [z_mate(s) for s in order] + [x_mate, up, down]
    for mate in mates:
        pl.semaphore_signal(barrier, inc=1, device_id={"net": mate}, device_id_type=MESH)

    def remote(src, dst, ss, rs, mate):
        return pltpu.make_async_remote_copy(
            src_ref=src,
            dst_ref=dst,
            send_sem=ss,
            recv_sem=rs,
            device_id={"net": mate},
            device_id_type=MESH,
        )

    node_iota = lax.broadcasted_iota(jnp.int32, (nodes, edges), 0)
    first = node_iota == ends_ref[0:1, :]
    second = node_iota == ends_ref[1:2, :]
    incidence = first.astype(F32) - second.astype(F32)
    ids = jnp.concatenate([bn_ref[0:1, :], bn_ref[1:2, :]], axis=1)
    conds = jnp.concatenate([bc_ref[0:1, :], bc_ref[1:2, :]], axis=1)
    pick = (lax.broadcasted_iota(jnp.int32, (nodes, 2 * rim), 0) == ids).astype(F32)
    pick_b = [pick.astype(BF16)]
    x_parts = pieces(x_ref[...], 3)

    def gather(parts, stage):
        halo_src[stage] = dot_pieces(pick_b, parts, TN)

    gather(x_parts, 0)
    incidence_b = incidence.astype(BF16)
    total = None
    for part in reversed(pieces(cond_ref[...], 3)):
        term = lax.dot_general(
            (incidence * part.astype(F32)).astype(BF16), incidence_b, NT, preferred_element_type=F32
        )
        total = term if total is None else total + term
    for part in reversed(pieces(conds, 3)):
        total = total + lax.dot_general(
            (pick * part.astype(F32)).astype(BF16), pick_b[0], NT, preferred_element_type=F32
        )
    square = lax.broadcasted_iota(jnp.int32, (nodes, nodes), 0) == lax.broadcasted_iota(
        jnp.int32, (nodes, nodes), 1
    )
    a_ref[...] = total + jnp.where(square, diag_ref[...], 0.0)
    couple = pieces(pick * conds, 3)

    pl.semaphore_wait(barrier, len(mates))

    def halo(stage):
        upper, lower = pl.ds(rim, rim), pl.ds(0, rim)
        return [
            remote(
                halo_src.at[stage, upper],
                halo_dst.at[stage, lower],
                halo_ss.at[2 * stage],
                halo_rs.at[2 * stage],
                up,
            ),
            remote(
                halo_src.at[stage, lower],
                halo_dst.at[stage, upper],
                halo_ss.at[2 * stage + 1],
                halo_rs.at[2 * stage + 1],
                down,
            ),
        ]

    def local(parts):
        return dot_pieces(pieces(a_ref[...], 3), parts, NN)

    def coupled(stage):
        return dot_pieces(couple, pieces(halo_dst[stage], 3), NN)

    halos = [halo(stage) for stage in range(3)]
    for copy in halos[0]:
        copy.start()
    hyd_local = hid_ref[...] - net * nodes
    demand = (lax.broadcasted_iota(jnp.int32, (nodes, cols), 0) == hyd_local).astype(F32)
    part_r = demand - local(x_parts)
    for copy in halos[0]:
        copy.wait_recv()
    residual = part_r + coupled(0)
    r_parts = pieces(residual, 3)
    gather(r_parts, 1)
    for copy in halos[1]:
        copy.start()
    r_ref[...] = residual
    part_q = local(r_parts)
    m0 = dot_pieces(r_parts, r_parts, TN)
    for copy in halos[1]:
        copy.wait_recv()
    image = part_q - coupled(1)
    q_parts = pieces(image, 3)
    gather(q_parts, 2)
    for copy in halos[2]:
        copy.start()
    q_ref[...] = image

    row = lax.broadcasted_iota(jnp.int32, (cols, cols), 0)
    col = lax.broadcasted_iota(jnp.int32, (cols, cols), 1)

    half = cols // 2
    chunk = half // nz

    def pack(lot, upper_m, lower_m):
        t_buf[lot] = jnp.where(row <= col, upper_m, lower_m)
        diagonal = jnp.sum(jnp.where(row == col, lower_m, 0.0), axis=0, keepdims=True)
        d_buf[lot] = jnp.broadcast_to(diagonal, (8, cols))

    def core_copies(lot):
        other = pl.ds(pl.multiple_of((1 - core) * half, half), half)
        return [
            remote(
                t_buf.at[lot, other],
                core_t.at[lot],
                core_ss.at[2 * lot],
                core_rs.at[2 * lot],
                core_mate,
            ),
            remote(
                d_buf.at[lot],
                core_d.at[lot],
                core_ss.at[2 * lot + 1],
                core_rs.at[2 * lot + 1],
                core_mate,
            ),
        ]

    def core_sum(lot):
        mine = pl.ds(pl.multiple_of(core * half, half), half)
        acc_t[lot] = t_buf[lot, mine] + core_t[lot]
        acc_d[lot] = d_buf[lot] + core_d[lot]

    owner_z = [nz // 4, (3 * nz) // 4]

    def z_copies(lot):
        out = []
        for step in order:
            owner = lax.rem(z + step, nz)
            rows = pl.ds(pl.multiple_of(owner * chunk, chunk), chunk)
            out.append(
                remote(
                    acc_t.at[lot, rows],
                    zr_t.at[lot, step - 1],
                    zr_ss.at[lot, step - 1],
                    zr_rs.at[lot, step - 1],
                    z_mate(step),
                )
            )
        return out

    def d_copy(lot, slot, mate):
        return remote(
            acc_d.at[lot],
            zr_d.at[lot, slot],
            zr_ss.at[lot, nz - 1],
            zr_rs.at[lot, nz - 1 + slot],
            mate,
        )

    def z_start(lot):
        for copy in z_copies(lot):
            copy.start()
        to_owner = lax.rem(owner_z[lot] - z + nz, nz)

        @pl.when(to_owner != 0)
        def _():
            d_copy(lot, to_owner - 1, lax.rem(net + 4 * to_owner, n_net)).start()

    def x_copy(lot):
        return remote(xs.at[lot], xr.at[lot], x_ss.at[lot], x_rs.at[lot], x_mate)

    def z_sum(lot):
        for copy in z_copies(lot):
            copy.wait_recv()
        mine = pl.ds(pl.multiple_of(z * chunk, chunk), chunk)
        total = acc_t[lot, mine]
        for step in range(1, nz):
            total = total + zr_t[lot, step - 1]
        xs[lot, 0:chunk] = total
        xs[lot, chunk : chunk + 8] = acc_d[lot]

        @pl.when(z == owner_z[lot])
        def _():
            total_d = acc_d[lot]
            for slot in range(nz - 1):
                d_copy(lot, slot, z_mate(slot + 1)).wait_recv()
            for slot in range(nz - 1):
                total_d = total_d + zr_d[lot, slot]
            xs[lot, chunk : chunk + 8] = total_d

        x_copy(lot).start()

    def full_rows(index):
        return pl.ds(pl.multiple_of(core * half + index * chunk, chunk), chunk)

    def ag_copies(lot, received):
        out = []
        for step in order:
            owner = lax.rem(z + nz - step, nz) if received else z
            out.append(
                remote(
                    t_out.at[lot, full_rows(owner)],
                    t_out.at[lot, full_rows(owner)],
                    ag_ss.at[lot, step - 1],
                    ag_rs.at[lot, step - 1],
                    z_mate(step),
                )
            )
        return out

    def agd_copy(lot, step):
        return remote(
            d_out.at[lot],
            d_out.at[lot],
            ag_ss.at[lot, nz - 1 + step - 1],
            ag_rs.at[lot, nz - 1],
            z_mate(step),
        )

    def x_sum(lot):
        x_copy(lot).wait_recv()
        t_out[lot, full_rows(z)] = xs[lot, 0:chunk] + xr[lot, 0:chunk]

        @pl.when(z == owner_z[lot])
        def _():
            d_out[lot] = xs[lot, chunk : chunk + 8] + xr[lot, chunk : chunk + 8]
            for step in order:
                agd_copy(lot, step).start()

        for copy in ag_copies(lot, False):
            copy.start()

    def fin_copy(lot, whose):
        rows = pl.ds(pl.multiple_of(whose * half, half), half)
        return remote(
            t_out.at[lot, rows], t_out.at[lot, rows], fin_ss.at[lot], fin_rs.at[lot], core_mate
        )

    def ag_finish(lot):
        for copy in ag_copies(lot, True):
            copy.wait_recv()
        fin_copy(lot, core).start()

        @pl.when(z != owner_z[lot])
        def _():
            agd_copy(lot, 1).wait_recv()

    def finish(lot):
        fin_copy(lot, 1 - core).wait_recv()

    def drain(lot):
        for copy in core_copies(lot):
            copy.wait_send()
        for copy in z_copies(lot):
            copy.wait_send()
        x_copy(lot).wait_send()
        for copy in ag_copies(lot, False):
            copy.wait_send()
        fin_copy(lot, core).wait_send()

        @pl.when(z != owner_z[lot])
        def _():
            d_copy(lot, 0, z_mate(1)).wait_send()

        @pl.when(z == owner_z[lot])
        def _():
            for step in order:
                agd_copy(lot, step).wait_send()

    pack(0, m0, dot_pieces(r_parts, q_parts, TN))
    for copy in core_copies(0):
        copy.start()
    part_w = local(q_parts)
    for copy in core_copies(0):
        copy.wait_recv()
    core_sum(0)
    z_start(0)
    m2 = dot_pieces(q_parts, q_parts, TN)
    for copy in halos[2]:
        copy.wait_recv()
    m3 = dot_pieces(q_parts, pieces(part_w - coupled(2), 3), TN)
    pack(1, m2, m3)
    for copy in core_copies(1):
        copy.start()
    for copy in core_copies(1):
        copy.wait_recv()
    core_sum(1)
    z_start(1)
    z_sum(0)
    x_sum(0)
    z_sum(1)
    x_sum(1)
    ag_finish(0)
    ag_finish(1)
    finish(0)
    finish(1)
    for stage in halos:
        for copy in stage:
            copy.wait_send()
    drain(0)
    drain(1)


def moments(diagonal, edge_ends, edge_cond, bnd_nodes, bnd_cond, hyd_ids, warm_start, n_net):
    nz = n_net // 4
    nodes, cols = warm_start.shape
    rim = bnd_nodes.shape[2]
    chunk = cols // 2 // nz
    dma = pltpu.SemaphoreType.DMA
    vmem = pl.BlockSpec(memory_space=pltpu.VMEM)
    return pl.pallas_call(
        functools.partial(moments_kernel, nz),
        name="moments",
        out_shape=[
            jax.ShapeDtypeStruct((nodes, cols), F32),
            jax.ShapeDtypeStruct((nodes, cols), F32),
            jax.ShapeDtypeStruct((2, cols, cols), F32),
            jax.ShapeDtypeStruct((2, 8, cols), F32),
        ],
        in_specs=[vmem] * 7,
        out_specs=[vmem] * 4,
        scratch_shapes=[
            pltpu.VMEM((nodes, nodes), F32),
            pltpu.VMEM((3, 2 * rim, cols), F32),
            pltpu.VMEM((3, 2 * rim, cols), F32),
            pltpu.VMEM((2, cols, cols), F32),
            pltpu.VMEM((2, 8, cols), F32),
            pltpu.VMEM((2, cols // 2, cols), F32),
            pltpu.VMEM((2, 8, cols), F32),
            pltpu.VMEM((2, cols // 2, cols), F32),
            pltpu.VMEM((2, 8, cols), F32),
            pltpu.VMEM((2, nz - 1, chunk, cols), F32),
            pltpu.VMEM((2, nz - 1, 8, cols), F32),
            pltpu.VMEM((2, chunk + 8, cols), F32),
            pltpu.VMEM((2, chunk + 8, cols), F32),
            dma((6,)),
            dma((6,)),
            dma((4,)),
            dma((4,)),
            dma((2, nz)),
            dma((2, 2 * nz - 2)),
            dma((2,)),
            dma((2,)),
            dma((2, 2 * nz - 2)),
            dma((2, nz)),
            dma((2,)),
            dma((2,)),
        ],
        compiler_params=pltpu.CompilerParams(
            collective_id=0, has_side_effects=True, vmem_limit_bytes=48 << 20
        ),
    )(
        diagonal[None, :],
        edge_ends.T,
        edge_cond[None, :],
        bnd_nodes[0],
        bnd_cond[0],
        hyd_ids[None, :],
        warm_start,
    )


def update_kernel(x_ref, r_ref, q_ref, t_ref, d_ref, out_ref, inv_ref):
    size = t_ref.shape[1]
    row = lax.broadcasted_iota(jnp.int32, (size, size), 0)
    col = lax.broadcasted_iota(jnp.int32, (size, size), 1)
    eye = (row == col).astype(F32)

    def unpack(lot):
        packed = t_ref[lot]
        upper = jnp.where(row < col, packed, 0.0)
        lower = jnp.where(row > col, packed, 0.0)
        first = jnp.where(row <= col, packed, 0.0) + upper.T
        second = lower + lower.T + eye * d_ref[lot, 0:1, :]
        return first, second

    def inverse(matrix):
        diag = eye * matrix
        by_row = lax.rsqrt(jnp.sum(diag, axis=1, keepdims=True))
        by_col = lax.rsqrt(jnp.sum(diag, axis=0, keepdims=True))
        scaled = matrix * by_row * by_col
        bound = jnp.max(jnp.sum(jnp.abs(scaled), axis=0, keepdims=True), axis=1, keepdims=True)
        gain = 2.0 / bound
        start = eye * gain
        error = eye - scaled * gain
        approx = start + error * gain
        for _ in range(5):
            error = dot_one(error, error)
            approx = approx + dot_one(approx, error)
        rest = eye - dot_full(scaled, approx)
        size_of = jnp.sum(rest * rest)
        good = size_of < 0.25
        inv_ref[...] = jnp.where(good, approx + dot_full(approx, rest), start)

        def unfinished(state):
            step, size_of = state
            return jnp.logical_and(step < 64, jnp.logical_not(size_of < 1e-6))

        def improve(state):
            approx = inv_ref[...]
            rest = eye - dot_full(scaled, approx)
            inv_ref[...] = approx + dot_full(approx, rest)
            return state[0] + 1, jnp.sum(rest * rest)

        lax.while_loop(unfinished, improve, (jnp.int32(0), size_of))
        return inv_ref[...] * by_row * by_col

    m0, m1 = unpack(0)
    m2, m3 = unpack(1)
    inv1 = inverse(m1)
    alpha = dot_full(inv1, m0)
    cross = dot_full(inv1, m2)
    schur = m3 - dot_full(m2, cross)
    rhs = m1 - dot_full(m2, alpha)
    weight_q = dot_full(inverse(schur), rhs)
    weight_r = alpha - dot_full(cross, weight_q)
    out_ref[...] = (
        x_ref[...]
        + dot_pieces(pieces(r_ref[...], 3), pieces(weight_r, 3), NN)
        + dot_pieces(pieces(q_ref[...], 3), pieces(weight_q, 3), NN)
    )


def update(warm_start, residual, image, packed, diagonals):
    cols = warm_start.shape[1]
    vmem = pl.BlockSpec(memory_space=pltpu.VMEM)
    return pl.pallas_call(
        update_kernel,
        name="update",
        out_shape=jax.ShapeDtypeStruct(warm_start.shape, F32),
        in_specs=[vmem] * 5,
        out_specs=vmem,
        scratch_shapes=[pltpu.VMEM((cols, cols), F32)],
        compiler_params=pltpu.CompilerParams(vmem_limit_bytes=48 << 20),
    )(warm_start, residual, image, packed, diagonals)


def heads_kernel(groups, x_ref, picks_ref, flows_ref, out_ref, src, dst, ss, rs):
    nodes, cols = x_ref.shape
    scen = out_ref.shape[0]
    hyd = lax.axis_index("hyd")
    order = sorted(range(1, groups), key=lambda s: -min(s % 4, 4 - s % 4) - 2 * (s >= 4))
    order = order[: groups - 1]

    def mate(step):
        return lax.rem(hyd + step, groups)

    barrier = pltpu.get_barrier_semaphore()
    for step in order:
        pl.semaphore_signal(barrier, inc=1, device_id={"hyd": mate(step)}, device_id_type=MESH)

    x_parts = pieces(x_ref[...], 3)
    column = lax.broadcasted_iota(jnp.int32, (cols, scen), 0) + hyd * cols

    def scenario(owner):
        lanes = pl.ds(pl.multiple_of(owner * scen, scen), scen)
        picks, flows = picks_ref[:, lanes], flows_ref[:, lanes]
        total = jnp.zeros((cols, scen), F32)
        for slot in range(PICK):
            total = total + jnp.where(
                column == picks[slot : slot + 1, :], flows[slot : slot + 1, :], 0.0
            )
        return total

    def copy(step):
        return pltpu.make_async_remote_copy(
            src_ref=src.at[step],
            dst_ref=dst.at[step],
            send_sem=ss.at[step],
            recv_sem=rs.at[step],
            device_id={"hyd": mate(step)},
            device_id_type=MESH,
        )

    every = order + [0]
    waited = False
    for at in range(0, len(every), 2):
        pair = every[at : at + 2]
        block = jnp.concatenate([scenario(mate(step)) for step in pair], axis=1)
        both = dot_pieces(x_parts, pieces(block, 3), NN)
        for i, step in enumerate(pair):
            src[step] = both[:, i * scen : (i + 1) * scen]
        if not waited:
            pl.semaphore_wait(barrier, len(order))
            waited = True
        for step in pair:
            if step:
                copy(step).start()
    total = src[0]
    for step in order:
        copy(step).wait_recv()
    for step in order:
        total = total + dst[step]
    out_ref[...] = total.T
    for step in order:
        copy(step).wait_send()


def heads_of(responses, picks, flows, groups):
    nodes, cols = responses.shape
    scen = picks.shape[0] // groups
    dma = pltpu.SemaphoreType.DMA
    vmem = pl.BlockSpec(memory_space=pltpu.VMEM)
    return pl.pallas_call(
        functools.partial(heads_kernel, groups),
        name="heads",
        out_shape=jax.ShapeDtypeStruct((scen, nodes), F32),
        in_specs=[vmem] * 3,
        out_specs=vmem,
        scratch_shapes=[
            pltpu.VMEM((groups, nodes, scen), F32),
            pltpu.VMEM((groups, nodes, scen), F32),
            dma((groups,)),
            dma((groups,)),
        ],
        compiler_params=pltpu.CompilerParams(
            collective_id=1, has_side_effects=True, vmem_limit_bytes=48 << 20
        ),
    )(responses, picks.T, flows.T)


def per_device(
    diagonal, edge_ends, edge_cond, bnd_nodes, bnd_cond, hyd_ids, warm_start, scen_picks, scen_flows
):
    residual, image, packed, diagonals = moments(
        diagonal,
        edge_ends,
        edge_cond,
        bnd_nodes,
        bnd_cond,
        hyd_ids,
        warm_start,
        lax.axis_size("net"),
    )
    responses = update(warm_start, residual, image, packed, diagonals)
    heads = heads_of(responses, scen_picks, scen_flows, lax.axis_size("hyd"))
    return responses, heads


def solution(mesh):
    placed = (
        P("net"),
        P("net", None),
        P("net"),
        P("net", None, None),
        P("net", None, None),
        P("hyd"),
        P("net", "hyd"),
        P(),
        P(),
    )
    return jax.shard_map(
        per_device,
        mesh=mesh,
        in_specs=placed,
        out_specs=(P("net", "hyd"), P("hyd", "net")),
        check_vma=False,
    )
```

```python
import functools

import jax
import jax.numpy as jnp
from jax import lax
from jax.experimental import pallas as pl
from jax.experimental.pallas import tpu as pltpu
from jax.sharding import PartitionSpec as P

MESH = pl.DeviceIdType.MESH
F32 = jnp.float32
BF16 = jnp.bfloat16
NN = (((1,), (0,)), ((), ()))
TN = (((0,), (0,)), ((), ()))
NT = (((1,), (1,)), ((), ()))
PICK = 4


def pieces(value, count):
    out = []
    for step in range(count):
        part = value.astype(BF16)
        out.append(part)
        if step + 1 < count:
            value = value - part.astype(F32)
    return out


def dot_pieces(first, second, dims):
    depth = max(len(first), len(second))
    total = None
    for level in reversed(range(depth)):
        for i, left in enumerate(first):
            j = level - i
            if 0 <= j < len(second):
                term = lax.dot_general(left, second[j], dims, preferred_element_type=F32)
                total = term if total is None else total + term
    return total


def dot_full(first, second, dims=NN):
    return lax.dot_general(
        first, second, dims, precision=lax.Precision.HIGHEST, preferred_element_type=F32
    )


def dot_one(first, second):
    return lax.dot_general(
        first.astype(BF16), second.astype(BF16), NN, preferred_element_type=F32
    )


def moments_kernel(
    nz,
    diag_ref,
    ends_ref,
    cond_ref,
    bn_ref,
    bc_ref,
    hid_ref,
    x_ref,
    r_ref,
    q_ref,
    t_out,
    d_out,
    a_ref,
    halo_src,
    halo_dst,
    t_buf,
    d_buf,
    core_t,
    core_d,
    acc_t,
    acc_d,
    zr_t,
    zr_d,
    xs,
    xr,
    halo_ss,
    halo_rs,
    core_ss,
    core_rs,
    zr_ss,
    zr_rs,
    x_ss,
    x_rs,
    ag_ss,
    ag_rs,
    fin_ss,
    fin_rs,
):
    nodes, cols = x_ref.shape
    edges = cond_ref.shape[1]
    rim = bn_ref.shape[1]
    n_net = 4 * nz
    net = lax.axis_index("net")
    z = net // 4
    x_lo = lax.rem(net // 2, 2)
    core = lax.rem(net, 2)
    up, down = lax.rem(net + 1, n_net), lax.rem(net + n_net - 1, n_net)
    core_mate = net + 1 - 2 * core
    x_mate = net + 2 - 4 * x_lo

    def z_mate(step):
        return lax.rem(net + 4 * step, n_net)

    barrier = pltpu.get_barrier_semaphore()
    order = sorted(range(1, nz), key=lambda s: -min(s, nz - s))
    mates = [z_mate(s) for s in order] + [x_mate, up, down]
    for mate in mates:
        pl.semaphore_signal(barrier, inc=1, device_id={"net": mate}, device_id_type=MESH)

    def remote(src, dst, ss, rs, mate):
        return pltpu.make_async_remote_copy(
            src_ref=src,
            dst_ref=dst,
            send_sem=ss,
            recv_sem=rs,
            device_id={"net": mate},
            device_id_type=MESH,
        )

    node_iota = lax.broadcasted_iota(jnp.int32, (nodes, edges), 0)
    first = node_iota == ends_ref[0:1, :]
    second = node_iota == ends_ref[1:2, :]
    incidence = first.astype(F32) - second.astype(F32)
    ids = jnp.concatenate([bn_ref[0:1, :], bn_ref[1:2, :]], axis=1)
    conds = jnp.concatenate([bc_ref[0:1, :], bc_ref[1:2, :]], axis=1)
    pick = (lax.broadcasted_iota(jnp.int32, (nodes, 2 * rim), 0) == ids).astype(F32)
    pick_b = [pick.astype(BF16)]
    x_parts = pieces(x_ref[...], 3)

    def gather(parts, stage):
        halo_src[stage] = dot_pieces(pick_b, parts, TN)

    gather(x_parts, 0)
    incidence_b = incidence.astype(BF16)
    total = None
    for part in reversed(pieces(cond_ref[...], 3)):
        term = lax.dot_general(
            (incidence * part.astype(F32)).astype(BF16), incidence_b, NT, preferred_element_type=F32
        )
        total = term if total is None else total + term
    for part in reversed(pieces(conds, 3)):
        total = total + lax.dot_general(
            (pick * part.astype(F32)).astype(BF16), pick_b[0], NT, preferred_element_type=F32
        )
    square = lax.broadcasted_iota(jnp.int32, (nodes, nodes), 0) == lax.broadcasted_iota(
        jnp.int32, (nodes, nodes), 1
    )
    a_ref[...] = total + jnp.where(square, diag_ref[...], 0.0)
    couple = pieces(pick * conds, 3)

    pl.semaphore_wait(barrier, len(mates))

    def halo(stage):
        upper, lower = pl.ds(rim, rim), pl.ds(0, rim)
        return [
            remote(
                halo_src.at[stage, upper],
                halo_dst.at[stage, lower],
                halo_ss.at[2 * stage],
                halo_rs.at[2 * stage],
                up,
            ),
            remote(
                halo_src.at[stage, lower],
                halo_dst.at[stage, upper],
                halo_ss.at[2 * stage + 1],
                halo_rs.at[2 * stage + 1],
                down,
            ),
        ]

    def local(parts):
        return dot_pieces(pieces(a_ref[...], 3), parts, NN)

    def coupled(stage):
        return dot_pieces(couple, pieces(halo_dst[stage], 3), NN)

    halos = [halo(stage) for stage in range(3)]
    for copy in halos[0]:
        copy.start()
    hyd_local = hid_ref[...] - net * nodes
    demand = (lax.broadcasted_iota(jnp.int32, (nodes, cols), 0) == hyd_local).astype(F32)
    part_r = demand - local(x_parts)
    for copy in halos[0]:
        copy.wait_recv()
    residual = part_r + coupled(0)
    r_parts = pieces(residual, 3)
    gather(r_parts, 1)
    for copy in halos[1]:
        copy.start()
    r_ref[...] = residual
    part_q = local(r_parts)
    m0 = dot_pieces(r_parts, r_parts, TN)
    for copy in halos[1]:
        copy.wait_recv()
    image = part_q - coupled(1)
    q_parts = pieces(image, 3)
    gather(q_parts, 2)
    for copy in halos[2]:
        copy.start()
    q_ref[...] = image

    row = lax.broadcasted_iota(jnp.int32, (cols, cols), 0)
    col = lax.broadcasted_iota(jnp.int32, (cols, cols), 1)

    half = cols // 2
    chunk = half // nz

    def pack(lot, upper_m, lower_m):
        t_buf[lot] = jnp.where(row <= col, upper_m, lower_m)
        diagonal = jnp.sum(jnp.where(row == col, lower_m, 0.0), axis=0, keepdims=True)
        d_buf[lot] = jnp.broadcast_to(diagonal, (8, cols))

    def core_copies(lot):
        other = pl.ds(pl.multiple_of((1 - core) * half, half), half)
        return [
            remote(
                t_buf.at[lot, other],
                core_t.at[lot],
                core_ss.at[2 * lot],
                core_rs.at[2 * lot],
                core_mate,
            ),
            remote(
                d_buf.at[lot],
                core_d.at[lot],
                core_ss.at[2 * lot + 1],
                core_rs.at[2 * lot + 1],
                core_mate,
            ),
        ]

    def core_sum(lot):
        mine = pl.ds(pl.multiple_of(core * half, half), half)
        acc_t[lot] = t_buf[lot, mine] + core_t[lot]
        acc_d[lot] = d_buf[lot] + core_d[lot]

    owner_z = [nz // 4, (3 * nz) // 4]

    def z_copies(lot):
        out = []
        for step in order:
            owner = lax.rem(z + step, nz)
            rows = pl.ds(pl.multiple_of(owner * chunk, chunk), chunk)
            out.append(
                remote(
                    acc_t.at[lot, rows],
                    zr_t.at[lot, step - 1],
                    zr_ss.at[lot, step - 1],
                    zr_rs.at[lot, step - 1],
                    z_mate(step),
                )
            )
        return out

    def d_copy(lot, slot, mate):
        return remote(
            acc_d.at[lot],
            zr_d.at[lot, slot],
            zr_ss.at[lot, nz - 1],
            zr_rs.at[lot, nz - 1 + slot],
            mate,
        )

    def z_start(lot):
        for copy in z_copies(lot):
            copy.start()
        to_owner = lax.rem(owner_z[lot] - z + nz, nz)

        @pl.when(to_owner != 0)
        def _():
            d_copy(lot, to_owner - 1, lax.rem(net + 4 * to_owner, n_net)).start()

    def x_copy(lot):
        return remote(xs.at[lot], xr.at[lot], x_ss.at[lot], x_rs.at[lot], x_mate)

    def z_sum(lot):
        for copy in z_copies(lot):
            copy.wait_recv()
        mine = pl.ds(pl.multiple_of(z * chunk, chunk), chunk)
        total = acc_t[lot, mine]
        for step in range(1, nz):
            total = total + zr_t[lot, step - 1]
        xs[lot, 0:chunk] = total
        xs[lot, chunk : chunk + 8] = acc_d[lot]

        @pl.when(z == owner_z[lot])
        def _():
            total_d = acc_d[lot]
            for slot in range(nz - 1):
                d_copy(lot, slot, z_mate(slot + 1)).wait_recv()
            for slot in range(nz - 1):
                total_d = total_d + zr_d[lot, slot]
            xs[lot, chunk : chunk + 8] = total_d

        x_copy(lot).start()

    def full_rows(index):
        return pl.ds(pl.multiple_of(core * half + index * chunk, chunk), chunk)

    def ag_copies(lot, received):
        out = []
        for step in order:
            owner = lax.rem(z + nz - step, nz) if received else z
            out.append(
                remote(
                    t_out.at[lot, full_rows(owner)],
                    t_out.at[lot, full_rows(owner)],
                    ag_ss.at[lot, step - 1],
                    ag_rs.at[lot, step - 1],
                    z_mate(step),
                )
            )
        return out

    def agd_copy(lot, step):
        return remote(
            d_out.at[lot],
            d_out.at[lot],
            ag_ss.at[lot, nz - 1 + step - 1],
            ag_rs.at[lot, nz - 1],
            z_mate(step),
        )

    def x_sum(lot):
        x_copy(lot).wait_recv()
        t_out[lot, full_rows(z)] = xs[lot, 0:chunk] + xr[lot, 0:chunk]

        @pl.when(z == owner_z[lot])
        def _():
            d_out[lot] = xs[lot, chunk : chunk + 8] + xr[lot, chunk : chunk + 8]
            for step in order:
                agd_copy(lot, step).start()

        for copy in ag_copies(lot, False):
            copy.start()

    def fin_copy(lot, whose):
        rows = pl.ds(pl.multiple_of(whose * half, half), half)
        return remote(
            t_out.at[lot, rows], t_out.at[lot, rows], fin_ss.at[lot], fin_rs.at[lot], core_mate
        )

    def ag_finish(lot):
        for copy in ag_copies(lot, True):
            copy.wait_recv()
        fin_copy(lot, core).start()

        @pl.when(z != owner_z[lot])
        def _():
            agd_copy(lot, 1).wait_recv()

    def finish(lot):
        fin_copy(lot, 1 - core).wait_recv()

    def drain(lot):
        for copy in core_copies(lot):
            copy.wait_send()
        for copy in z_copies(lot):
            copy.wait_send()
        x_copy(lot).wait_send()
        for copy in ag_copies(lot, False):
            copy.wait_send()
        fin_copy(lot, core).wait_send()

        @pl.when(z != owner_z[lot])
        def _():
            d_copy(lot, 0, z_mate(1)).wait_send()

        @pl.when(z == owner_z[lot])
        def _():
            for step in order:
                agd_copy(lot, step).wait_send()

    pack(0, m0, dot_pieces(r_parts, q_parts, TN))
    for copy in core_copies(0):
        copy.start()
    part_w = local(q_parts)
    for copy in core_copies(0):
        copy.wait_recv()
    core_sum(0)
    z_start(0)
    m2 = dot_pieces(q_parts, q_parts, TN)
    for copy in halos[2]:
        copy.wait_recv()
    m3 = dot_pieces(q_parts, pieces(part_w - coupled(2), 3), TN)
    pack(1, m2, m3)
    for copy in core_copies(1):
        copy.start()
    for copy in core_copies(1):
        copy.wait_recv()
    core_sum(1)
    z_start(1)
    z_sum(0)
    x_sum(0)
    z_sum(1)
    x_sum(1)
    ag_finish(0)
    ag_finish(1)
    finish(0)
    finish(1)
    for stage in halos:
        for copy in stage:
            copy.wait_send()
    drain(0)
    drain(1)


def moments(diagonal, edge_ends, edge_cond, bnd_nodes, bnd_cond, hyd_ids, warm_start, n_net):
    nz = n_net // 4
    nodes, cols = warm_start.shape
    rim = bnd_nodes.shape[2]
    chunk = cols // 2 // nz
    dma = pltpu.SemaphoreType.DMA
    vmem = pl.BlockSpec(memory_space=pltpu.VMEM)
    return pl.pallas_call(
        functools.partial(moments_kernel, nz),
        name="moments",
        out_shape=[
            jax.ShapeDtypeStruct((nodes, cols), F32),
            jax.ShapeDtypeStruct((nodes, cols), F32),
            jax.ShapeDtypeStruct((2, cols, cols), F32),
            jax.ShapeDtypeStruct((2, 8, cols), F32),
        ],
        in_specs=[vmem] * 7,
        out_specs=[vmem] * 4,
        scratch_shapes=[
            pltpu.VMEM((nodes, nodes), F32),
            pltpu.VMEM((3, 2 * rim, cols), F32),
            pltpu.VMEM((3, 2 * rim, cols), F32),
            pltpu.VMEM((2, cols, cols), F32),
            pltpu.VMEM((2, 8, cols), F32),
            pltpu.VMEM((2, cols // 2, cols), F32),
            pltpu.VMEM((2, 8, cols), F32),
            pltpu.VMEM((2, cols // 2, cols), F32),
            pltpu.VMEM((2, 8, cols), F32),
            pltpu.VMEM((2, nz - 1, chunk, cols), F32),
            pltpu.VMEM((2, nz - 1, 8, cols), F32),
            pltpu.VMEM((2, chunk + 8, cols), F32),
            pltpu.VMEM((2, chunk + 8, cols), F32),
            dma((6,)),
            dma((6,)),
            dma((4,)),
            dma((4,)),
            dma((2, nz)),
            dma((2, 2 * nz - 2)),
            dma((2,)),
            dma((2,)),
            dma((2, 2 * nz - 2)),
            dma((2, nz)),
            dma((2,)),
            dma((2,)),
        ],
        compiler_params=pltpu.CompilerParams(
            collective_id=0, has_side_effects=True, vmem_limit_bytes=48 << 20
        ),
    )(
        diagonal[None, :],
        edge_ends.T,
        edge_cond[None, :],
        bnd_nodes[0],
        bnd_cond[0],
        hyd_ids[None, :],
        warm_start,
    )


def update_kernel(x_ref, r_ref, q_ref, t_ref, d_ref, out_ref, inv_ref):
    size = t_ref.shape[1]
    row = lax.broadcasted_iota(jnp.int32, (size, size), 0)
    col = lax.broadcasted_iota(jnp.int32, (size, size), 1)
    eye = (row == col).astype(F32)

    def unpack(lot):
        packed = t_ref[lot]
        upper = jnp.where(row < col, packed, 0.0)
        lower = jnp.where(row > col, packed, 0.0)
        first = jnp.where(row <= col, packed, 0.0) + upper.T
        second = lower + lower.T + eye * d_ref[lot, 0:1, :]
        return first, second

    def inverse(matrix):
        diag = eye * matrix
        by_row = lax.rsqrt(jnp.sum(diag, axis=1, keepdims=True))
        by_col = lax.rsqrt(jnp.sum(diag, axis=0, keepdims=True))
        scaled = matrix * by_row * by_col
        bound = jnp.max(jnp.sum(jnp.abs(scaled), axis=0, keepdims=True), axis=1, keepdims=True)
        gain = 2.0 / bound
        start = eye * gain
        error = eye - scaled * gain
        approx = start + error * gain
        for _ in range(5):
            error = dot_one(error, error)
            approx = approx + dot_one(approx, error)
        rest = eye - dot_full(scaled, approx)
        size_of = jnp.sum(rest * rest)
        good = size_of < 0.25
        inv_ref[...] = jnp.where(good, approx + dot_full(approx, rest), start)

        def unfinished(state):
            step, size_of = state
            return jnp.logical_and(step < 64, jnp.logical_not(size_of < 1e-6))

        def improve(state):
            approx = inv_ref[...]
            rest = eye - dot_full(scaled, approx)
            inv_ref[...] = approx + dot_full(approx, rest)
            return state[0] + 1, jnp.sum(rest * rest)

        lax.while_loop(unfinished, improve, (jnp.int32(0), size_of))
        return inv_ref[...] * by_row * by_col

    m0, m1 = unpack(0)
    m2, m3 = unpack(1)
    inv1 = inverse(m1)
    alpha = dot_full(inv1, m0)
    cross = dot_full(inv1, m2)
    schur = m3 - dot_full(m2, cross)
    rhs = m1 - dot_full(m2, alpha)
    weight_q = dot_full(inverse(schur), rhs)
    weight_r = alpha - dot_full(cross, weight_q)
    out_ref[...] = (
        x_ref[...]
        + dot_pieces(pieces(r_ref[...], 3), pieces(weight_r, 3), NN)
        + dot_pieces(pieces(q_ref[...], 3), pieces(weight_q, 3), NN)
    )


def update(warm_start, residual, image, packed, diagonals):
    cols = warm_start.shape[1]
    vmem = pl.BlockSpec(memory_space=pltpu.VMEM)
    return pl.pallas_call(
        update_kernel,
        name="update",
        out_shape=jax.ShapeDtypeStruct(warm_start.shape, F32),
        in_specs=[vmem] * 5,
        out_specs=vmem,
        scratch_shapes=[pltpu.VMEM((cols, cols), F32)],
        compiler_params=pltpu.CompilerParams(vmem_limit_bytes=48 << 20),
    )(warm_start, residual, image, packed, diagonals)


def heads_kernel(groups, x_ref, picks_ref, flows_ref, out_ref, src, dst, ss, rs):
    nodes, cols = x_ref.shape
    scen = out_ref.shape[0]
    hyd = lax.axis_index("hyd")
    order = sorted(range(1, groups), key=lambda s: -min(s % 4, 4 - s % 4) - 2 * (s >= 4))
    order = order[: groups - 1]

    def mate(step):
        return lax.rem(hyd + step, groups)

    barrier = pltpu.get_barrier_semaphore()
    for step in order:
        pl.semaphore_signal(barrier, inc=1, device_id={"hyd": mate(step)}, device_id_type=MESH)

    x_parts = pieces(x_ref[...], 3)
    column = lax.broadcasted_iota(jnp.int32, (cols, scen), 0) + hyd * cols

    def scenario(owner):
        lanes = pl.ds(pl.multiple_of(owner * scen, scen), scen)
        picks, flows = picks_ref[:, lanes], flows_ref[:, lanes]
        total = jnp.zeros((cols, scen), F32)
        for slot in range(PICK):
            total = total + jnp.where(
                column == picks[slot : slot + 1, :], flows[slot : slot + 1, :], 0.0
            )
        return total

    def copy(step):
        return pltpu.make_async_remote_copy(
            src_ref=src.at[step],
            dst_ref=dst.at[step],
            send_sem=ss.at[step],
            recv_sem=rs.at[step],
            device_id={"hyd": mate(step)},
            device_id_type=MESH,
        )

    every = order + [0]
    waited = False
    for at in range(0, len(every), 2):
        pair = every[at : at + 2]
        block = jnp.concatenate([scenario(mate(step)) for step in pair], axis=1)
        both = dot_pieces(x_parts, pieces(block, 3), NN)
        for i, step in enumerate(pair):
            src[step] = both[:, i * scen : (i + 1) * scen]
        if not waited:
            pl.semaphore_wait(barrier, len(order))
            waited = True
        for step in pair:
            if step:
                copy(step).start()
    total = src[0]
    for step in order:
        copy(step).wait_recv()
    for step in order:
        total = total + dst[step]
    out_ref[...] = total.T
    for step in order:
        copy(step).wait_send()


def heads_of(responses, picks, flows, groups):
    nodes, cols = responses.shape
    scen = picks.shape[0] // groups
    dma = pltpu.SemaphoreType.DMA
    vmem = pl.BlockSpec(memory_space=pltpu.VMEM)
    return pl.pallas_call(
        functools.partial(heads_kernel, groups),
        name="heads",
        out_shape=jax.ShapeDtypeStruct((scen, nodes), F32),
        in_specs=[vmem] * 3,
        out_specs=vmem,
        scratch_shapes=[
            pltpu.VMEM((groups, nodes, scen), F32),
            pltpu.VMEM((groups, nodes, scen), F32),
            dma((groups,)),
            dma((groups,)),
        ],
        compiler_params=pltpu.CompilerParams(
            collective_id=1, has_side_effects=True, vmem_limit_bytes=48 << 20
        ),
    )(responses, picks.T, flows.T)


def fused_kernel(
    nz,
    groups,
    diag_ref,
    ends_ref,
    cond_ref,
    bn_ref,
    bc_ref,
    hid_ref,
    x_hbm,
    picks_hbm,
    flows_hbm,
    resp_hbm,
    heads_ref,
    flag_ref,
    x_ref,
    picks_ref,
    flows_ref,
    r_ref,
    q_ref,
    x2_ref,
    a_ref,
    halo_src,
    halo_dst,
    t_buf,
    d_buf,
    core_t,
    core_d,
    acc_t,
    acc_d,
    zr_t,
    zr_d,
    t_all,
    d_all,
    part_src,
    part_dst,
    in_sem,
    out_sem,
    know,
    halo_ss,
    halo_rs,
    core_ss,
    core_rs,
    zr_ss,
    zr_rs,
    dr_ss,
    dr_rs,
    ag_ss,
    ag_rs,
    ad_ss,
    ad_rs,
    fin_ss,
    fin_rs,
    part_ss,
    part_rs,
):
    nodes, cols = x_ref.shape
    edges = cond_ref.shape[1]
    rim = bn_ref.shape[1]
    scen = heads_ref.shape[0]
    n_net = 4 * nz
    net = lax.axis_index("net")
    hyd = lax.axis_index("hyd")
    z = net // 4
    x_lo = lax.rem(net // 2, 2)
    core = lax.rem(net, 2)
    up, down = lax.rem(net + 1, n_net), lax.rem(net + n_net - 1, n_net)
    core_mate = net + 1 - 2 * core
    half = cols // 2
    chunk = half // nz

    def net_mate(key):
        return lax.rem(net + 4 * (key // 2) + (key % 2) * (2 - 4 * x_lo) + n_net, n_net)

    def z_mate(step):
        return lax.rem(net + 4 * step + n_net, n_net)

    def hyd_mate(step):
        return lax.rem(hyd + step, groups)

    keys = sorted(range(1, 2 * nz), key=lambda k: -min(k // 2, nz - k // 2))
    steps = sorted(range(1, groups), key=lambda s: -min(s % 4, 4 - s % 4) - 2 * (s >= 4))
    near = [1] + ([2, 3, 2 * nz - 2, 2 * nz - 1] if nz > 2 else [2, 3])
    rounds = []
    reach = 1
    while 2 * reach <= nz // 2:
        rounds.append(reach)
        reach *= 2

    barrier = pltpu.get_barrier_semaphore()
    mates = [{"hyd": hyd_mate(s)} for s in steps]
    mates += [{"net": net_mate(k)} for k in near] + [{"net": up}, {"net": down}]
    for mate in mates:
        pl.semaphore_signal(barrier, inc=1, device_id=mate, device_id_type=MESH)

    loads = [
        pltpu.make_async_copy(x_hbm, x_ref, in_sem.at[0]),
        pltpu.make_async_copy(picks_hbm, picks_ref, in_sem.at[1]),
        pltpu.make_async_copy(flows_hbm, flows_ref, in_sem.at[2]),
    ]
    for load in loads:
        load.start()

    def learn(at):
        for step in (rounds[at], nz - rounds[at]):
            pl.semaphore_signal(
                know.at[at], inc=1, device_id={"net": z_mate(step)}, device_id_type=MESH
            )

    def learned(at):
        pl.semaphore_wait(know.at[at], 2)

    def remote(src, dst, ss, rs, mate):
        return pltpu.make_async_remote_copy(
            src_ref=src,
            dst_ref=dst,
            send_sem=ss,
            recv_sem=rs,
            device_id={"net": mate},
            device_id_type=MESH,
        )

    node_iota = lax.broadcasted_iota(jnp.int32, (nodes, edges), 0)
    first = node_iota == ends_ref[0:1, :]
    second = node_iota == ends_ref[1:2, :]
    incidence = first.astype(F32) - second.astype(F32)
    ids = jnp.concatenate([bn_ref[0:1, :], bn_ref[1:2, :]], axis=1)
    conds = jnp.concatenate([bc_ref[0:1, :], bc_ref[1:2, :]], axis=1)
    pick = (lax.broadcasted_iota(jnp.int32, (nodes, 2 * rim), 0) == ids).astype(F32)
    pick_b = [pick.astype(BF16)]
    couple = pieces(pick * conds, 3)
    incidence_b = incidence.astype(BF16)
    total = None
    for part in reversed(pieces(cond_ref[...], 3)):
        term = lax.dot_general(
            (incidence * part.astype(F32)).astype(BF16), incidence_b, NT, preferred_element_type=F32
        )
        total = term if total is None else total + term
    for part in reversed(pieces(conds, 3)):
        total = total + lax.dot_general(
            (pick * part.astype(F32)).astype(BF16), pick_b[0], NT, preferred_element_type=F32
        )
    square = lax.broadcasted_iota(jnp.int32, (nodes, nodes), 0) == lax.broadcasted_iota(
        jnp.int32, (nodes, nodes), 1
    )
    a_ref[...] = total + jnp.where(square, diag_ref[...], 0.0)

    def gather(parts, stage):
        halo_src[stage] = dot_pieces(pick_b, parts, TN)

    for load in loads:
        load.wait()
    x_parts = pieces(x_ref[...], 3)
    gather(x_parts, 0)

    pl.semaphore_wait(barrier, len(mates))

    def halo(stage):
        upper, lower = pl.ds(rim, rim), pl.ds(0, rim)
        at = 2 * stage
        return [
            remote(
                halo_src.at[stage, upper],
                halo_dst.at[stage, lower],
                halo_ss.at[at],
                halo_rs.at[at],
                up,
            ),
            remote(
                halo_src.at[stage, lower],
                halo_dst.at[stage, upper],
                halo_ss.at[at + 1],
                halo_rs.at[at + 1],
                down,
            ),
        ]

    def local(parts):
        return dot_pieces(pieces(a_ref[...], 3), parts, NN)

    def coupled(stage):
        return dot_pieces(couple, pieces(halo_dst[stage], 3), NN)

    row = lax.broadcasted_iota(jnp.int32, (cols, cols), 0)
    col = lax.broadcasted_iota(jnp.int32, (cols, cols), 1)
    eye = (row == col).astype(F32)

    def pack(lot, upper_m, lower_m):
        t_buf[lot] = jnp.where(row <= col, upper_m, lower_m)
        diagonal = jnp.sum(eye * lower_m, axis=0, keepdims=True)
        d_buf[lot] = jnp.concatenate(
            [diagonal[:, :half], diagonal[:, half:], jnp.zeros((6, half), F32)], axis=0
        )

    def core_copies(lot):
        other = pl.ds(pl.multiple_of((1 - core) * half, half), half)
        at = 2 * lot
        return [
            remote(t_buf.at[lot, other], core_t.at[lot], core_ss.at[at], core_rs.at[at], core_mate),
            remote(
                d_buf.at[lot], core_d.at[lot], core_ss.at[at + 1], core_rs.at[at + 1], core_mate
            ),
        ]

    def core_sum(lot):
        mine = pl.ds(pl.multiple_of(core * half, half), half)
        acc_t[lot] = t_buf[lot, mine] + core_t[lot]
        acc_d[lot] = d_buf[lot] + core_d[lot]

    owner_z = [nz // 4, (3 * nz) // 4]

    def is_owner(lot):
        return jnp.logical_and(z == owner_z[lot], x_lo == 0)

    def spot(zz, xx, base):
        return (
            pl.ds(pl.multiple_of(base + zz * chunk, chunk), chunk),
            pl.ds(pl.multiple_of(xx * half, half), half),
        )

    def share_copies(lot):
        out = []
        for key in keys:
            rows, lanes = spot(
                lax.rem(z + key // 2, nz), (1 - x_lo) if key % 2 else x_lo, 0
            )
            out.append(
                remote(
                    acc_t.at[lot, rows, lanes],
                    zr_t.at[lot, key - 1],
                    zr_ss.at[lot, key - 1],
                    zr_rs.at[lot, key - 1],
                    net_mate(key),
                )
            )
        return out

    def share_d(lot, slot, mate):
        return remote(
            acc_d.at[lot], zr_d.at[lot, slot], dr_ss.at[lot], dr_rs.at[lot, slot], mate
        )

    def share_start(lot):
        for copy in share_copies(lot):
            copy.start()

        @pl.when(jnp.logical_not(is_owner(lot)))
        def _():
            slot = 2 * lax.rem(owner_z[lot] - z + nz, nz) + x_lo - 1
            share_d(lot, slot, 4 * owner_z[lot] + core).start()

    def full_spot(zz, xx):
        return spot(zz, xx, core * half)

    def all_copies(lot, received):
        out = []
        for key in keys:
            if received:
                rows, lanes = full_spot(
                    lax.rem(z + nz - key // 2, nz), (1 - x_lo) if key % 2 else x_lo
                )
            else:
                rows, lanes = full_spot(z, x_lo)
            out.append(
                remote(
                    t_all.at[lot, rows, lanes],
                    t_all.at[lot, rows, lanes],
                    ag_ss.at[lot, key - 1],
                    ag_rs.at[lot, key - 1],
                    net_mate(key),
                )
            )
        return out

    def all_d(lot, key):
        return remote(
            d_all.at[lot], d_all.at[lot], ad_ss.at[lot, key - 1], ad_rs.at[lot], net_mate(key)
        )

    def share_sum(lot):
        for copy in share_copies(lot):
            copy.wait_recv()
        rows, lanes = spot(z, x_lo, 0)
        total = acc_t[lot, rows, lanes]
        for key in range(1, 2 * nz):
            total = total + zr_t[lot, key - 1]
        rows, lanes = full_spot(z, x_lo)
        t_all[lot, rows, lanes] = total
        for copy in all_copies(lot, False):
            copy.start()

        @pl.when(is_owner(lot))
        def _():
            total_d = acc_d[lot]
            for slot in range(2 * nz - 1):
                share_d(lot, slot, core_mate).wait_recv()
            for slot in range(2 * nz - 1):
                total_d = total_d + zr_d[lot, slot]
            d_all[lot] = total_d
            for key in keys:
                all_d(lot, key).start()

    def last_copy(lot, whose):
        rows = pl.ds(pl.multiple_of(whose * half, half), half)
        return remote(
            t_all.at[lot, rows], t_all.at[lot, rows], fin_ss.at[lot], fin_rs.at[lot], core_mate
        )

    def all_finish(lot):
        for copy in all_copies(lot, True):
            copy.wait_recv()
        last_copy(lot, core).start()

        @pl.when(jnp.logical_not(is_owner(lot)))
        def _():
            all_d(lot, 1).wait_recv()

    def drain(lot):
        for copy in core_copies(lot) + share_copies(lot) + all_copies(lot, False):
            copy.wait_send()
        last_copy(lot, core).wait_send()

        @pl.when(jnp.logical_not(is_owner(lot)))
        def _():
            share_d(lot, 0, core_mate).wait_send()

        @pl.when(is_owner(lot))
        def _():
            for key in keys:
                all_d(lot, key).wait_send()

    halos = [halo(stage) for stage in range(3)]
    for copy in halos[0]:
        copy.start()
    if rounds:
        learn(0)
    hyd_local = hid_ref[...] - net * nodes
    demand = (lax.broadcasted_iota(jnp.int32, (nodes, cols), 0) == hyd_local).astype(F32)
    part_r = demand - local(x_parts)
    for at in range(len(rounds)):
        if at == 0:
            learned(0)
            if len(rounds) > 1:
                learn(1)
    for copy in halos[0]:
        copy.wait_recv()
    residual = part_r + coupled(0)
    r_parts = pieces(residual, 3)
    gather(r_parts, 1)
    for copy in halos[1]:
        copy.start()
    r_ref[...] = residual
    part_q = local(r_parts)
    if len(rounds) > 1:
        learned(1)
        if len(rounds) > 2:
            learn(2)
    m0 = dot_pieces(r_parts, r_parts, TN)
    for copy in halos[1]:
        copy.wait_recv()
    image = part_q - coupled(1)
    q_parts = pieces(image, 3)
    gather(q_parts, 2)
    for copy in halos[2]:
        copy.start()
    q_ref[...] = image
    pack(0, m0, dot_pieces(r_parts, q_parts, TN))
    for copy in core_copies(0):
        copy.start()
    part_w = local(q_parts)
    for copy in core_copies(0):
        copy.wait_recv()
    core_sum(0)
    for at in range(2, len(rounds)):
        learned(at)
        if at + 1 < len(rounds):
            learn(at + 1)
    share_start(0)
    m2 = dot_pieces(q_parts, q_parts, TN)
    for copy in halos[2]:
        copy.wait_recv()
    m3 = dot_pieces(q_parts, pieces(part_w - coupled(2), 3), TN)
    pack(1, m2, m3)
    for copy in core_copies(1):
        copy.start()
    for copy in core_copies(1):
        copy.wait_recv()
    core_sum(1)
    share_start(1)
    share_sum(0)
    share_sum(1)
    all_finish(0)
    last_copy(0, 1 - core).wait_recv()

    def unpack(lot):
        packed = t_all[lot]
        upper = jnp.where(row < col, packed, 0.0)
        lower = jnp.where(row > col, packed, 0.0)
        diagonal = jnp.concatenate([d_all[lot, 0:1, :], d_all[lot, 1:2, :]], axis=1)
        return jnp.where(row <= col, packed, 0.0) + upper.T, lower + lower.T + eye * diagonal

    def inverse(matrix):
        diag = eye * matrix
        by_row = lax.rsqrt(jnp.sum(diag, axis=1, keepdims=True))
        by_col = lax.rsqrt(jnp.sum(diag, axis=0, keepdims=True))
        scaled = matrix * by_row * by_col
        bound = jnp.max(jnp.sum(jnp.abs(scaled), axis=0, keepdims=True), axis=1, keepdims=True)
        gain = 2.0 / bound
        error = eye - scaled * gain
        approx = eye * gain + error * gain
        for _ in range(5):
            error = dot_one(error, error)
            approx = approx + dot_one(approx, error)
        approx = approx + dot_one(approx, eye - dot_full(scaled, approx))
        rest = eye - dot_full(scaled, approx)
        approx = approx + dot_one(approx, rest)
        left = jnp.sum(jnp.sum(rest * rest, axis=0, keepdims=True), axis=1, keepdims=True)
        return approx * by_row * by_col, left

    m0, m1 = unpack(0)
    inv1, left1 = inverse(m1)
    alpha = dot_full(inv1, m0)
    all_finish(1)
    last_copy(1, 1 - core).wait_recv()
    m2, m3 = unpack(1)
    cross = dot_full(inv1, m2)
    schur = m3 - dot_full(m2, cross)
    rhs = m1 - dot_full(m2, alpha)
    inv2, left2 = inverse(schur)
    weight_q = dot_full(inv2, rhs)
    weight_r = alpha - dot_full(cross, weight_q)
    converged = jnp.logical_and(left1 < 2e-5, left2 < 2e-5)
    flag = jnp.broadcast_to(jnp.where(converged, 0.0, 1.0), (8, scen))
    answer = (
        x_ref[...]
        + dot_pieces(pieces(r_ref[...], 2), pieces(weight_r, 2), NN)
        + dot_pieces(pieces(q_ref[...], 2), pieces(weight_q, 2), NN)
    )
    x2_ref[...] = answer
    store = pltpu.make_async_copy(x2_ref, resp_hbm, out_sem.at[0])
    store.start()
    a_parts = pieces(answer, 2)
    column = lax.broadcasted_iota(jnp.int32, (cols, scen), 0) + hyd * cols

    def scenario(owner):
        lanes = pl.ds(pl.multiple_of(owner * scen, scen), scen)
        picks, flows = picks_ref[:, lanes], flows_ref[:, lanes]
        total = jnp.zeros((cols, scen), F32)
        for slot in range(PICK):
            total = total + jnp.where(
                column == picks[slot : slot + 1, :], flows[slot : slot + 1, :], 0.0
            )
        return total

    def part_copy(step):
        return pltpu.make_async_remote_copy(
            src_ref=part_src.at[step],
            dst_ref=part_dst.at[step],
            send_sem=part_ss.at[step],
            recv_sem=part_rs.at[step],
            device_id={"hyd": hyd_mate(step)},
            device_id_type=MESH,
        )

    every = steps + [0]
    for at in range(0, groups, 2):
        pair = every[at : at + 2]
        block = jnp.concatenate([scenario(hyd_mate(step)) for step in pair], axis=1)
        both = dot_pieces(a_parts, pieces(block, 2), NN)
        for i, step in enumerate(pair):
            part_src[step, 0:nodes] = both[:, i * scen : (i + 1) * scen]
            part_src[step, nodes : nodes + 8] = flag
            if step:
                part_copy(step).start()
    for stage in halos:
        for copy in stage:
            copy.wait_send()
    drain(0)
    drain(1)
    total = part_src[0]
    for step in steps:
        part_copy(step).wait_recv()
        total = total + part_dst[step]
    heads_ref[...] = total[0:nodes].T
    flag_ref[...] = total[nodes : nodes + 8]
    store.wait()
    for step in steps:
        part_copy(step).wait_send()


def fused(
    diagonal,
    edge_ends,
    edge_cond,
    bnd_nodes,
    bnd_cond,
    hyd_ids,
    warm_start,
    picks,
    flows,
    n_net,
    groups,
):
    nz = n_net // 4
    nodes, cols = warm_start.shape
    rim = bnd_nodes.shape[2]
    scen = picks.shape[0] // groups
    half = cols // 2
    chunk = half // nz
    peers = 2 * nz - 1
    dma = pltpu.SemaphoreType.DMA
    vmem = pl.BlockSpec(memory_space=pltpu.VMEM)
    anywhere = pl.BlockSpec(memory_space=pl.ANY)
    return pl.pallas_call(
        functools.partial(fused_kernel, nz, groups),
        name="fused",
        out_shape=[
            jax.ShapeDtypeStruct((nodes, cols), F32),
            jax.ShapeDtypeStruct((scen, nodes), F32),
            jax.ShapeDtypeStruct((8, scen), F32),
        ],
        in_specs=[vmem] * 6 + [anywhere] * 3,
        out_specs=[anywhere, vmem, vmem],
        scratch_shapes=[
            pltpu.VMEM((nodes, cols), F32),
            pltpu.VMEM((PICK, scen * groups), jnp.int32),
            pltpu.VMEM((PICK, scen * groups), F32),
            pltpu.VMEM((nodes, cols), F32),
            pltpu.VMEM((nodes, cols), F32),
            pltpu.VMEM((nodes, cols), F32),
            pltpu.VMEM((nodes, nodes), F32),
            pltpu.VMEM((3, 2 * rim, cols), F32),
            pltpu.VMEM((3, 2 * rim, cols), F32),
            pltpu.VMEM((2, cols, cols), F32),
            pltpu.VMEM((2, 8, half), F32),
            pltpu.VMEM((2, half, cols), F32),
            pltpu.VMEM((2, 8, half), F32),
            pltpu.VMEM((2, half, cols), F32),
            pltpu.VMEM((2, 8, half), F32),
            pltpu.VMEM((2, peers, chunk, half), F32),
            pltpu.VMEM((2, peers, 8, half), F32),
            pltpu.VMEM((2, cols, cols), F32),
            pltpu.VMEM((2, 8, half), F32),
            pltpu.VMEM((groups, nodes + 8, scen), F32),
            pltpu.VMEM((groups, nodes + 8, scen), F32),
            dma((3,)),
            dma((1,)),
            pltpu.SemaphoreType.REGULAR((3,)),
            dma((6,)),
            dma((6,)),
            dma((4,)),
            dma((4,)),
            dma((2, peers)),
            dma((2, peers)),
            dma((2,)),
            dma((2, peers)),
            dma((2, peers)),
            dma((2, peers)),
            dma((2, peers)),
            dma((2,)),
            dma((2,)),
            dma((2,)),
            dma((groups,)),
            dma((groups,)),
        ],
        compiler_params=pltpu.CompilerParams(
            collective_id=2, has_side_effects=True, vmem_limit_bytes=48 << 20
        ),
    )(
        diagonal[None, :],
        edge_ends.T,
        edge_cond[None, :],
        bnd_nodes[0],
        bnd_cond[0],
        hyd_ids[None, :],
        warm_start,
        picks.T,
        flows.T,
    )


def per_device(
    diagonal, edge_ends, edge_cond, bnd_nodes, bnd_cond, hyd_ids, warm_start, scen_picks, scen_flows
):
    n_net, groups = lax.axis_size("net"), lax.axis_size("hyd")
    local = (diagonal, edge_ends, edge_cond, bnd_nodes, bnd_cond, hyd_ids, warm_start)
    responses, heads, flag = fused(*local, scen_picks, scen_flows, n_net, groups)

    def keep(responses, heads):
        return responses, heads

    def redo(responses, heads):
        residual, image, packed, diagonals = moments(*local, n_net)
        responses = update(warm_start, residual, image, packed, diagonals)
        return responses, heads_of(responses, scen_picks, scen_flows, groups)

    return lax.cond(flag[0, 0] > 0.0, redo, keep, responses, heads)


def solution(mesh):
    placed = (
        P("net"),
        P("net", None),
        P("net"),
        P("net", None, None),
        P("net", None, None),
        P("hyd"),
        P("net", "hyd"),
        P(),
        P(),
    )
    return jax.shard_map(
        per_device,
        mesh=mesh,
        in_specs=placed,
        out_specs=(P("net", "hyd"), P("hyd", "net")),
        check_vma=False,
    )
```

```python
import functools

import jax
import jax.numpy as jnp
from jax import lax
from jax.experimental import pallas as pl
from jax.experimental.pallas import tpu as pltpu
from jax.sharding import PartitionSpec as P

MESH = pl.DeviceIdType.MESH
F32 = jnp.float32
BF16 = jnp.bfloat16
NN = (((1,), (0,)), ((), ()))
TN = (((0,), (0,)), ((), ()))
NT = (((1,), (1,)), ((), ()))
PICK = 4
SPLIT = 38
CROSS_FIRST = (0, 1)
CROSS_LAST = (0, 1)


def pieces(value, count):
    out = []
    for step in range(count):
        part = value.astype(BF16)
        out.append(part)
        if step + 1 < count:
            value = value - part.astype(F32)
    return out


def dot_pieces(first, second, dims):
    depth = max(len(first), len(second))
    total = None
    for level in reversed(range(depth)):
        for i, left in enumerate(first):
            j = level - i
            if 0 <= j < len(second):
                term = lax.dot_general(left, second[j], dims, preferred_element_type=F32)
                total = term if total is None else total + term
    return total


def dot_full(first, second, dims=NN):
    return lax.dot_general(
        first, second, dims, precision=lax.Precision.HIGHEST, preferred_element_type=F32
    )


def dot_one(first, second):
    return lax.dot_general(
        first.astype(BF16), second.astype(BF16), NN, preferred_element_type=F32
    )


def moments_kernel(
    nz,
    diag_ref,
    ends_ref,
    cond_ref,
    bn_ref,
    bc_ref,
    hid_ref,
    x_ref,
    r_ref,
    q_ref,
    t_out,
    d_out,
    a_ref,
    halo_src,
    halo_dst,
    t_buf,
    d_buf,
    core_t,
    core_d,
    acc_t,
    acc_d,
    zr_t,
    zr_d,
    xs,
    xr,
    halo_ss,
    halo_rs,
    core_ss,
    core_rs,
    zr_ss,
    zr_rs,
    x_ss,
    x_rs,
    ag_ss,
    ag_rs,
    fin_ss,
    fin_rs,
):
    nodes, cols = x_ref.shape
    edges = cond_ref.shape[1]
    rim = bn_ref.shape[1]
    n_net = 4 * nz
    net = lax.axis_index("net")
    z = net // 4
    x_lo = lax.rem(net // 2, 2)
    core = lax.rem(net, 2)
    up, down = lax.rem(net + 1, n_net), lax.rem(net + n_net - 1, n_net)
    core_mate = net + 1 - 2 * core
    x_mate = net + 2 - 4 * x_lo

    def z_mate(step):
        return lax.rem(net + 4 * step, n_net)

    barrier = pltpu.get_barrier_semaphore()
    order = sorted(range(1, nz), key=lambda s: -min(s, nz - s))
    mates = [z_mate(s) for s in order] + [x_mate, up, down]
    for mate in mates:
        pl.semaphore_signal(barrier, inc=1, device_id={"net": mate}, device_id_type=MESH)

    def remote(src, dst, ss, rs, mate):
        return pltpu.make_async_remote_copy(
            src_ref=src,
            dst_ref=dst,
            send_sem=ss,
            recv_sem=rs,
            device_id={"net": mate},
            device_id_type=MESH,
        )

    node_iota = lax.broadcasted_iota(jnp.int32, (nodes, edges), 0)
    first = node_iota == ends_ref[0:1, :]
    second = node_iota == ends_ref[1:2, :]
    incidence = first.astype(F32) - second.astype(F32)
    ids = jnp.concatenate([bn_ref[0:1, :], bn_ref[1:2, :]], axis=1)
    conds = jnp.concatenate([bc_ref[0:1, :], bc_ref[1:2, :]], axis=1)
    pick = (lax.broadcasted_iota(jnp.int32, (nodes, 2 * rim), 0) == ids).astype(F32)
    pick_b = [pick.astype(BF16)]
    x_parts = pieces(x_ref[...], 3)

    def gather(parts, stage):
        halo_src[stage] = dot_pieces(pick_b, parts, TN)

    gather(x_parts, 0)
    incidence_b = incidence.astype(BF16)
    total = None
    for part in reversed(pieces(cond_ref[...], 3)):
        term = lax.dot_general(
            (incidence * part.astype(F32)).astype(BF16), incidence_b, NT, preferred_element_type=F32
        )
        total = term if total is None else total + term
    for part in reversed(pieces(conds, 3)):
        total = total + lax.dot_general(
            (pick * part.astype(F32)).astype(BF16), pick_b[0], NT, preferred_element_type=F32
        )
    square = lax.broadcasted_iota(jnp.int32, (nodes, nodes), 0) == lax.broadcasted_iota(
        jnp.int32, (nodes, nodes), 1
    )
    a_ref[...] = total + jnp.where(square, diag_ref[...], 0.0)
    couple = pieces(pick * conds, 3)

    pl.semaphore_wait(barrier, len(mates))

    def halo(stage):
        upper, lower = pl.ds(rim, rim), pl.ds(0, rim)
        return [
            remote(
                halo_src.at[stage, upper],
                halo_dst.at[stage, lower],
                halo_ss.at[2 * stage],
                halo_rs.at[2 * stage],
                up,
            ),
            remote(
                halo_src.at[stage, lower],
                halo_dst.at[stage, upper],
                halo_ss.at[2 * stage + 1],
                halo_rs.at[2 * stage + 1],
                down,
            ),
        ]

    def local(parts):
        return dot_pieces(pieces(a_ref[...], 3), parts, NN)

    def coupled(stage):
        return dot_pieces(couple, pieces(halo_dst[stage], 3), NN)

    halos = [halo(stage) for stage in range(3)]
    for copy in halos[0]:
        copy.start()
    hyd_local = hid_ref[...] - net * nodes
    demand = (lax.broadcasted_iota(jnp.int32, (nodes, cols), 0) == hyd_local).astype(F32)
    part_r = demand - local(x_parts)
    for copy in halos[0]:
        copy.wait_recv()
    residual = part_r + coupled(0)
    r_parts = pieces(residual, 3)
    gather(r_parts, 1)
    for copy in halos[1]:
        copy.start()
    r_ref[...] = residual
    part_q = local(r_parts)
    m0 = dot_pieces(r_parts, r_parts, TN)
    for copy in halos[1]:
        copy.wait_recv()
    image = part_q - coupled(1)
    q_parts = pieces(image, 3)
    gather(q_parts, 2)
    for copy in halos[2]:
        copy.start()
    q_ref[...] = image

    row = lax.broadcasted_iota(jnp.int32, (cols, cols), 0)
    col = lax.broadcasted_iota(jnp.int32, (cols, cols), 1)

    half = cols // 2
    chunk = half // nz

    def pack(lot, upper_m, lower_m):
        t_buf[lot] = jnp.where(row <= col, upper_m, lower_m)
        diagonal = jnp.sum(jnp.where(row == col, lower_m, 0.0), axis=0, keepdims=True)
        d_buf[lot] = jnp.broadcast_to(diagonal, (8, cols))

    def core_copies(lot):
        other = pl.ds(pl.multiple_of((1 - core) * half, half), half)
        return [
            remote(
                t_buf.at[lot, other],
                core_t.at[lot],
                core_ss.at[2 * lot],
                core_rs.at[2 * lot],
                core_mate,
            ),
            remote(
                d_buf.at[lot],
                core_d.at[lot],
                core_ss.at[2 * lot + 1],
                core_rs.at[2 * lot + 1],
                core_mate,
            ),
        ]

    def core_sum(lot):
        mine = pl.ds(pl.multiple_of(core * half, half), half)
        acc_t[lot] = t_buf[lot, mine] + core_t[lot]
        acc_d[lot] = d_buf[lot] + core_d[lot]

    owner_z = [nz // 4, (3 * nz) // 4]

    def z_copies(lot):
        out = []
        for step in order:
            owner = lax.rem(z + step, nz)
            rows = pl.ds(pl.multiple_of(owner * chunk, chunk), chunk)
            out.append(
                remote(
                    acc_t.at[lot, rows],
                    zr_t.at[lot, step - 1],
                    zr_ss.at[lot, step - 1],
                    zr_rs.at[lot, step - 1],
                    z_mate(step),
                )
            )
        return out

    def d_copy(lot, slot, mate):
        return remote(
            acc_d.at[lot],
            zr_d.at[lot, slot],
            zr_ss.at[lot, nz - 1],
            zr_rs.at[lot, nz - 1 + slot],
            mate,
        )

    def z_start(lot):
        for copy in z_copies(lot):
            copy.start()
        to_owner = lax.rem(owner_z[lot] - z + nz, nz)

        @pl.when(to_owner != 0)
        def _():
            d_copy(lot, to_owner - 1, lax.rem(net + 4 * to_owner, n_net)).start()

    def x_copy(lot):
        return remote(xs.at[lot], xr.at[lot], x_ss.at[lot], x_rs.at[lot], x_mate)

    def z_sum(lot):
        for copy in z_copies(lot):
            copy.wait_recv()
        mine = pl.ds(pl.multiple_of(z * chunk, chunk), chunk)
        total = acc_t[lot, mine]
        for step in range(1, nz):
            total = total + zr_t[lot, step - 1]
        xs[lot, 0:chunk] = total
        xs[lot, chunk : chunk + 8] = acc_d[lot]

        @pl.when(z == owner_z[lot])
        def _():
            total_d = acc_d[lot]
            for slot in range(nz - 1):
                d_copy(lot, slot, z_mate(slot + 1)).wait_recv()
            for slot in range(nz - 1):
                total_d = total_d + zr_d[lot, slot]
            xs[lot, chunk : chunk + 8] = total_d

        x_copy(lot).start()

    def full_rows(index):
        return pl.ds(pl.multiple_of(core * half + index * chunk, chunk), chunk)

    def ag_copies(lot, received):
        out = []
        for step in order:
            owner = lax.rem(z + nz - step, nz) if received else z
            out.append(
                remote(
                    t_out.at[lot, full_rows(owner)],
                    t_out.at[lot, full_rows(owner)],
                    ag_ss.at[lot, step - 1],
                    ag_rs.at[lot, step - 1],
                    z_mate(step),
                )
            )
        return out

    def agd_copy(lot, step):
        return remote(
            d_out.at[lot],
            d_out.at[lot],
            ag_ss.at[lot, nz - 1 + step - 1],
            ag_rs.at[lot, nz - 1],
            z_mate(step),
        )

    def x_sum(lot):
        x_copy(lot).wait_recv()
        t_out[lot, full_rows(z)] = xs[lot, 0:chunk] + xr[lot, 0:chunk]

        @pl.when(z == owner_z[lot])
        def _():
            d_out[lot] = xs[lot, chunk : chunk + 8] + xr[lot, chunk : chunk + 8]
            for step in order:
                agd_copy(lot, step).start()

        for copy in ag_copies(lot, False):
            copy.start()

    def fin_copy(lot, whose):
        rows = pl.ds(pl.multiple_of(whose * half, half), half)
        return remote(
            t_out.at[lot, rows], t_out.at[lot, rows], fin_ss.at[lot], fin_rs.at[lot], core_mate
        )

    def ag_finish(lot):
        for copy in ag_copies(lot, True):
            copy.wait_recv()
        fin_copy(lot, core).start()

        @pl.when(z != owner_z[lot])
        def _():
            agd_copy(lot, 1).wait_recv()

    def finish(lot):
        fin_copy(lot, 1 - core).wait_recv()

    def drain(lot):
        for copy in core_copies(lot):
            copy.wait_send()
        for copy in z_copies(lot):
            copy.wait_send()
        x_copy(lot).wait_send()
        for copy in ag_copies(lot, False):
            copy.wait_send()
        fin_copy(lot, core).wait_send()

        @pl.when(z != owner_z[lot])
        def _():
            d_copy(lot, 0, z_mate(1)).wait_send()

        @pl.when(z == owner_z[lot])
        def _():
            for step in order:
                agd_copy(lot, step).wait_send()

    pack(0, m0, dot_pieces(r_parts, q_parts, TN))
    for copy in core_copies(0):
        copy.start()
    part_w = local(q_parts)
    for copy in core_copies(0):
        copy.wait_recv()
    core_sum(0)
    z_start(0)
    m2 = dot_pieces(q_parts, q_parts, TN)
    for copy in halos[2]:
        copy.wait_recv()
    m3 = dot_pieces(q_parts, pieces(part_w - coupled(2), 3), TN)
    pack(1, m2, m3)
    for copy in core_copies(1):
        copy.start()
    for copy in core_copies(1):
        copy.wait_recv()
    core_sum(1)
    z_start(1)
    z_sum(0)
    x_sum(0)
    z_sum(1)
    x_sum(1)
    ag_finish(0)
    ag_finish(1)
    finish(0)
    finish(1)
    for stage in halos:
        for copy in stage:
            copy.wait_send()
    drain(0)
    drain(1)


def moments(diagonal, edge_ends, edge_cond, bnd_nodes, bnd_cond, hyd_ids, warm_start, n_net):
    nz = n_net // 4
    nodes, cols = warm_start.shape
    rim = bnd_nodes.shape[2]
    chunk = cols // 2 // nz
    dma = pltpu.SemaphoreType.DMA
    vmem = pl.BlockSpec(memory_space=pltpu.VMEM)
    return pl.pallas_call(
        functools.partial(moments_kernel, nz),
        name="moments",
        out_shape=[
            jax.ShapeDtypeStruct((nodes, cols), F32),
            jax.ShapeDtypeStruct((nodes, cols), F32),
            jax.ShapeDtypeStruct((2, cols, cols), F32),
            jax.ShapeDtypeStruct((2, 8, cols), F32),
        ],
        in_specs=[vmem] * 7,
        out_specs=[vmem] * 4,
        scratch_shapes=[
            pltpu.VMEM((nodes, nodes), F32),
            pltpu.VMEM((3, 2 * rim, cols), F32),
            pltpu.VMEM((3, 2 * rim, cols), F32),
            pltpu.VMEM((2, cols, cols), F32),
            pltpu.VMEM((2, 8, cols), F32),
            pltpu.VMEM((2, cols // 2, cols), F32),
            pltpu.VMEM((2, 8, cols), F32),
            pltpu.VMEM((2, cols // 2, cols), F32),
            pltpu.VMEM((2, 8, cols), F32),
            pltpu.VMEM((2, nz - 1, chunk, cols), F32),
            pltpu.VMEM((2, nz - 1, 8, cols), F32),
            pltpu.VMEM((2, chunk + 8, cols), F32),
            pltpu.VMEM((2, chunk + 8, cols), F32),
            dma((6,)),
            dma((6,)),
            dma((4,)),
            dma((4,)),
            dma((2, nz)),
            dma((2, 2 * nz - 2)),
            dma((2,)),
            dma((2,)),
            dma((2, 2 * nz - 2)),
            dma((2, nz)),
            dma((2,)),
            dma((2,)),
        ],
        compiler_params=pltpu.CompilerParams(
            collective_id=0, has_side_effects=True, vmem_limit_bytes=48 << 20
        ),
    )(
        diagonal[None, :],
        edge_ends.T,
        edge_cond[None, :],
        bnd_nodes[0],
        bnd_cond[0],
        hyd_ids[None, :],
        warm_start,
    )


def update_kernel(x_ref, r_ref, q_ref, t_ref, d_ref, out_ref, inv_ref):
    size = t_ref.shape[1]
    row = lax.broadcasted_iota(jnp.int32, (size, size), 0)
    col = lax.broadcasted_iota(jnp.int32, (size, size), 1)
    eye = (row == col).astype(F32)

    def unpack(lot):
        packed = t_ref[lot]
        upper = jnp.where(row < col, packed, 0.0)
        lower = jnp.where(row > col, packed, 0.0)
        first = jnp.where(row <= col, packed, 0.0) + upper.T
        second = lower + lower.T + eye * d_ref[lot, 0:1, :]
        return first, second

    def inverse(matrix):
        diag = eye * matrix
        by_row = lax.rsqrt(jnp.sum(diag, axis=1, keepdims=True))
        by_col = lax.rsqrt(jnp.sum(diag, axis=0, keepdims=True))
        scaled = matrix * by_row * by_col
        bound = jnp.max(jnp.sum(jnp.abs(scaled), axis=0, keepdims=True), axis=1, keepdims=True)
        gain = 2.0 / bound
        start = eye * gain
        error = eye - scaled * gain
        approx = start + error * gain
        for _ in range(5):
            error = dot_one(error, error)
            approx = approx + dot_one(approx, error)
        rest = eye - dot_full(scaled, approx)
        size_of = jnp.sum(rest * rest)
        good = size_of < 0.25
        inv_ref[...] = jnp.where(good, approx + dot_full(approx, rest), start)

        def unfinished(state):
            step, size_of = state
            return jnp.logical_and(step < 64, jnp.logical_not(size_of < 1e-6))

        def improve(state):
            approx = inv_ref[...]
            rest = eye - dot_full(scaled, approx)
            inv_ref[...] = approx + dot_full(approx, rest)
            return state[0] + 1, jnp.sum(rest * rest)

        lax.while_loop(unfinished, improve, (jnp.int32(0), size_of))
        return inv_ref[...] * by_row * by_col

    m0, m1 = unpack(0)
    m2, m3 = unpack(1)
    inv1 = inverse(m1)
    alpha = dot_full(inv1, m0)
    cross = dot_full(inv1, m2)
    schur = m3 - dot_full(m2, cross)
    rhs = m1 - dot_full(m2, alpha)
    weight_q = dot_full(inverse(schur), rhs)
    weight_r = alpha - dot_full(cross, weight_q)
    out_ref[...] = (
        x_ref[...]
        + dot_pieces(pieces(r_ref[...], 3), pieces(weight_r, 3), NN)
        + dot_pieces(pieces(q_ref[...], 3), pieces(weight_q, 3), NN)
    )


def update(warm_start, residual, image, packed, diagonals):
    cols = warm_start.shape[1]
    vmem = pl.BlockSpec(memory_space=pltpu.VMEM)
    return pl.pallas_call(
        update_kernel,
        name="update",
        out_shape=jax.ShapeDtypeStruct(warm_start.shape, F32),
        in_specs=[vmem] * 5,
        out_specs=vmem,
        scratch_shapes=[pltpu.VMEM((cols, cols), F32)],
        compiler_params=pltpu.CompilerParams(vmem_limit_bytes=48 << 20),
    )(warm_start, residual, image, packed, diagonals)


def heads_kernel(groups, x_ref, picks_ref, flows_ref, out_ref, src, dst, ss, rs):
    nodes, cols = x_ref.shape
    scen = out_ref.shape[0]
    hyd = lax.axis_index("hyd")
    order = sorted(range(1, groups), key=lambda s: -min(s % 4, 4 - s % 4) - 2 * (s >= 4))
    order = order[: groups - 1]

    def mate(step):
        return lax.rem(hyd + step, groups)

    barrier = pltpu.get_barrier_semaphore()
    for step in order:
        pl.semaphore_signal(barrier, inc=1, device_id={"hyd": mate(step)}, device_id_type=MESH)

    x_parts = pieces(x_ref[...], 3)
    column = lax.broadcasted_iota(jnp.int32, (cols, scen), 0) + hyd * cols

    def scenario(owner):
        lanes = pl.ds(pl.multiple_of(owner * scen, scen), scen)
        picks, flows = picks_ref[:, lanes], flows_ref[:, lanes]
        total = jnp.zeros((cols, scen), F32)
        for slot in range(PICK):
            total = total + jnp.where(
                column == picks[slot : slot + 1, :], flows[slot : slot + 1, :], 0.0
            )
        return total

    def copy(step):
        return pltpu.make_async_remote_copy(
            src_ref=src.at[step],
            dst_ref=dst.at[step],
            send_sem=ss.at[step],
            recv_sem=rs.at[step],
            device_id={"hyd": mate(step)},
            device_id_type=MESH,
        )

    every = order + [0]
    waited = False
    for at in range(0, len(every), 2):
        pair = every[at : at + 2]
        block = jnp.concatenate([scenario(mate(step)) for step in pair], axis=1)
        both = dot_pieces(x_parts, pieces(block, 3), NN)
        for i, step in enumerate(pair):
            src[step] = both[:, i * scen : (i + 1) * scen]
        if not waited:
            pl.semaphore_wait(barrier, len(order))
            waited = True
        for step in pair:
            if step:
                copy(step).start()
    total = src[0]
    for step in order:
        copy(step).wait_recv()
    for step in order:
        total = total + dst[step]
    out_ref[...] = total.T
    for step in order:
        copy(step).wait_send()


def heads_of(responses, picks, flows, groups):
    nodes, cols = responses.shape
    scen = picks.shape[0] // groups
    dma = pltpu.SemaphoreType.DMA
    vmem = pl.BlockSpec(memory_space=pltpu.VMEM)
    return pl.pallas_call(
        functools.partial(heads_kernel, groups),
        name="heads",
        out_shape=jax.ShapeDtypeStruct((scen, nodes), F32),
        in_specs=[vmem] * 3,
        out_specs=vmem,
        scratch_shapes=[
            pltpu.VMEM((groups, nodes, scen), F32),
            pltpu.VMEM((groups, nodes, scen), F32),
            dma((groups,)),
            dma((groups,)),
        ],
        compiler_params=pltpu.CompilerParams(
            collective_id=1, has_side_effects=True, vmem_limit_bytes=48 << 20
        ),
    )(responses, picks.T, flows.T)


def fused_kernel(
    nz,
    groups,
    diag_in,
    ends_in,
    cond_in,
    bn_in,
    bc_in,
    hid_in,
    x_in,
    picks_in,
    flows_in,
    resp_ref,
    heads_ref,
    flag_ref,
    diag_ref,
    ends_ref,
    cond_ref,
    bn_ref,
    bc_ref,
    hid_ref,
    x_ref,
    picks_ref,
    flows_ref,
    r_ref,
    q_ref,
    a_ref,
    halo_src,
    halo_dst,
    t_buf,
    d_buf,
    core_t,
    core_d,
    cross_t,
    acc_t,
    acc_d,
    share_t,
    share_dd,
    t_all,
    d_all,
    part,
    mid_a,
    fin_a,
    mid_b,
    fin_b,
    in_sem,
    know,
    halo_ss,
    halo_rs,
    core_ss,
    core_rs,
    cd_ss,
    cd_rs,
    sh_ss,
    sh_rs,
    sd_ss,
    sd_rs,
    ag_ss,
    ag_rs,
    ad_ss,
    ad_rs,
    last_ss,
    last_rs,
    cr_ss,
    cr_rs,
    ca_ss,
    ca_rs,
    a1_ss,
    a1_rs,
    a2_ss,
    a2_rs,
    b1_ss,
    b1_rs,
    b2_ss,
    b2_rs,
):
    nodes, cols = x_ref.shape
    edges = ends_ref.shape[1]
    rim = bn_ref.shape[1]
    scen = heads_ref.shape[0]
    ny = groups // 2
    n_net = 4 * nz
    net = lax.axis_index("net")
    hyd = lax.axis_index("hyd")
    z = net // 4
    x_lo = lax.rem(net // 2, 2)
    core = lax.rem(net, 2)
    x_hi = hyd // ny
    y = lax.rem(hyd, ny)
    up, down = lax.rem(net + 1, n_net), lax.rem(net + n_net - 1, n_net)
    core_mate = net + 1 - 2 * core
    half = cols // 2

    def net_mate(key):
        return lax.rem(net + 4 * (key // 2) + (key % 2) * (2 - 4 * x_lo) + n_net, n_net)

    def z_mate(step):
        return lax.rem(net + 4 * step + n_net, n_net)

    def y_mate(step):
        return x_hi * ny + lax.rem(y + step, ny)

    hi_mate = (1 - x_hi) * ny + y

    keys = sorted(range(1, 2 * nz), key=lambda k: -min(k // 2, nz - k // 2))
    steps = sorted(range(nz), key=lambda s: -min(s, nz - s))
    near = [1] + ([2, 3, 2 * nz - 2, 2 * nz - 1] if nz > 2 else [2, 3])
    rounds = []
    reach = 1
    while 2 * reach <= nz // 2:
        rounds.append(reach)
        reach *= 2

    barrier = pltpu.get_barrier_semaphore()
    mates = [{"net": net_mate(k)} for k in near] + [{"net": up}, {"net": down}]
    mates += [{"hyd": hi_mate}] + [{"hyd": y_mate(s)} for s in range(1, ny)]
    for mate in mates:
        pl.semaphore_signal(barrier, inc=1, device_id=mate, device_id_type=MESH)

    loads = [
        pltpu.make_async_copy(whole, place, in_sem.at[at])
        for at, (whole, place) in enumerate(
            [
                (x_in, x_ref),
                (bn_in, bn_ref),
                (bc_in, bc_ref),
                (ends_in, ends_ref),
                (cond_in, cond_ref),
                (diag_in, diag_ref),
                (hid_in, hid_ref),
                (picks_in, picks_ref),
                (flows_in, flows_ref),
            ]
        )
    ]
    for load in loads:
        load.start()

    def learn(at):
        for step in (rounds[at], nz - rounds[at]):
            pl.semaphore_signal(
                know.at[at], inc=1, device_id={"net": z_mate(step)}, device_id_type=MESH
            )

    def learned(at):
        pl.semaphore_wait(know.at[at], 2)

    def remote(src, dst, ss, rs, mate):
        return pltpu.make_async_remote_copy(
            src_ref=src,
            dst_ref=dst,
            send_sem=ss,
            recv_sem=rs,
            device_id=mate if isinstance(mate, dict) else {"net": mate},
            device_id_type=MESH,
        )

    def gather(parts, stage):
        halo_src[stage] = dot_pieces(pick_b, parts, TN)

    for load in loads[:3]:
        load.wait()
    ids = jnp.concatenate([bn_ref[0:1, :], bn_ref[1:2, :]], axis=1)
    conds = jnp.concatenate([bc_ref[0:1, :], bc_ref[1:2, :]], axis=1)
    pick = (lax.broadcasted_iota(jnp.int32, (nodes, 2 * rim), 0) == ids).astype(F32)
    pick_b = [pick.astype(BF16)]
    couple = pieces(pick * conds, 3)
    x_parts = pieces(x_ref[...], 3)
    gather(x_parts, 0)
    for load in loads[3:]:
        load.wait()

    pl.semaphore_wait(barrier, len(mates))

    def build():
        node_iota = lax.broadcasted_iota(jnp.int32, (nodes, edges), 0)
        first = node_iota == ends_ref[0:1, :]
        second = node_iota == ends_ref[1:2, :]
        incidence = first.astype(F32) - second.astype(F32)
        incidence_b = incidence.astype(BF16)
        weights = jnp.concatenate(
            [cond_ref[i : i + 1, :] for i in range(cond_ref.shape[0])], axis=1
        )
        total = None
        for part_c in reversed(pieces(weights, 3)):
            term = lax.dot_general(
                (incidence * part_c.astype(F32)).astype(BF16),
                incidence_b,
                NT,
                preferred_element_type=F32,
            )
            total = term if total is None else total + term
        for part_c in reversed(pieces(conds, 3)):
            total = total + lax.dot_general(
                (pick * part_c.astype(F32)).astype(BF16),
                pick_b[0],
                NT,
                preferred_element_type=F32,
            )
        square = lax.broadcasted_iota(jnp.int32, (nodes, nodes), 0) == lax.broadcasted_iota(
            jnp.int32, (nodes, nodes), 1
        )
        a_ref[...] = total + jnp.where(square, diag_ref[...], 0.0)

    def halo(stage):
        upper, lower = pl.ds(rim, rim), pl.ds(0, rim)
        at = 2 * stage
        return [
            remote(
                halo_src.at[stage, upper],
                halo_dst.at[stage, lower],
                halo_ss.at[at],
                halo_rs.at[at],
                up,
            ),
            remote(
                halo_src.at[stage, lower],
                halo_dst.at[stage, upper],
                halo_ss.at[at + 1],
                halo_rs.at[at + 1],
                down,
            ),
        ]

    def local(parts):
        return dot_pieces(pieces(a_ref[...], 3), parts, NN)

    def coupled(stage):
        return dot_pieces(couple, pieces(halo_dst[stage], 3), NN)

    tri_row = lax.broadcasted_iota(jnp.int32, (half, half), 0)
    tri_col = lax.broadcasted_iota(jnp.int32, (half, half), 1)
    half_eye = (tri_row == tri_col).astype(F32)
    base = [0, half, 3 * half]
    rows_of = [half // 2, half, half // 2]
    spot_rows = [2 * rows // nz for rows in rows_of]

    def pack(place, matrix):
        folded = jnp.where(tri_row <= tri_col, matrix[:half, :half], matrix[half:, half:])
        t_buf[place : place + half, 0:half] = folded
        t_buf[place : place + half, half:cols] = matrix[:half, half:]
        return jnp.sum(half_eye * matrix[half:, half:], axis=0, keepdims=True)

    def unpack(place, diagonal):
        folded, cross = t_all[place : place + half, 0:half], t_all[place : place + half, half:cols]
        upper = jnp.where(tri_row < tri_col, folded, 0.0)
        lower = jnp.where(tri_row > tri_col, folded, 0.0)
        first = jnp.where(tri_row <= tri_col, folded, 0.0) + upper.T
        second = lower + lower.T + half_eye * diagonal
        return jnp.concatenate(
            [
                jnp.concatenate([first, cross], axis=1),
                jnp.concatenate([cross.T, second], axis=1),
            ],
            axis=0,
        )

    def lot_rows(lot, whose):
        rows = rows_of[lot]
        return pl.ds(pl.multiple_of(base[lot] + whose * rows, rows), rows)

    def own_rows(lot):
        return pl.ds(base[lot] // 2, rows_of[lot])

    def core_copy(lot):
        return remote(
            t_buf.at[lot_rows(lot, 1 - core)],
            core_t.at[own_rows(lot)],
            core_ss.at[lot],
            core_rs.at[lot],
            core_mate,
        )

    def core_sum(lot):
        core_copy(lot).wait_recv()
        acc_t[own_rows(lot)] = t_buf[lot_rows(lot, core)] + core_t[own_rows(lot)]

    def core_d_copy(at):
        return remote(d_buf.at[at], core_d.at[at], cd_ss.at[at], cd_rs.at[at], core_mate)

    def core_d_sum(at):
        core_d_copy(at).wait_recv()
        acc_d[at] = d_buf[at] + core_d[at]

    mine = x_lo == lax.rem(z, 2)

    def spot(lot, zc, start):
        rows = spot_rows[lot]
        return (
            pl.ds(pl.multiple_of(start + (zc // 2) * rows, rows), rows),
            pl.ds(pl.multiple_of(lax.rem(zc, 2) * half, half), half),
        )

    x_mate = net + 2 - 4 * x_lo
    own_lanes = pl.ds(pl.multiple_of(x_lo * half, half), half)
    far_lanes = pl.ds(pl.multiple_of((1 - x_lo) * half, half), half)
    odd = lax.rem(x_lo + z, 2)

    def cross_copy(lot):
        return remote(
            acc_t.at[own_rows(lot), far_lanes],
            cross_t.at[own_rows(lot)],
            cr_ss.at[lot],
            cr_rs.at[lot],
            x_mate,
        )

    def cross_start(lot):
        if lot in CROSS_FIRST:
            cross_copy(lot).start()

    def cross_sum(lot):
        if lot in CROSS_FIRST:
            cross_copy(lot).wait_recv()
            acc_t[own_rows(lot), own_lanes] = (
                acc_t[own_rows(lot), own_lanes] + cross_t[own_rows(lot)]
            )

    def share_copy(lot, step):
        zc = lax.rem(z + step, nz)
        if lot in CROSS_FIRST:
            slot = step - 1
        else:
            slot = 2 * step - 1 + (lax.rem(x_lo + zc, 2) if step else 1)
        rows, lanes = spot(lot, zc, base[lot] // 2)
        return remote(
            acc_t.at[rows, lanes],
            share_t.at[lot, slot, pl.ds(0, spot_rows[lot])],
            sh_ss.at[lot, step],
            sh_rs.at[lot, slot],
            4 * zc + 2 * lax.rem(zc, 2) + core,
        )

    def share_slots(lot):
        return nz - 1 if lot in CROSS_FIRST else 2 * nz - 1

    def share_arrival(lot, slot):
        rows, lanes = spot(lot, z, base[lot] // 2)
        return remote(
            acc_t.at[rows, lanes],
            share_t.at[lot, slot, pl.ds(0, spot_rows[lot])],
            sh_ss.at[lot, 0],
            sh_rs.at[lot, slot],
            core_mate,
        )

    def share_each(lot, act):
        if lot in CROSS_FIRST:
            for step in sorted(range(2, nz, 2), key=lambda s: -min(s, nz - s)):
                act(share_copy(lot, step + odd))
        else:
            for step in steps:
                if step:
                    act(share_copy(lot, step))

        @pl.when(jnp.logical_not(mine))
        def _():
            act(share_copy(lot, 1 if lot in CROSS_FIRST else 0))

    def share_start(lot):
        share_each(lot, lambda copy: copy.start())

    def all_spot(lot, zc):
        return spot(lot, zc, base[lot] + core * rows_of[lot])

    def all_copy(lot, zc, key):
        rows, lanes = all_spot(lot, zc)
        return remote(
            t_all.at[rows, lanes],
            t_all.at[rows, lanes],
            ag_ss.at[lot, key - 1],
            ag_rs.at[lot, zc],
            net_mate(key),
        )

    def all_keys(lot):
        return [key for key in keys if key % 2 == 0 or lot not in CROSS_LAST]

    def share_sum(lot):
        @pl.when(mine)
        def _():
            for slot in range(share_slots(lot)):
                share_arrival(lot, slot).wait_recv()
            rows, lanes = spot(lot, z, base[lot] // 2)
            total = acc_t[rows, lanes]
            for slot in range(share_slots(lot)):
                total = total + share_t[lot, slot, 0 : spot_rows[lot]]
            rows, lanes = all_spot(lot, z)
            t_all[rows, lanes] = total
            for key in all_keys(lot):
                all_copy(lot, z, key).start()

    owner_z = [nz // 4, (3 * nz) // 4]

    def is_owner(at):
        return jnp.logical_and(z == owner_z[at], x_lo == 0)

    def share_d(at, slot, mate):
        return remote(
            acc_d.at[at], share_dd.at[at, slot], sd_ss.at[at], sd_rs.at[at, slot], mate
        )

    def all_d(at, key):
        return remote(
            d_all.at[at], d_all.at[at], ad_ss.at[at, key - 1], ad_rs.at[at], net_mate(key)
        )

    def share_d_start(at):
        @pl.when(jnp.logical_not(is_owner(at)))
        def _():
            slot = 2 * lax.rem(owner_z[at] - z + nz, nz) + x_lo - 1
            share_d(at, slot, 4 * owner_z[at] + core).start()

    def share_d_sum(at):
        @pl.when(is_owner(at))
        def _():
            total_d = acc_d[at]
            for slot in range(2 * nz - 1):
                share_d(at, slot, core_mate).wait_recv()
            for slot in range(2 * nz - 1):
                total_d = total_d + share_dd[at, slot]
            d_all[at] = total_d
            for key in keys:
                all_d(at, key).start()

    def all_d_finish(at):
        @pl.when(jnp.logical_not(is_owner(at)))
        def _():
            all_d(at, 1).wait_recv()

    def last_copy(lot, whose):
        return remote(
            t_all.at[lot_rows(lot, whose)],
            t_all.at[lot_rows(lot, whose)],
            last_ss.at[lot],
            last_rs.at[lot],
            core_mate,
        )

    def level_copy(lot, lanes):
        rows = lot_rows(lot, core)
        return remote(
            t_all.at[rows, lanes], t_all.at[rows, lanes], ca_ss.at[lot], ca_rs.at[lot], x_mate
        )

    def all_finish(lot):
        if lot in CROSS_LAST:
            for step in range(2, nz, 2):
                all_copy(lot, lax.rem(z + step + odd, nz), 1).wait_recv()
        else:
            for step in range(1, nz):
                all_copy(lot, lax.rem(z + step, nz), 1).wait_recv()

        @pl.when(jnp.logical_not(mine))
        def _():
            zc = lax.rem(z + 1, nz) if lot in CROSS_LAST else z
            all_copy(lot, zc, 1).wait_recv()

        if lot in CROSS_LAST:
            level_copy(lot, own_lanes).start()
        else:
            last_copy(lot, core).start()

    def level(lot):
        if lot in CROSS_LAST:
            level_copy(lot, far_lanes).wait_recv()
            last_copy(lot, core).start()

    def drain(lot):
        core_copy(lot).wait_send()
        share_each(lot, lambda copy: copy.wait_send())
        if lot in CROSS_FIRST:
            cross_copy(lot).wait_send()
        if lot in CROSS_LAST:
            level_copy(lot, own_lanes).wait_send()

        @pl.when(mine)
        def _():
            for key in all_keys(lot):
                all_copy(lot, z, key).wait_send()

        last_copy(lot, core).wait_send()

    def drain_d(at):
        core_d_copy(at).wait_send()

        @pl.when(jnp.logical_not(is_owner(at)))
        def _():
            share_d(at, 0, core_mate).wait_send()

        @pl.when(is_owner(at))
        def _():
            for key in keys:
                all_d(at, key).wait_send()

    halos = [halo(stage) for stage in range(3)]
    for copy in halos[0]:
        copy.start()
    if rounds:
        learn(0)
    build()
    hyd_local = hid_ref[...] - net * nodes
    demand = (lax.broadcasted_iota(jnp.int32, (nodes, cols), 0) == hyd_local).astype(F32)
    part_r = demand - local(x_parts)
    if rounds:
        learned(0)
        if len(rounds) > 1:
            learn(1)
    for copy in halos[0]:
        copy.wait_recv()
    residual = part_r + coupled(0)
    r_parts = pieces(residual, 3)
    gather(r_parts, 1)
    for copy in halos[1]:
        copy.start()
    r_ref[...] = residual
    d0 = pack(base[0], dot_pieces(r_parts, r_parts, TN))
    core_copy(0).start()
    if len(rounds) > 1:
        learned(1)
        if len(rounds) > 2:
            learn(2)
    part_q = local(r_parts)
    core_sum(0)
    cross_start(0)
    for copy in halos[1]:
        copy.wait_recv()
    image = part_q - coupled(1)
    q_parts = pieces(image, 3)
    gather(q_parts, 2)
    for copy in halos[2]:
        copy.start()
    q_ref[...] = image
    for at in range(2, len(rounds)):
        learned(at)
        if at + 1 < len(rounds):
            learn(at + 1)
    cross_sum(0)
    share_start(0)
    d1 = pack(base[1], dot_pieces(r_parts, q_parts, TN))
    d2 = pack(base[1] + half, dot_pieces(q_parts, q_parts, TN))
    d_buf[0] = jnp.concatenate([d0, d1, d2, jnp.zeros((5, half), F32)], axis=0)
    core_copy(1).start()
    core_d_copy(0).start()
    part_w = local(q_parts)
    core_d_sum(0)
    share_d_start(0)
    core_sum(1)
    cross_start(1)
    if 1 not in CROSS_FIRST:
        share_start(1)
    for copy in halos[2]:
        copy.wait_recv()
    d3 = pack(base[2], dot_pieces(q_parts, pieces(part_w - coupled(2), 3), TN))
    d_buf[1] = jnp.broadcast_to(d3, (8, half))
    core_copy(2).start()
    core_d_copy(1).start()
    if 1 in CROSS_FIRST:
        cross_sum(1)
        share_start(1)
    core_d_sum(1)
    share_d_start(1)
    core_sum(2)
    cross_start(2)
    cross_sum(2)
    share_start(2)
    share_sum(0)
    share_d_sum(0)
    share_sum(1)
    share_d_sum(1)
    share_sum(2)
    all_finish(0)
    level(0)
    all_finish(1)
    level(1)
    all_d_finish(0)
    last_copy(0, 1 - core).wait_recv()
    last_copy(1, 1 - core).wait_recv()

    row = lax.broadcasted_iota(jnp.int32, (cols, cols), 0)
    col = lax.broadcasted_iota(jnp.int32, (cols, cols), 1)
    eye = (row == col).astype(F32)

    def inverse(matrix):
        diag = eye * matrix
        by_row = lax.rsqrt(jnp.sum(diag, axis=1, keepdims=True))
        by_col = lax.rsqrt(jnp.sum(diag, axis=0, keepdims=True))
        scaled = matrix * by_row * by_col
        bound = jnp.max(jnp.sum(jnp.abs(scaled), axis=0, keepdims=True), axis=1, keepdims=True)
        gain = 2.0 / bound
        error = eye - scaled * gain
        approx = eye * gain + error * gain
        for _ in range(5):
            error = dot_one(error, error)
            approx = approx + dot_one(approx, error)
        approx = approx + dot_one(approx, eye - dot_full(scaled, approx))
        rest = eye - dot_full(scaled, approx)
        approx = approx + dot_one(approx, rest)
        left = jnp.sum(jnp.sum(rest * rest, axis=0, keepdims=True), axis=1, keepdims=True)
        return approx * by_row * by_col, left

    m0 = unpack(base[0], d_all[0, 0:1, :])
    m1 = unpack(base[1], d_all[0, 1:2, :])
    m2 = unpack(base[1] + half, d_all[0, 2:3, :])
    inv1, left1 = inverse(m1)
    all_finish(2)
    level(2)
    all_d_finish(1)
    alpha = dot_full(inv1, m0)
    cross = dot_full(inv1, m2)
    rhs = m1 - dot_full(m2, alpha)
    fill = dot_full(m2, cross)
    last_copy(2, 1 - core).wait_recv()
    inv2, left2 = inverse(unpack(base[2], d_all[1, 0:1, :]) - fill)
    weight_q = dot_full(inv2, rhs)
    weight_r = alpha - dot_full(cross, weight_q)
    converged = jnp.logical_and(left1 < 2e-5, left2 < 2e-5)
    flag = jnp.broadcast_to(jnp.where(converged, 0.0, 1.0), (8, scen))
    answer = (
        x_ref[...]
        + dot_pieces(pieces(r_ref[...], 2), pieces(weight_r, 2), NN)
        + dot_pieces(pieces(q_ref[...], 2), pieces(weight_q, 2), NN)
    )
    resp_ref[...] = answer
    a_parts = pieces(answer, 2)
    column = lax.broadcasted_iota(jnp.int32, (cols, scen), 0) + hyd * cols

    def scenario(owner):
        lanes = pl.ds(pl.multiple_of(owner * scen, scen), scen)
        picks, flows = picks_ref[:, lanes], flows_ref[:, lanes]
        total = jnp.zeros((cols, scen), F32)
        for slot in range(PICK):
            total = total + jnp.where(
                column == picks[slot : slot + 1, :], flows[slot : slot + 1, :], 0.0
            )
        return total

    deep = mid_a.shape[1]
    rows_a, rows_b = pl.ds(0, deep), pl.ds(deep, part.shape[1] - deep)

    def a1_copy(dy):
        return remote(
            part.at[ny + dy, rows_a], mid_a.at[dy], a1_ss.at[dy], a1_rs.at[dy], {"hyd": hi_mate}
        )

    def a2_copy(dy):
        return remote(
            part.at[dy, rows_a],
            fin_a.at[dy - 1],
            a2_ss.at[dy - 1],
            a2_rs.at[dy - 1],
            {"hyd": y_mate(dy)},
        )

    def b1_copy(fx, dy):
        return remote(
            part.at[fx * ny + dy, rows_b],
            mid_b.at[fx, dy - 1],
            b1_ss.at[fx, dy - 1],
            b1_rs.at[fx, dy - 1],
            {"hyd": y_mate(dy)},
        )

    def b2_copy():
        return remote(part.at[ny, rows_b], fin_b, b2_ss.at[0], b2_rs.at[0], {"hyd": hi_mate})

    order = sorted(range(1, ny), key=lambda s: -min(s, ny - s)) + [0]
    every = [(1, dy) for dy in order] + [(0, dy) for dy in order]
    for at in range(0, groups, 2):
        pair = every[at : at + 2]
        block = jnp.concatenate(
            [scenario((x_hi if fx == 0 else 1 - x_hi) * ny + lax.rem(y + dy, ny)) for fx, dy in pair],
            axis=1,
        )
        both = dot_pieces(a_parts, pieces(block, 2), NN)
        for i, (fx, dy) in enumerate(pair):
            part[fx * ny + dy, 0:8] = flag
            part[fx * ny + dy, 8 : nodes + 8] = both[:, i * scen : (i + 1) * scen]
            if fx:
                a1_copy(dy).start()
            if dy:
                b1_copy(fx, dy).start()

    def a_step(dy):
        a1_copy(dy).wait_recv()
        part[dy, rows_a] = part[dy, rows_a] + mid_a[dy]
        if dy:
            a2_copy(dy).start()

    half_way = (len(order) - 1) // 2 + 1
    for dy in order[:half_way]:
        a_step(dy)
    total_b = part[ny, rows_b]
    for dy in range(1, ny):
        b1_copy(1, dy).wait_recv()
        total_b = total_b + mid_b[1, dy - 1]
    part[ny, rows_b] = total_b
    b2_copy().start()
    for dy in order[half_way:]:
        a_step(dy)
    for stage in halos:
        for copy in stage:
            copy.wait_send()
    for lot in range(3):
        drain(lot)
    drain_d(0)
    drain_d(1)
    total_b = part[0, rows_b]
    for dy in range(1, ny):
        b1_copy(0, dy).wait_recv()
        total_b = total_b + mid_b[0, dy - 1]
    b2_copy().wait_recv()
    total_b = total_b + fin_b[...]
    total_a = part[0, rows_a]
    for dy in order[:-1]:
        a2_copy(dy).wait_recv()
        total_a = total_a + fin_a[dy - 1]
    flag_ref[...] = total_a[0:8]
    heads_ref[...] = jnp.concatenate([total_a[8:], total_b], axis=0).T
    for dy in range(ny):
        a1_copy(dy).wait_send()
        if dy:
            a2_copy(dy).wait_send()
            b1_copy(0, dy).wait_send()
            b1_copy(1, dy).wait_send()
    b2_copy().wait_send()


def fused(
    diagonal,
    edge_ends,
    edge_cond,
    bnd_nodes,
    bnd_cond,
    hyd_ids,
    warm_start,
    picks,
    flows,
    n_net,
    groups,
):
    nz = n_net // 4
    ny = groups // 2
    nodes, cols = warm_start.shape
    rim = bnd_nodes.shape[2]
    edges = edge_cond.shape[0]
    scen = picks.shape[0] // groups
    half = cols // 2
    peers = 2 * nz - 1
    spot = 2 * half // nz
    deep = 8 + (nodes * SPLIT // 64) // 8 * 8
    dma = pltpu.SemaphoreType.DMA
    vmem = pl.BlockSpec(memory_space=pltpu.VMEM)
    anywhere = pl.BlockSpec(memory_space=pl.ANY)
    return pl.pallas_call(
        functools.partial(fused_kernel, nz, groups),
        name="fused",
        out_shape=[
            jax.ShapeDtypeStruct((nodes, cols), F32),
            jax.ShapeDtypeStruct((scen, nodes), F32),
            jax.ShapeDtypeStruct((8, scen), F32),
        ],
        in_specs=[anywhere] * 9,
        out_specs=[vmem] * 3,
        scratch_shapes=[
            pltpu.VMEM((1, nodes), F32),
            pltpu.VMEM((2, edges), jnp.int32),
            pltpu.VMEM((edges // 128, 128), F32),
            pltpu.VMEM((2, rim), jnp.int32),
            pltpu.VMEM((2, rim), F32),
            pltpu.VMEM((1, cols), jnp.int32),
            pltpu.VMEM((nodes, cols), F32),
            pltpu.VMEM((PICK, scen * groups), jnp.int32),
            pltpu.VMEM((PICK, scen * groups), F32),
            pltpu.VMEM((nodes, cols), F32),
            pltpu.VMEM((nodes, cols), F32),
            pltpu.VMEM((nodes, nodes), F32),
            pltpu.VMEM((3, 2 * rim, cols), F32),
            pltpu.VMEM((3, 2 * rim, cols), F32),
            pltpu.VMEM((2 * cols, cols), F32),
            pltpu.VMEM((2, 8, half), F32),
            pltpu.VMEM((cols, cols), F32),
            pltpu.VMEM((2, 8, half), F32),
            pltpu.VMEM((cols, half), F32),
            pltpu.VMEM((cols, cols), F32),
            pltpu.VMEM((2, 8, half), F32),
            pltpu.VMEM((3, peers, spot, half), F32),
            pltpu.VMEM((2, peers, 8, half), F32),
            pltpu.VMEM((2 * cols, cols), F32),
            pltpu.VMEM((2, 8, half), F32),
            pltpu.VMEM((groups, nodes + 8, scen), F32),
            pltpu.VMEM((ny, deep, scen), F32),
            pltpu.VMEM((ny - 1, deep, scen), F32),
            pltpu.VMEM((2, ny - 1, nodes + 8 - deep, scen), F32),
            pltpu.VMEM((nodes + 8 - deep, scen), F32),
            dma((9,)),
            pltpu.SemaphoreType.REGULAR((3,)),
            dma((6,)),
            dma((6,)),
            dma((3,)),
            dma((3,)),
            dma((2,)),
            dma((2,)),
            dma((3, nz)),
            dma((3, peers)),
            dma((2,)),
            dma((2, peers)),
            dma((3, peers)),
            dma((3, nz)),
            dma((2, peers)),
            dma((2,)),
            dma((3,)),
            dma((3,)),
            dma((3,)),
            dma((3,)),
            dma((3,)),
            dma((3,)),
            dma((ny,)),
            dma((ny,)),
            dma((ny - 1,)),
            dma((ny - 1,)),
            dma((2, ny - 1)),
            dma((2, ny - 1)),
            dma((1,)),
            dma((1,)),
        ],
        compiler_params=pltpu.CompilerParams(
            collective_id=2, has_side_effects=True, vmem_limit_bytes=48 << 20
        ),
    )(
        diagonal[None, :],
        edge_ends.T,
        edge_cond.reshape(edges // 128, 128),
        bnd_nodes[0],
        bnd_cond[0],
        hyd_ids[None, :],
        warm_start,
        picks.T,
        flows.T,
    )


def per_device(
    diagonal, edge_ends, edge_cond, bnd_nodes, bnd_cond, hyd_ids, warm_start, scen_picks, scen_flows
):
    n_net, groups = lax.axis_size("net"), lax.axis_size("hyd")
    local = (diagonal, edge_ends, edge_cond, bnd_nodes, bnd_cond, hyd_ids, warm_start)
    responses, heads, flag = fused(*local, scen_picks, scen_flows, n_net, groups)

    def keep(responses, heads):
        return responses, heads

    def redo(responses, heads):
        residual, image, packed, diagonals = moments(*local, n_net)
        responses = update(warm_start, residual, image, packed, diagonals)
        return responses, heads_of(responses, scen_picks, scen_flows, groups)

    return lax.cond(flag[0, 0] > 0.0, redo, keep, responses, heads)


def solution(mesh):
    placed = (
        P("net"),
        P("net", None),
        P("net"),
        P("net", None, None),
        P("net", None, None),
        P("hyd"),
        P("net", "hyd"),
        P(),
        P(),
    )
    return jax.shard_map(
        per_device,
        mesh=mesh,
        in_specs=placed,
        out_specs=(P("net", "hyd"), P("hyd", "net")),
        check_vma=False,
    )
```

```python
import functools

import jax
import jax.numpy as jnp
from jax import lax
from jax.experimental import pallas as pl
from jax.experimental.pallas import tpu as pltpu
from jax.sharding import PartitionSpec as P

MESH = pl.DeviceIdType.MESH
F32 = jnp.float32
BF16 = jnp.bfloat16
NN = (((1,), (0,)), ((), ()))
TN = (((0,), (0,)), ((), ()))
NT = (((1,), (1,)), ((), ()))
PICK = 4
SPLIT = 38
CROSS_FIRST = (0, 1)
CROSS_LAST = (0, 1)


def pieces(value, count):
    out = []
    for step in range(count):
        part = value.astype(BF16)
        out.append(part)
        if step + 1 < count:
            value = value - part.astype(F32)
    return out


def dot_pieces(first, second, dims):
    depth = max(len(first), len(second))
    total = None
    for level in reversed(range(depth)):
        for i, left in enumerate(first):
            j = level - i
            if 0 <= j < len(second):
                term = lax.dot_general(left, second[j], dims, preferred_element_type=F32)
                total = term if total is None else total + term
    return total


def dot_full(first, second, dims=NN):
    return lax.dot_general(
        first, second, dims, precision=lax.Precision.HIGHEST, preferred_element_type=F32
    )


def dot_one(first, second):
    return lax.dot_general(
        first.astype(BF16), second.astype(BF16), NN, preferred_element_type=F32
    )


def moments_kernel(
    nz,
    diag_ref,
    ends_ref,
    cond_ref,
    bn_ref,
    bc_ref,
    hid_ref,
    x_ref,
    r_ref,
    q_ref,
    t_out,
    d_out,
    a_ref,
    halo_src,
    halo_dst,
    t_buf,
    d_buf,
    core_t,
    core_d,
    acc_t,
    acc_d,
    zr_t,
    zr_d,
    xs,
    xr,
    halo_ss,
    halo_rs,
    core_ss,
    core_rs,
    zr_ss,
    zr_rs,
    x_ss,
    x_rs,
    ag_ss,
    ag_rs,
    fin_ss,
    fin_rs,
):
    nodes, cols = x_ref.shape
    edges = cond_ref.shape[1]
    rim = bn_ref.shape[1]
    n_net = 4 * nz
    net = lax.axis_index("net")
    z = net // 4
    x_lo = lax.rem(net // 2, 2)
    core = lax.rem(net, 2)
    up, down = lax.rem(net + 1, n_net), lax.rem(net + n_net - 1, n_net)
    core_mate = net + 1 - 2 * core
    x_mate = net + 2 - 4 * x_lo

    def z_mate(step):
        return lax.rem(net + 4 * step, n_net)

    barrier = pltpu.get_barrier_semaphore()
    order = sorted(range(1, nz), key=lambda s: -min(s, nz - s))
    mates = [z_mate(s) for s in order] + [x_mate, up, down]
    for mate in mates:
        pl.semaphore_signal(barrier, inc=1, device_id={"net": mate}, device_id_type=MESH)

    def remote(src, dst, ss, rs, mate):
        return pltpu.make_async_remote_copy(
            src_ref=src,
            dst_ref=dst,
            send_sem=ss,
            recv_sem=rs,
            device_id={"net": mate},
            device_id_type=MESH,
        )

    node_iota = lax.broadcasted_iota(jnp.int32, (nodes, edges), 0)
    first = node_iota == ends_ref[0:1, :]
    second = node_iota == ends_ref[1:2, :]
    incidence = first.astype(F32) - second.astype(F32)
    ids = jnp.concatenate([bn_ref[0:1, :], bn_ref[1:2, :]], axis=1)
    conds = jnp.concatenate([bc_ref[0:1, :], bc_ref[1:2, :]], axis=1)
    pick = (lax.broadcasted_iota(jnp.int32, (nodes, 2 * rim), 0) == ids).astype(F32)
    pick_b = [pick.astype(BF16)]
    x_parts = pieces(x_ref[...], 3)

    def gather(parts, stage):
        halo_src[stage] = dot_pieces(pick_b, parts, TN)

    gather(x_parts, 0)
    incidence_b = incidence.astype(BF16)
    total = None
    for part in reversed(pieces(cond_ref[...], 3)):
        term = lax.dot_general(
            (incidence * part.astype(F32)).astype(BF16), incidence_b, NT, preferred_element_type=F32
        )
        total = term if total is None else total + term
    for part in reversed(pieces(conds, 3)):
        total = total + lax.dot_general(
            (pick * part.astype(F32)).astype(BF16), pick_b[0], NT, preferred_element_type=F32
        )
    square = lax.broadcasted_iota(jnp.int32, (nodes, nodes), 0) == lax.broadcasted_iota(
        jnp.int32, (nodes, nodes), 1
    )
    a_ref[...] = total + jnp.where(square, diag_ref[...], 0.0)
    couple = pieces(pick * conds, 3)

    pl.semaphore_wait(barrier, len(mates))

    def halo(stage):
        upper, lower = pl.ds(rim, rim), pl.ds(0, rim)
        return [
            remote(
                halo_src.at[stage, upper],
                halo_dst.at[stage, lower],
                halo_ss.at[2 * stage],
                halo_rs.at[2 * stage],
                up,
            ),
            remote(
                halo_src.at[stage, lower],
                halo_dst.at[stage, upper],
                halo_ss.at[2 * stage + 1],
                halo_rs.at[2 * stage + 1],
                down,
            ),
        ]

    def local(parts):
        return dot_pieces(pieces(a_ref[...], 3), parts, NN)

    def coupled(stage):
        return dot_pieces(couple, pieces(halo_dst[stage], 3), NN)

    halos = [halo(stage) for stage in range(3)]
    for copy in halos[0]:
        copy.start()
    hyd_local = hid_ref[...] - net * nodes
    demand = (lax.broadcasted_iota(jnp.int32, (nodes, cols), 0) == hyd_local).astype(F32)
    part_r = demand - local(x_parts)
    for copy in halos[0]:
        copy.wait_recv()
    residual = part_r + coupled(0)
    r_parts = pieces(residual, 3)
    gather(r_parts, 1)
    for copy in halos[1]:
        copy.start()
    r_ref[...] = residual
    part_q = local(r_parts)
    m0 = dot_pieces(r_parts, r_parts, TN)
    for copy in halos[1]:
        copy.wait_recv()
    image = part_q - coupled(1)
    q_parts = pieces(image, 3)
    gather(q_parts, 2)
    for copy in halos[2]:
        copy.start()
    q_ref[...] = image

    row = lax.broadcasted_iota(jnp.int32, (cols, cols), 0)
    col = lax.broadcasted_iota(jnp.int32, (cols, cols), 1)

    half = cols // 2
    chunk = half // nz

    def pack(lot, upper_m, lower_m):
        t_buf[lot] = jnp.where(row <= col, upper_m, lower_m)
        diagonal = jnp.sum(jnp.where(row == col, lower_m, 0.0), axis=0, keepdims=True)
        d_buf[lot] = jnp.broadcast_to(diagonal, (8, cols))

    def core_copies(lot):
        other = pl.ds(pl.multiple_of((1 - core) * half, half), half)
        return [
            remote(
                t_buf.at[lot, other],
                core_t.at[lot],
                core_ss.at[2 * lot],
                core_rs.at[2 * lot],
                core_mate,
            ),
            remote(
                d_buf.at[lot],
                core_d.at[lot],
                core_ss.at[2 * lot + 1],
                core_rs.at[2 * lot + 1],
                core_mate,
            ),
        ]

    def core_sum(lot):
        mine = pl.ds(pl.multiple_of(core * half, half), half)
        acc_t[lot] = t_buf[lot, mine] + core_t[lot]
        acc_d[lot] = d_buf[lot] + core_d[lot]

    owner_z = [nz // 4, (3 * nz) // 4]

    def z_copies(lot):
        out = []
        for step in order:
            owner = lax.rem(z + step, nz)
            rows = pl.ds(pl.multiple_of(owner * chunk, chunk), chunk)
            out.append(
                remote(
                    acc_t.at[lot, rows],
                    zr_t.at[lot, step - 1],
                    zr_ss.at[lot, step - 1],
                    zr_rs.at[lot, step - 1],
                    z_mate(step),
                )
            )
        return out

    def d_copy(lot, slot, mate):
        return remote(
            acc_d.at[lot],
            zr_d.at[lot, slot],
            zr_ss.at[lot, nz - 1],
            zr_rs.at[lot, nz - 1 + slot],
            mate,
        )

    def z_start(lot):
        for copy in z_copies(lot):
            copy.start()
        to_owner = lax.rem(owner_z[lot] - z + nz, nz)

        @pl.when(to_owner != 0)
        def _():
            d_copy(lot, to_owner - 1, lax.rem(net + 4 * to_owner, n_net)).start()

    def x_copy(lot):
        return remote(xs.at[lot], xr.at[lot], x_ss.at[lot], x_rs.at[lot], x_mate)

    def z_sum(lot):
        for copy in z_copies(lot):
            copy.wait_recv()
        mine = pl.ds(pl.multiple_of(z * chunk, chunk), chunk)
        total = acc_t[lot, mine]
        for step in range(1, nz):
            total = total + zr_t[lot, step - 1]
        xs[lot, 0:chunk] = total
        xs[lot, chunk : chunk + 8] = acc_d[lot]

        @pl.when(z == owner_z[lot])
        def _():
            total_d = acc_d[lot]
            for slot in range(nz - 1):
                d_copy(lot, slot, z_mate(slot + 1)).wait_recv()
            for slot in range(nz - 1):
                total_d = total_d + zr_d[lot, slot]
            xs[lot, chunk : chunk + 8] = total_d

        x_copy(lot).start()

    def full_rows(index):
        return pl.ds(pl.multiple_of(core * half + index * chunk, chunk), chunk)

    def ag_copies(lot, received):
        out = []
        for step in order:
            owner = lax.rem(z + nz - step, nz) if received else z
            out.append(
                remote(
                    t_out.at[lot, full_rows(owner)],
                    t_out.at[lot, full_rows(owner)],
                    ag_ss.at[lot, step - 1],
                    ag_rs.at[lot, step - 1],
                    z_mate(step),
                )
            )
        return out

    def agd_copy(lot, step):
        return remote(
            d_out.at[lot],
            d_out.at[lot],
            ag_ss.at[lot, nz - 1 + step - 1],
            ag_rs.at[lot, nz - 1],
            z_mate(step),
        )

    def x_sum(lot):
        x_copy(lot).wait_recv()
        t_out[lot, full_rows(z)] = xs[lot, 0:chunk] + xr[lot, 0:chunk]

        @pl.when(z == owner_z[lot])
        def _():
            d_out[lot] = xs[lot, chunk : chunk + 8] + xr[lot, chunk : chunk + 8]
            for step in order:
                agd_copy(lot, step).start()

        for copy in ag_copies(lot, False):
            copy.start()

    def fin_copy(lot, whose):
        rows = pl.ds(pl.multiple_of(whose * half, half), half)
        return remote(
            t_out.at[lot, rows], t_out.at[lot, rows], fin_ss.at[lot], fin_rs.at[lot], core_mate
        )

    def ag_finish(lot):
        for copy in ag_copies(lot, True):
            copy.wait_recv()
        fin_copy(lot, core).start()

        @pl.when(z != owner_z[lot])
        def _():
            agd_copy(lot, 1).wait_recv()

    def finish(lot):
        fin_copy(lot, 1 - core).wait_recv()

    def drain(lot):
        for copy in core_copies(lot):
            copy.wait_send()
        for copy in z_copies(lot):
            copy.wait_send()
        x_copy(lot).wait_send()
        for copy in ag_copies(lot, False):
            copy.wait_send()
        fin_copy(lot, core).wait_send()

        @pl.when(z != owner_z[lot])
        def _():
            d_copy(lot, 0, z_mate(1)).wait_send()

        @pl.when(z == owner_z[lot])
        def _():
            for step in order:
                agd_copy(lot, step).wait_send()

    pack(0, m0, dot_pieces(r_parts, q_parts, TN))
    for copy in core_copies(0):
        copy.start()
    part_w = local(q_parts)
    for copy in core_copies(0):
        copy.wait_recv()
    core_sum(0)
    z_start(0)
    m2 = dot_pieces(q_parts, q_parts, TN)
    for copy in halos[2]:
        copy.wait_recv()
    m3 = dot_pieces(q_parts, pieces(part_w - coupled(2), 3), TN)
    pack(1, m2, m3)
    for copy in core_copies(1):
        copy.start()
    for copy in core_copies(1):
        copy.wait_recv()
    core_sum(1)
    z_start(1)
    z_sum(0)
    x_sum(0)
    z_sum(1)
    x_sum(1)
    ag_finish(0)
    ag_finish(1)
    finish(0)
    finish(1)
    for stage in halos:
        for copy in stage:
            copy.wait_send()
    drain(0)
    drain(1)


def moments(diagonal, edge_ends, edge_cond, bnd_nodes, bnd_cond, hyd_ids, warm_start, n_net):
    nz = n_net // 4
    nodes, cols = warm_start.shape
    rim = bnd_nodes.shape[2]
    chunk = cols // 2 // nz
    dma = pltpu.SemaphoreType.DMA
    vmem = pl.BlockSpec(memory_space=pltpu.VMEM)
    return pl.pallas_call(
        functools.partial(moments_kernel, nz),
        name="moments",
        out_shape=[
            jax.ShapeDtypeStruct((nodes, cols), F32),
            jax.ShapeDtypeStruct((nodes, cols), F32),
            jax.ShapeDtypeStruct((2, cols, cols), F32),
            jax.ShapeDtypeStruct((2, 8, cols), F32),
        ],
        in_specs=[vmem] * 7,
        out_specs=[vmem] * 4,
        scratch_shapes=[
            pltpu.VMEM((nodes, nodes), F32),
            pltpu.VMEM((3, 2 * rim, cols), F32),
            pltpu.VMEM((3, 2 * rim, cols), F32),
            pltpu.VMEM((2, cols, cols), F32),
            pltpu.VMEM((2, 8, cols), F32),
            pltpu.VMEM((2, cols // 2, cols), F32),
            pltpu.VMEM((2, 8, cols), F32),
            pltpu.VMEM((2, cols // 2, cols), F32),
            pltpu.VMEM((2, 8, cols), F32),
            pltpu.VMEM((2, nz - 1, chunk, cols), F32),
            pltpu.VMEM((2, nz - 1, 8, cols), F32),
            pltpu.VMEM((2, chunk + 8, cols), F32),
            pltpu.VMEM((2, chunk + 8, cols), F32),
            dma((6,)),
            dma((6,)),
            dma((4,)),
            dma((4,)),
            dma((2, nz)),
            dma((2, 2 * nz - 2)),
            dma((2,)),
            dma((2,)),
            dma((2, 2 * nz - 2)),
            dma((2, nz)),
            dma((2,)),
            dma((2,)),
        ],
        compiler_params=pltpu.CompilerParams(
            collective_id=0, has_side_effects=True, vmem_limit_bytes=48 << 20
        ),
    )(
        diagonal[None, :],
        edge_ends.T,
        edge_cond[None, :],
        bnd_nodes[0],
        bnd_cond[0],
        hyd_ids[None, :],
        warm_start,
    )


def update_kernel(x_ref, r_ref, q_ref, t_ref, d_ref, out_ref, inv_ref):
    size = t_ref.shape[1]
    row = lax.broadcasted_iota(jnp.int32, (size, size), 0)
    col = lax.broadcasted_iota(jnp.int32, (size, size), 1)
    eye = (row == col).astype(F32)

    def unpack(lot):
        packed = t_ref[lot]
        upper = jnp.where(row < col, packed, 0.0)
        lower = jnp.where(row > col, packed, 0.0)
        first = jnp.where(row <= col, packed, 0.0) + upper.T
        second = lower + lower.T + eye * d_ref[lot, 0:1, :]
        return first, second

    def inverse(matrix):
        diag = eye * matrix
        by_row = lax.rsqrt(jnp.sum(diag, axis=1, keepdims=True))
        by_col = lax.rsqrt(jnp.sum(diag, axis=0, keepdims=True))
        scaled = matrix * by_row * by_col
        bound = jnp.max(jnp.sum(jnp.abs(scaled), axis=0, keepdims=True), axis=1, keepdims=True)
        gain = 2.0 / bound
        start = eye * gain
        error = eye - scaled * gain
        approx = start + error * gain
        for _ in range(5):
            error = dot_one(error, error)
            approx = approx + dot_one(approx, error)
        rest = eye - dot_full(scaled, approx)
        size_of = jnp.sum(rest * rest)
        good = size_of < 0.25
        inv_ref[...] = jnp.where(good, approx + dot_full(approx, rest), start)

        def unfinished(state):
            step, size_of = state
            return jnp.logical_and(step < 64, jnp.logical_not(size_of < 1e-6))

        def improve(state):
            approx = inv_ref[...]
            rest = eye - dot_full(scaled, approx)
            inv_ref[...] = approx + dot_full(approx, rest)
            return state[0] + 1, jnp.sum(rest * rest)

        lax.while_loop(unfinished, improve, (jnp.int32(0), size_of))
        return inv_ref[...] * by_row * by_col

    m0, m1 = unpack(0)
    m2, m3 = unpack(1)
    inv1 = inverse(m1)
    alpha = dot_full(inv1, m0)
    cross = dot_full(inv1, m2)
    schur = m3 - dot_full(m2, cross)
    rhs = m1 - dot_full(m2, alpha)
    weight_q = dot_full(inverse(schur), rhs)
    weight_r = alpha - dot_full(cross, weight_q)
    out_ref[...] = (
        x_ref[...]
        + dot_pieces(pieces(r_ref[...], 3), pieces(weight_r, 3), NN)
        + dot_pieces(pieces(q_ref[...], 3), pieces(weight_q, 3), NN)
    )


def update(warm_start, residual, image, packed, diagonals):
    cols = warm_start.shape[1]
    vmem = pl.BlockSpec(memory_space=pltpu.VMEM)
    return pl.pallas_call(
        update_kernel,
        name="update",
        out_shape=jax.ShapeDtypeStruct(warm_start.shape, F32),
        in_specs=[vmem] * 5,
        out_specs=vmem,
        scratch_shapes=[pltpu.VMEM((cols, cols), F32)],
        compiler_params=pltpu.CompilerParams(vmem_limit_bytes=48 << 20),
    )(warm_start, residual, image, packed, diagonals)


def heads_kernel(groups, x_ref, picks_ref, flows_ref, out_ref, src, dst, ss, rs):
    nodes, cols = x_ref.shape
    scen = out_ref.shape[0]
    hyd = lax.axis_index("hyd")
    order = sorted(range(1, groups), key=lambda s: -min(s % 4, 4 - s % 4) - 2 * (s >= 4))
    order = order[: groups - 1]

    def mate(step):
        return lax.rem(hyd + step, groups)

    barrier = pltpu.get_barrier_semaphore()
    for step in order:
        pl.semaphore_signal(barrier, inc=1, device_id={"hyd": mate(step)}, device_id_type=MESH)

    x_parts = pieces(x_ref[...], 3)
    column = lax.broadcasted_iota(jnp.int32, (cols, scen), 0) + hyd * cols

    def scenario(owner):
        lanes = pl.ds(pl.multiple_of(owner * scen, scen), scen)
        picks, flows = picks_ref[:, lanes], flows_ref[:, lanes]
        total = jnp.zeros((cols, scen), F32)
        for slot in range(PICK):
            total = total + jnp.where(
                column == picks[slot : slot + 1, :], flows[slot : slot + 1, :], 0.0
            )
        return total

    def copy(step):
        return pltpu.make_async_remote_copy(
            src_ref=src.at[step],
            dst_ref=dst.at[step],
            send_sem=ss.at[step],
            recv_sem=rs.at[step],
            device_id={"hyd": mate(step)},
            device_id_type=MESH,
        )

    every = order + [0]
    waited = False
    for at in range(0, len(every), 2):
        pair = every[at : at + 2]
        block = jnp.concatenate([scenario(mate(step)) for step in pair], axis=1)
        both = dot_pieces(x_parts, pieces(block, 3), NN)
        for i, step in enumerate(pair):
            src[step] = both[:, i * scen : (i + 1) * scen]
        if not waited:
            pl.semaphore_wait(barrier, len(order))
            waited = True
        for step in pair:
            if step:
                copy(step).start()
    total = src[0]
    for step in order:
        copy(step).wait_recv()
    for step in order:
        total = total + dst[step]
    out_ref[...] = total.T
    for step in order:
        copy(step).wait_send()


def heads_of(responses, picks, flows, groups):
    nodes, cols = responses.shape
    scen = picks.shape[0] // groups
    dma = pltpu.SemaphoreType.DMA
    vmem = pl.BlockSpec(memory_space=pltpu.VMEM)
    return pl.pallas_call(
        functools.partial(heads_kernel, groups),
        name="heads",
        out_shape=jax.ShapeDtypeStruct((scen, nodes), F32),
        in_specs=[vmem] * 3,
        out_specs=vmem,
        scratch_shapes=[
            pltpu.VMEM((groups, nodes, scen), F32),
            pltpu.VMEM((groups, nodes, scen), F32),
            dma((groups,)),
            dma((groups,)),
        ],
        compiler_params=pltpu.CompilerParams(
            collective_id=1, has_side_effects=True, vmem_limit_bytes=48 << 20
        ),
    )(responses, picks.T, flows.T)


def fused_kernel(
    nz,
    groups,
    diag_in,
    ends_in,
    cond_in,
    bn_in,
    bc_in,
    hid_in,
    x_in,
    picks_in,
    flows_in,
    resp_ref,
    heads_ref,
    flag_ref,
    diag_ref,
    ends_ref,
    cond_ref,
    bn_ref,
    bc_ref,
    hid_ref,
    x_ref,
    picks_ref,
    flows_ref,
    r_ref,
    q_ref,
    a_ref,
    halo_src,
    halo_dst,
    t_buf,
    d_buf,
    core_t,
    core_d,
    cross_t,
    acc_t,
    acc_d,
    share_t,
    share_dd,
    t_all,
    d_all,
    part,
    mid_a,
    fin_a,
    mid_b,
    fin_b,
    in_sem,
    know,
    halo_ss,
    halo_rs,
    core_ss,
    core_rs,
    cd_ss,
    cd_rs,
    sh_ss,
    sh_rs,
    sd_ss,
    sd_rs,
    ag_ss,
    ag_rs,
    ad_ss,
    ad_rs,
    last_ss,
    last_rs,
    cr_ss,
    cr_rs,
    ca_ss,
    ca_rs,
    a1_ss,
    a1_rs,
    a2_ss,
    a2_rs,
    b1_ss,
    b1_rs,
    b2_ss,
    b2_rs,
):
    nodes, cols = x_ref.shape
    edges = ends_ref.shape[1]
    rim = bn_ref.shape[1]
    scen = heads_ref.shape[0]
    ny = groups // 2
    n_net = 4 * nz
    net = lax.axis_index("net")
    hyd = lax.axis_index("hyd")
    z = net // 4
    x_lo = lax.rem(net // 2, 2)
    core = lax.rem(net, 2)
    x_hi = hyd // ny
    y = lax.rem(hyd, ny)
    up, down = lax.rem(net + 1, n_net), lax.rem(net + n_net - 1, n_net)
    core_mate = net + 1 - 2 * core
    half = cols // 2

    def net_mate(key):
        return lax.rem(net + 4 * (key // 2) + (key % 2) * (2 - 4 * x_lo) + n_net, n_net)

    def z_mate(step):
        return lax.rem(net + 4 * step + n_net, n_net)

    def y_mate(step):
        return x_hi * ny + lax.rem(y + step, ny)

    hi_mate = (1 - x_hi) * ny + y

    keys = sorted(range(1, 2 * nz), key=lambda k: -min(k // 2, nz - k // 2))
    steps = sorted(range(nz), key=lambda s: -min(s, nz - s))
    near = [1] + ([2, 3, 2 * nz - 2, 2 * nz - 1] if nz > 2 else [2, 3])
    rounds = []
    reach = 1
    while 2 * reach <= nz // 2:
        rounds.append(reach)
        reach *= 2

    barrier = pltpu.get_barrier_semaphore()
    mates = [{"net": net_mate(k)} for k in near] + [{"net": up}, {"net": down}]
    mates += [{"hyd": hi_mate}] + [{"hyd": y_mate(s)} for s in range(1, ny)]
    for mate in mates:
        pl.semaphore_signal(barrier, inc=1, device_id=mate, device_id_type=MESH)

    loads = [
        pltpu.make_async_copy(whole, place, in_sem.at[at])
        for at, (whole, place) in enumerate(
            [
                (x_in, x_ref),
                (bn_in, bn_ref),
                (bc_in, bc_ref),
                (ends_in, ends_ref),
                (cond_in, cond_ref),
                (diag_in, diag_ref),
                (hid_in, hid_ref),
                (picks_in, picks_ref),
                (flows_in, flows_ref),
            ]
        )
    ]
    for load in loads:
        load.start()

    def learn(at):
        for step in (rounds[at], nz - rounds[at]):
            pl.semaphore_signal(
                know.at[at], inc=1, device_id={"net": z_mate(step)}, device_id_type=MESH
            )

    def learned(at):
        pl.semaphore_wait(know.at[at], 2)

    def remote(src, dst, ss, rs, mate):
        return pltpu.make_async_remote_copy(
            src_ref=src,
            dst_ref=dst,
            send_sem=ss,
            recv_sem=rs,
            device_id=mate if isinstance(mate, dict) else {"net": mate},
            device_id_type=MESH,
        )

    def gather(parts, stage):
        halo_src[stage] = dot_pieces(pick_b, parts, TN)

    for load in loads[:3]:
        load.wait()
    ids = jnp.concatenate([bn_ref[0:1, :], bn_ref[1:2, :]], axis=1)
    conds = jnp.concatenate([bc_ref[0:1, :], bc_ref[1:2, :]], axis=1)
    pick = (lax.broadcasted_iota(jnp.int32, (nodes, 2 * rim), 0) == ids).astype(F32)
    pick_b = [pick.astype(BF16)]
    couple = pieces(pick * conds, 3)
    x_parts = pieces(x_ref[...], 3)
    gather(x_parts, 0)
    for load in loads[3:]:
        load.wait()

    pl.semaphore_wait(barrier, len(mates))

    def build():
        node_iota = lax.broadcasted_iota(jnp.int32, (nodes, edges), 0)
        first = node_iota == ends_ref[0:1, :]
        second = node_iota == ends_ref[1:2, :]
        incidence = first.astype(F32) - second.astype(F32)
        incidence_b = incidence.astype(BF16)
        weights = jnp.concatenate(
            [cond_ref[i : i + 1, :] for i in range(cond_ref.shape[0])], axis=1
        )
        total = None
        for part_c in reversed(pieces(weights, 3)):
            term = lax.dot_general(
                (incidence * part_c.astype(F32)).astype(BF16),
                incidence_b,
                NT,
                preferred_element_type=F32,
            )
            total = term if total is None else total + term
        for part_c in reversed(pieces(conds, 3)):
            total = total + lax.dot_general(
                (pick * part_c.astype(F32)).astype(BF16),
                pick_b[0],
                NT,
                preferred_element_type=F32,
            )
        square = lax.broadcasted_iota(jnp.int32, (nodes, nodes), 0) == lax.broadcasted_iota(
            jnp.int32, (nodes, nodes), 1
        )
        a_ref[...] = total + jnp.where(square, diag_ref[...], 0.0)

    def halo(stage):
        upper, lower = pl.ds(rim, rim), pl.ds(0, rim)
        at = 2 * stage
        return [
            remote(
                halo_src.at[stage, upper],
                halo_dst.at[stage, lower],
                halo_ss.at[at],
                halo_rs.at[at],
                up,
            ),
            remote(
                halo_src.at[stage, lower],
                halo_dst.at[stage, upper],
                halo_ss.at[at + 1],
                halo_rs.at[at + 1],
                down,
            ),
        ]

    def local(parts):
        return dot_pieces(pieces(a_ref[...], 3), parts, NN)

    def coupled(stage):
        return dot_pieces(couple, pieces(halo_dst[stage], 3), NN)

    tri_row = lax.broadcasted_iota(jnp.int32, (half, half), 0)
    tri_col = lax.broadcasted_iota(jnp.int32, (half, half), 1)
    half_eye = (tri_row == tri_col).astype(F32)
    base = [0, half, 3 * half]
    rows_of = [half // 2, half, half // 2]
    spot_rows = [2 * rows // nz for rows in rows_of]

    def pack(place, matrix):
        folded = jnp.where(tri_row <= tri_col, matrix[:half, :half], matrix[half:, half:])
        t_buf[place : place + half, 0:half] = folded
        t_buf[place : place + half, half:cols] = matrix[:half, half:]
        return jnp.sum(half_eye * matrix[half:, half:], axis=0, keepdims=True)

    def unpack(place, diagonal):
        folded, cross = t_all[place : place + half, 0:half], t_all[place : place + half, half:cols]
        upper = jnp.where(tri_row < tri_col, folded, 0.0)
        lower = jnp.where(tri_row > tri_col, folded, 0.0)
        first = jnp.where(tri_row <= tri_col, folded, 0.0) + upper.T
        second = lower + lower.T + half_eye * diagonal
        return jnp.concatenate(
            [
                jnp.concatenate([first, cross], axis=1),
                jnp.concatenate([cross.T, second], axis=1),
            ],
            axis=0,
        )

    def lot_rows(lot, whose):
        rows = rows_of[lot]
        return pl.ds(pl.multiple_of(base[lot] + whose * rows, rows), rows)

    def own_rows(lot):
        return pl.ds(base[lot] // 2, rows_of[lot])

    def core_copy(lot):
        return remote(
            t_buf.at[lot_rows(lot, 1 - core)],
            core_t.at[own_rows(lot)],
            core_ss.at[lot],
            core_rs.at[lot],
            core_mate,
        )

    def core_sum(lot):
        core_copy(lot).wait_recv()
        acc_t[own_rows(lot)] = t_buf[lot_rows(lot, core)] + core_t[own_rows(lot)]

    def core_d_copy(at):
        return remote(d_buf.at[at], core_d.at[at], cd_ss.at[at], cd_rs.at[at], core_mate)

    def core_d_sum(at):
        core_d_copy(at).wait_recv()
        acc_d[at] = d_buf[at] + core_d[at]

    mine = x_lo == lax.rem(z, 2)

    def spot(lot, zc, start):
        rows = spot_rows[lot]
        return (
            pl.ds(pl.multiple_of(start + (zc // 2) * rows, rows), rows),
            pl.ds(pl.multiple_of(lax.rem(zc, 2) * half, half), half),
        )

    x_mate = net + 2 - 4 * x_lo
    own_lanes = pl.ds(pl.multiple_of(x_lo * half, half), half)
    far_lanes = pl.ds(pl.multiple_of((1 - x_lo) * half, half), half)
    odd = lax.rem(x_lo + z, 2)

    def cross_copy(lot):
        return remote(
            acc_t.at[own_rows(lot), far_lanes],
            cross_t.at[own_rows(lot)],
            cr_ss.at[lot],
            cr_rs.at[lot],
            x_mate,
        )

    def cross_start(lot):
        if lot in CROSS_FIRST:
            cross_copy(lot).start()

    def cross_sum(lot):
        if lot in CROSS_FIRST:
            cross_copy(lot).wait_recv()
            acc_t[own_rows(lot), own_lanes] = (
                acc_t[own_rows(lot), own_lanes] + cross_t[own_rows(lot)]
            )

    def share_copy(lot, step):
        zc = lax.rem(z + step, nz)
        if lot in CROSS_FIRST:
            slot = step - 1
        else:
            slot = 2 * step - 1 + (lax.rem(x_lo + zc, 2) if step else 1)
        rows, lanes = spot(lot, zc, base[lot] // 2)
        return remote(
            acc_t.at[rows, lanes],
            share_t.at[lot, slot, pl.ds(0, spot_rows[lot])],
            sh_ss.at[lot, step],
            sh_rs.at[lot, slot],
            4 * zc + 2 * lax.rem(zc, 2) + core,
        )

    def share_slots(lot):
        return nz - 1 if lot in CROSS_FIRST else 2 * nz - 1

    def share_arrival(lot, slot):
        rows, lanes = spot(lot, z, base[lot] // 2)
        return remote(
            acc_t.at[rows, lanes],
            share_t.at[lot, slot, pl.ds(0, spot_rows[lot])],
            sh_ss.at[lot, 0],
            sh_rs.at[lot, slot],
            core_mate,
        )

    def share_each(lot, act):
        if lot in CROSS_FIRST:
            for step in sorted(range(2, nz, 2), key=lambda s: -min(s, nz - s)):
                act(share_copy(lot, step + odd))
        else:
            for step in steps:
                if step:
                    act(share_copy(lot, step))

        @pl.when(jnp.logical_not(mine))
        def _():
            act(share_copy(lot, 1 if lot in CROSS_FIRST else 0))

    def share_start(lot):
        share_each(lot, lambda copy: copy.start())

    def all_spot(lot, zc):
        return spot(lot, zc, base[lot] + core * rows_of[lot])

    def all_copy(lot, zc, key):
        rows, lanes = all_spot(lot, zc)
        return remote(
            t_all.at[rows, lanes],
            t_all.at[rows, lanes],
            ag_ss.at[lot, key - 1],
            ag_rs.at[lot, zc],
            net_mate(key),
        )

    def all_keys(lot):
        return [key for key in keys if key % 2 == 0 or lot not in CROSS_LAST]

    def share_sum(lot):
        @pl.when(mine)
        def _():
            for slot in range(share_slots(lot)):
                share_arrival(lot, slot).wait_recv()
            rows, lanes = spot(lot, z, base[lot] // 2)
            total = acc_t[rows, lanes]
            for slot in range(share_slots(lot)):
                total = total + share_t[lot, slot, 0 : spot_rows[lot]]
            rows, lanes = all_spot(lot, z)
            t_all[rows, lanes] = total
            for key in all_keys(lot):
                all_copy(lot, z, key).start()

    owner_z = [nz // 4, (3 * nz) // 4]

    def is_owner(at):
        return jnp.logical_and(z == owner_z[at], x_lo == 0)

    def share_d(at, slot, mate):
        return remote(
            acc_d.at[at], share_dd.at[at, slot], sd_ss.at[at], sd_rs.at[at, slot], mate
        )

    def all_d(at, key):
        return remote(
            d_all.at[at], d_all.at[at], ad_ss.at[at, key - 1], ad_rs.at[at], net_mate(key)
        )

    def share_d_start(at):
        @pl.when(jnp.logical_not(is_owner(at)))
        def _():
            slot = 2 * lax.rem(owner_z[at] - z + nz, nz) + x_lo - 1
            share_d(at, slot, 4 * owner_z[at] + core).start()

    def share_d_sum(at):
        @pl.when(is_owner(at))
        def _():
            total_d = acc_d[at]
            for slot in range(2 * nz - 1):
                share_d(at, slot, core_mate).wait_recv()
            for slot in range(2 * nz - 1):
                total_d = total_d + share_dd[at, slot]
            d_all[at] = total_d
            for key in keys:
                all_d(at, key).start()

    def all_d_finish(at):
        @pl.when(jnp.logical_not(is_owner(at)))
        def _():
            all_d(at, 1).wait_recv()

    def last_copy(lot, whose):
        return remote(
            t_all.at[lot_rows(lot, whose)],
            t_all.at[lot_rows(lot, whose)],
            last_ss.at[lot],
            last_rs.at[lot],
            core_mate,
        )

    def level_copy(lot, lanes):
        rows = lot_rows(lot, core)
        return remote(
            t_all.at[rows, lanes], t_all.at[rows, lanes], ca_ss.at[lot], ca_rs.at[lot], x_mate
        )

    def all_finish(lot):
        if lot in CROSS_LAST:
            for step in range(2, nz, 2):
                all_copy(lot, lax.rem(z + step + odd, nz), 1).wait_recv()
        else:
            for step in range(1, nz):
                all_copy(lot, lax.rem(z + step, nz), 1).wait_recv()

        @pl.when(jnp.logical_not(mine))
        def _():
            zc = lax.rem(z + 1, nz) if lot in CROSS_LAST else z
            all_copy(lot, zc, 1).wait_recv()

        if lot in CROSS_LAST:
            level_copy(lot, own_lanes).start()
        else:
            last_copy(lot, core).start()

    def level(lot):
        if lot in CROSS_LAST:
            level_copy(lot, far_lanes).wait_recv()
            last_copy(lot, core).start()

    def drain(lot):
        core_copy(lot).wait_send()
        share_each(lot, lambda copy: copy.wait_send())
        if lot in CROSS_FIRST:
            cross_copy(lot).wait_send()
        if lot in CROSS_LAST:
            level_copy(lot, own_lanes).wait_send()

        @pl.when(mine)
        def _():
            for key in all_keys(lot):
                all_copy(lot, z, key).wait_send()

        last_copy(lot, core).wait_send()

    def drain_d(at):
        core_d_copy(at).wait_send()

        @pl.when(jnp.logical_not(is_owner(at)))
        def _():
            share_d(at, 0, core_mate).wait_send()

        @pl.when(is_owner(at))
        def _():
            for key in keys:
                all_d(at, key).wait_send()

    halos = [halo(stage) for stage in range(3)]
    for copy in halos[0]:
        copy.start()
    if rounds:
        learn(0)
    build()
    hyd_local = hid_ref[...] - net * nodes
    demand = (lax.broadcasted_iota(jnp.int32, (nodes, cols), 0) == hyd_local).astype(F32)
    part_r = demand - local(x_parts)
    if rounds:
        learned(0)
        if len(rounds) > 1:
            learn(1)
    for copy in halos[0]:
        copy.wait_recv()
    residual = part_r + coupled(0)
    r_parts = pieces(residual, 3)
    gather(r_parts, 1)
    for copy in halos[1]:
        copy.start()
    r_ref[...] = residual
    d0 = pack(base[0], dot_pieces(r_parts, r_parts, TN))
    core_copy(0).start()
    if len(rounds) > 1:
        learned(1)
        if len(rounds) > 2:
            learn(2)
    part_q = local(r_parts)
    core_sum(0)
    cross_start(0)
    for copy in halos[1]:
        copy.wait_recv()
    image = part_q - coupled(1)
    q_parts = pieces(image, 3)
    gather(q_parts, 2)
    for copy in halos[2]:
        copy.start()
    q_ref[...] = image
    for at in range(2, len(rounds)):
        learned(at)
        if at + 1 < len(rounds):
            learn(at + 1)
    cross_sum(0)
    share_start(0)
    d1 = pack(base[1], dot_pieces(r_parts, q_parts, TN))
    d2 = pack(base[1] + half, dot_pieces(q_parts, q_parts, TN))
    d_buf[0] = jnp.concatenate([d0, d1, d2, jnp.zeros((5, half), F32)], axis=0)
    core_copy(1).start()
    core_d_copy(0).start()
    part_w = local(q_parts)
    core_d_sum(0)
    share_d_start(0)
    core_sum(1)
    cross_start(1)
    if 1 not in CROSS_FIRST:
        share_start(1)
    for copy in halos[2]:
        copy.wait_recv()
    d3 = pack(base[2], dot_pieces(q_parts, pieces(part_w - coupled(2), 3), TN))
    d_buf[1] = jnp.broadcast_to(d3, (8, half))
    core_copy(2).start()
    core_d_copy(1).start()
    if 1 in CROSS_FIRST:
        cross_sum(1)
        share_start(1)
    core_d_sum(1)
    share_d_start(1)
    core_sum(2)
    cross_start(2)
    cross_sum(2)
    share_start(2)
    share_sum(0)
    share_d_sum(0)
    share_sum(1)
    share_d_sum(1)
    share_sum(2)
    all_finish(0)
    level(0)
    all_finish(1)
    level(1)
    all_d_finish(0)
    last_copy(0, 1 - core).wait_recv()
    last_copy(1, 1 - core).wait_recv()

    row = lax.broadcasted_iota(jnp.int32, (cols, cols), 0)
    col = lax.broadcasted_iota(jnp.int32, (cols, cols), 1)
    eye = (row == col).astype(F32)

    def inverse(matrix):
        diag = eye * matrix
        by_row = lax.rsqrt(jnp.sum(diag, axis=1, keepdims=True))
        by_col = lax.rsqrt(jnp.sum(diag, axis=0, keepdims=True))
        scaled = matrix * by_row * by_col
        bound = jnp.max(jnp.sum(jnp.abs(scaled), axis=0, keepdims=True), axis=1, keepdims=True)
        gain = 2.0 / bound
        error = eye - scaled * gain
        approx = eye * gain + error * gain
        for _ in range(5):
            error = dot_one(error, error)
            approx = approx + dot_one(approx, error)
        approx = approx + dot_one(approx, eye - dot_full(scaled, approx))
        rest = eye - dot_full(scaled, approx)
        approx = approx + dot_one(approx, rest)
        left = jnp.sum(jnp.sum(rest * rest, axis=0, keepdims=True), axis=1, keepdims=True)
        return approx * by_row * by_col, left

    m0 = unpack(base[0], d_all[0, 0:1, :])
    m1 = unpack(base[1], d_all[0, 1:2, :])
    m2 = unpack(base[1] + half, d_all[0, 2:3, :])
    inv1, left1 = inverse(m1)
    all_finish(2)
    level(2)
    all_d_finish(1)
    alpha = dot_full(inv1, m0)
    cross = dot_full(inv1, m2)
    rhs = m1 - dot_full(m2, alpha)
    fill = dot_full(m2, cross)
    last_copy(2, 1 - core).wait_recv()
    inv2, left2 = inverse(unpack(base[2], d_all[1, 0:1, :]) - fill)
    weight_q = dot_full(inv2, rhs)
    weight_r = alpha - dot_full(cross, weight_q)
    converged = jnp.logical_and(left1 < 2e-5, left2 < 2e-5)
    flag = jnp.broadcast_to(jnp.where(converged, 0.0, 1.0), (8, scen))
    answer = (
        x_ref[...]
        + dot_pieces(pieces(r_ref[...], 2), pieces(weight_r, 2), NN)
        + dot_pieces(pieces(q_ref[...], 2), pieces(weight_q, 2), NN)
    )
    resp_ref[...] = answer
    a_parts = pieces(answer, 2)
    column = lax.broadcasted_iota(jnp.int32, (cols, scen), 0) + hyd * cols

    def scenario(owner):
        lanes = pl.ds(pl.multiple_of(owner * scen, scen), scen)
        picks, flows = picks_ref[:, lanes], flows_ref[:, lanes]
        total = jnp.zeros((cols, scen), F32)
        for slot in range(PICK):
            total = total + jnp.where(
                column == picks[slot : slot + 1, :], flows[slot : slot + 1, :], 0.0
            )
        return total

    deep = mid_a.shape[1]
    rows_a, rows_b = pl.ds(0, deep), pl.ds(deep, part.shape[1] - deep)

    def a1_copy(dy):
        return remote(
            part.at[ny + dy, rows_a], mid_a.at[dy], a1_ss.at[dy], a1_rs.at[dy], {"hyd": hi_mate}
        )

    def a2_copy(dy):
        return remote(
            part.at[dy, rows_a],
            fin_a.at[dy - 1],
            a2_ss.at[dy - 1],
            a2_rs.at[dy - 1],
            {"hyd": y_mate(dy)},
        )

    def b1_copy(fx, dy):
        return remote(
            part.at[fx * ny + dy, rows_b],
            mid_b.at[fx, dy - 1],
            b1_ss.at[fx, dy - 1],
            b1_rs.at[fx, dy - 1],
            {"hyd": y_mate(dy)},
        )

    def b2_copy():
        return remote(part.at[ny, rows_b], fin_b, b2_ss.at[0], b2_rs.at[0], {"hyd": hi_mate})

    order = sorted(range(1, ny), key=lambda s: -min(s, ny - s)) + [0]
    every = [(1, dy) for dy in order] + [(0, dy) for dy in order]
    for at in range(0, groups, 2):
        pair = every[at : at + 2]
        block = jnp.concatenate(
            [scenario((x_hi if fx == 0 else 1 - x_hi) * ny + lax.rem(y + dy, ny)) for fx, dy in pair],
            axis=1,
        )
        both = dot_pieces(a_parts, pieces(block, 2), NN)
        for i, (fx, dy) in enumerate(pair):
            part[fx * ny + dy, 0:8] = flag
            part[fx * ny + dy, 8 : nodes + 8] = both[:, i * scen : (i + 1) * scen]
            if fx:
                a1_copy(dy).start()
            if dy:
                b1_copy(fx, dy).start()

    def a_step(dy):
        a1_copy(dy).wait_recv()
        part[dy, rows_a] = part[dy, rows_a] + mid_a[dy]
        if dy:
            a2_copy(dy).start()

    half_way = (len(order) - 1) // 2 + 1
    for dy in order[:half_way]:
        a_step(dy)
    total_b = part[ny, rows_b]
    for dy in range(1, ny):
        b1_copy(1, dy).wait_recv()
        total_b = total_b + mid_b[1, dy - 1]
    part[ny, rows_b] = total_b
    b2_copy().start()
    for dy in order[half_way:]:
        a_step(dy)
    for stage in halos:
        for copy in stage:
            copy.wait_send()
    for lot in range(3):
        drain(lot)
    drain_d(0)
    drain_d(1)
    total_b = part[0, rows_b]
    for dy in range(1, ny):
        b1_copy(0, dy).wait_recv()
        total_b = total_b + mid_b[0, dy - 1]
    b2_copy().wait_recv()
    total_b = total_b + fin_b[...]
    total_a = part[0, rows_a]
    for dy in order[:-1]:
        a2_copy(dy).wait_recv()
        total_a = total_a + fin_a[dy - 1]
    flag_ref[0, 0] = jnp.where(jnp.max(total_a[0:8]) > 0.0, 1, 0).astype(jnp.int32)
    heads_ref[...] = jnp.concatenate([total_a[8:], total_b], axis=0).T
    for dy in range(ny):
        a1_copy(dy).wait_send()
        if dy:
            a2_copy(dy).wait_send()
            b1_copy(0, dy).wait_send()
            b1_copy(1, dy).wait_send()
    b2_copy().wait_send()


def fused(
    diagonal,
    edge_ends,
    edge_cond,
    bnd_nodes,
    bnd_cond,
    hyd_ids,
    warm_start,
    picks,
    flows,
    n_net,
    groups,
):
    nz = n_net // 4
    ny = groups // 2
    nodes, cols = warm_start.shape
    rim = bnd_nodes.shape[2]
    edges = edge_cond.shape[0]
    scen = picks.shape[0] // groups
    half = cols // 2
    peers = 2 * nz - 1
    spot = 2 * half // nz
    deep = 8 + (nodes * SPLIT // 64) // 8 * 8
    dma = pltpu.SemaphoreType.DMA
    vmem = pl.BlockSpec(memory_space=pltpu.VMEM)
    return pl.pallas_call(
        functools.partial(fused_kernel, nz, groups),
        name="fused",
        out_shape=[
            jax.ShapeDtypeStruct((nodes, cols), F32),
            jax.ShapeDtypeStruct((scen, nodes), F32),
            jax.ShapeDtypeStruct((1, 1), jnp.int32),
        ],
        in_specs=[pl.BlockSpec(memory_space=pltpu.HBM)] * 9,
        out_specs=[vmem] * 2 + [pl.BlockSpec(memory_space=pltpu.SMEM)],
        scratch_shapes=[
            pltpu.VMEM((1, nodes), F32),
            pltpu.VMEM((2, edges), jnp.int32),
            pltpu.VMEM((edges // 128, 128), F32),
            pltpu.VMEM((2, rim), jnp.int32),
            pltpu.VMEM((2, rim), F32),
            pltpu.VMEM((1, cols), jnp.int32),
            pltpu.VMEM((nodes, cols), F32),
            pltpu.VMEM((PICK, scen * groups), jnp.int32),
            pltpu.VMEM((PICK, scen * groups), F32),
            pltpu.VMEM((nodes, cols), F32),
            pltpu.VMEM((nodes, cols), F32),
            pltpu.VMEM((nodes, nodes), F32),
            pltpu.VMEM((3, 2 * rim, cols), F32),
            pltpu.VMEM((3, 2 * rim, cols), F32),
            pltpu.VMEM((2 * cols, cols), F32),
            pltpu.VMEM((2, 8, half), F32),
            pltpu.VMEM((cols, cols), F32),
            pltpu.VMEM((2, 8, half), F32),
            pltpu.VMEM((cols, half), F32),
            pltpu.VMEM((cols, cols), F32),
            pltpu.VMEM((2, 8, half), F32),
            pltpu.VMEM((3, peers, spot, half), F32),
            pltpu.VMEM((2, peers, 8, half), F32),
            pltpu.VMEM((2 * cols, cols), F32),
            pltpu.VMEM((2, 8, half), F32),
            pltpu.VMEM((groups, nodes + 8, scen), F32),
            pltpu.VMEM((ny, deep, scen), F32),
            pltpu.VMEM((ny - 1, deep, scen), F32),
            pltpu.VMEM((2, ny - 1, nodes + 8 - deep, scen), F32),
            pltpu.VMEM((nodes + 8 - deep, scen), F32),
            dma((9,)),
            pltpu.SemaphoreType.REGULAR((3,)),
            dma((6,)),
            dma((6,)),
            dma((3,)),
            dma((3,)),
            dma((2,)),
            dma((2,)),
            dma((3, nz)),
            dma((3, peers)),
            dma((2,)),
            dma((2, peers)),
            dma((3, peers)),
            dma((3, nz)),
            dma((2, peers)),
            dma((2,)),
            dma((3,)),
            dma((3,)),
            dma((3,)),
            dma((3,)),
            dma((3,)),
            dma((3,)),
            dma((ny,)),
            dma((ny,)),
            dma((ny - 1,)),
            dma((ny - 1,)),
            dma((2, ny - 1)),
            dma((2, ny - 1)),
            dma((1,)),
            dma((1,)),
        ],
        compiler_params=pltpu.CompilerParams(
            collective_id=2, has_side_effects=True, vmem_limit_bytes=48 << 20
        ),
    )(
        diagonal[None, :],
        edge_ends.T,
        edge_cond.reshape(edges // 128, 128),
        bnd_nodes[0],
        bnd_cond[0],
        hyd_ids[None, :],
        warm_start,
        picks.T,
        flows.T,
    )


def settle_kernel(resp_in, heads_in, resp_out, heads_out, sems):
    copies = [
        pltpu.make_async_copy(resp_in, resp_out, sems.at[0]),
        pltpu.make_async_copy(heads_in, heads_out, sems.at[1]),
    ]
    for copy in copies:
        copy.start()
    for copy in copies:
        copy.wait()


def settle(responses, heads):
    anywhere = pl.BlockSpec(memory_space=pl.ANY)
    return pl.pallas_call(
        settle_kernel,
        name="settle",
        out_shape=[jax.ShapeDtypeStruct(a.shape, a.dtype) for a in (responses, heads)],
        in_specs=[anywhere] * 2,
        out_specs=[anywhere] * 2,
        scratch_shapes=[pltpu.SemaphoreType.DMA((2,))],
    )(responses, heads)


def per_device(
    diagonal, edge_ends, edge_cond, bnd_nodes, bnd_cond, hyd_ids, warm_start, scen_picks, scen_flows
):
    n_net, groups = lax.axis_size("net"), lax.axis_size("hyd")
    local = (diagonal, edge_ends, edge_cond, bnd_nodes, bnd_cond, hyd_ids, warm_start)
    responses, heads, flag = fused(*local, scen_picks, scen_flows, n_net, groups)

    def keep(responses, heads):
        return settle(responses, heads)

    def redo(responses, heads):
        residual, image, packed, diagonals = moments(*local, n_net)
        responses = update(warm_start, residual, image, packed, diagonals)
        return settle(responses, heads_of(responses, scen_picks, scen_flows, groups))

    return lax.switch(flag[0, 0], [keep, redo], responses, heads)


def solution(mesh):
    placed = (
        P("net"),
        P("net", None),
        P("net"),
        P("net", None, None),
        P("net", None, None),
        P("hyd"),
        P("net", "hyd"),
        P(),
        P(),
    )
    return jax.shard_map(
        per_device,
        mesh=mesh,
        in_specs=placed,
        out_specs=(P("net", "hyd"), P("hyd", "net")),
        check_vma=False,
    )
```

```python
import functools

import jax
import jax.numpy as jnp
from jax import lax
from jax.experimental import pallas as pl
from jax.experimental.pallas import tpu as pltpu
from jax.sharding import PartitionSpec as P

MESH = pl.DeviceIdType.MESH
F32 = jnp.float32
BF16 = jnp.bfloat16
NN = (((1,), (0,)), ((), ()))
TN = (((0,), (0,)), ((), ()))
NT = (((1,), (1,)), ((), ()))
PICK = 4
SPLIT = 38
CROSS_FIRST = (0,)
CROSS_LAST = (0,)


def pieces(value, count):
    out = []
    for step in range(count):
        part = value.astype(BF16)
        out.append(part)
        if step + 1 < count:
            value = value - part.astype(F32)
    return out


def dot_pieces(first, second, dims):
    depth = max(len(first), len(second))
    total = None
    for level in reversed(range(depth)):
        for i, left in enumerate(first):
            j = level - i
            if 0 <= j < len(second):
                term = lax.dot_general(left, second[j], dims, preferred_element_type=F32)
                total = term if total is None else total + term
    return total


def dot_full(first, second, dims=NN):
    return lax.dot_general(
        first, second, dims, precision=lax.Precision.HIGHEST, preferred_element_type=F32
    )


def dot_one(first, second):
    return lax.dot_general(
        first.astype(BF16), second.astype(BF16), NN, preferred_element_type=F32
    )


def moments_kernel(
    nz,
    diag_ref,
    ends_ref,
    cond_ref,
    bn_ref,
    bc_ref,
    hid_ref,
    x_ref,
    r_ref,
    q_ref,
    t_out,
    d_out,
    a_ref,
    halo_src,
    halo_dst,
    t_buf,
    d_buf,
    core_t,
    core_d,
    acc_t,
    acc_d,
    zr_t,
    zr_d,
    xs,
    xr,
    halo_ss,
    halo_rs,
    core_ss,
    core_rs,
    zr_ss,
    zr_rs,
    x_ss,
    x_rs,
    ag_ss,
    ag_rs,
    fin_ss,
    fin_rs,
):
    nodes, cols = x_ref.shape
    edges = cond_ref.shape[1]
    rim = bn_ref.shape[1]
    n_net = 4 * nz
    net = lax.axis_index("net")
    z = net // 4
    x_lo = lax.rem(net // 2, 2)
    core = lax.rem(net, 2)
    up, down = lax.rem(net + 1, n_net), lax.rem(net + n_net - 1, n_net)
    core_mate = net + 1 - 2 * core
    x_mate = net + 2 - 4 * x_lo

    def z_mate(step):
        return lax.rem(net + 4 * step, n_net)

    barrier = pltpu.get_barrier_semaphore()
    order = sorted(range(1, nz), key=lambda s: -min(s, nz - s))
    mates = [z_mate(s) for s in order] + [x_mate, up, down]
    for mate in mates:
        pl.semaphore_signal(barrier, inc=1, device_id={"net": mate}, device_id_type=MESH)

    def remote(src, dst, ss, rs, mate):
        return pltpu.make_async_remote_copy(
            src_ref=src,
            dst_ref=dst,
            send_sem=ss,
            recv_sem=rs,
            device_id={"net": mate},
            device_id_type=MESH,
        )

    node_iota = lax.broadcasted_iota(jnp.int32, (nodes, edges), 0)
    first = node_iota == ends_ref[0:1, :]
    second = node_iota == ends_ref[1:2, :]
    incidence = first.astype(F32) - second.astype(F32)
    ids = jnp.concatenate([bn_ref[0:1, :], bn_ref[1:2, :]], axis=1)
    conds = jnp.concatenate([bc_ref[0:1, :], bc_ref[1:2, :]], axis=1)
    pick = (lax.broadcasted_iota(jnp.int32, (nodes, 2 * rim), 0) == ids).astype(F32)
    pick_b = [pick.astype(BF16)]
    x_parts = pieces(x_ref[...], 3)

    def gather(parts, stage):
        halo_src[stage] = dot_pieces(pick_b, parts, TN)

    gather(x_parts, 0)
    incidence_b = incidence.astype(BF16)
    total = None
    for part in reversed(pieces(cond_ref[...], 3)):
        term = lax.dot_general(
            (incidence * part.astype(F32)).astype(BF16), incidence_b, NT, preferred_element_type=F32
        )
        total = term if total is None else total + term
    for part in reversed(pieces(conds, 3)):
        total = total + lax.dot_general(
            (pick * part.astype(F32)).astype(BF16), pick_b[0], NT, preferred_element_type=F32
        )
    square = lax.broadcasted_iota(jnp.int32, (nodes, nodes), 0) == lax.broadcasted_iota(
        jnp.int32, (nodes, nodes), 1
    )
    a_ref[...] = total + jnp.where(square, diag_ref[...], 0.0)
    couple = pieces(pick * conds, 3)

    pl.semaphore_wait(barrier, len(mates))

    def halo(stage):
        upper, lower = pl.ds(rim, rim), pl.ds(0, rim)
        return [
            remote(
                halo_src.at[stage, upper],
                halo_dst.at[stage, lower],
                halo_ss.at[2 * stage],
                halo_rs.at[2 * stage],
                up,
            ),
            remote(
                halo_src.at[stage, lower],
                halo_dst.at[stage, upper],
                halo_ss.at[2 * stage + 1],
                halo_rs.at[2 * stage + 1],
                down,
            ),
        ]

    def local(parts):
        return dot_pieces(pieces(a_ref[...], 3), parts, NN)

    def coupled(stage):
        return dot_pieces(couple, pieces(halo_dst[stage], 3), NN)

    halos = [halo(stage) for stage in range(3)]
    for copy in halos[0]:
        copy.start()
    hyd_local = hid_ref[...] - net * nodes
    demand = (lax.broadcasted_iota(jnp.int32, (nodes, cols), 0) == hyd_local).astype(F32)
    part_r = demand - local(x_parts)
    for copy in halos[0]:
        copy.wait_recv()
    residual = part_r + coupled(0)
    r_parts = pieces(residual, 3)
    gather(r_parts, 1)
    for copy in halos[1]:
        copy.start()
    r_ref[...] = residual
    part_q = local(r_parts)
    m0 = dot_pieces(r_parts, r_parts, TN)
    for copy in halos[1]:
        copy.wait_recv()
    image = part_q - coupled(1)
    q_parts = pieces(image, 3)
    gather(q_parts, 2)
    for copy in halos[2]:
        copy.start()
    q_ref[...] = image

    row = lax.broadcasted_iota(jnp.int32, (cols, cols), 0)
    col = lax.broadcasted_iota(jnp.int32, (cols, cols), 1)

    half = cols // 2
    chunk = half // nz

    def pack(lot, upper_m, lower_m):
        t_buf[lot] = jnp.where(row <= col, upper_m, lower_m)
        diagonal = jnp.sum(jnp.where(row == col, lower_m, 0.0), axis=0, keepdims=True)
        d_buf[lot] = jnp.broadcast_to(diagonal, (8, cols))

    def core_copies(lot):
        other = pl.ds(pl.multiple_of((1 - core) * half, half), half)
        return [
            remote(
                t_buf.at[lot, other],
                core_t.at[lot],
                core_ss.at[2 * lot],
                core_rs.at[2 * lot],
                core_mate,
            ),
            remote(
                d_buf.at[lot],
                core_d.at[lot],
                core_ss.at[2 * lot + 1],
                core_rs.at[2 * lot + 1],
                core_mate,
            ),
        ]

    def core_sum(lot):
        mine = pl.ds(pl.multiple_of(core * half, half), half)
        acc_t[lot] = t_buf[lot, mine] + core_t[lot]
        acc_d[lot] = d_buf[lot] + core_d[lot]

    owner_z = [nz // 4, (3 * nz) // 4]

    def z_copies(lot):
        out = []
        for step in order:
            owner = lax.rem(z + step, nz)
            rows = pl.ds(pl.multiple_of(owner * chunk, chunk), chunk)
            out.append(
                remote(
                    acc_t.at[lot, rows],
                    zr_t.at[lot, step - 1],
                    zr_ss.at[lot, step - 1],
                    zr_rs.at[lot, step - 1],
                    z_mate(step),
                )
            )
        return out

    def d_copy(lot, slot, mate):
        return remote(
            acc_d.at[lot],
            zr_d.at[lot, slot],
            zr_ss.at[lot, nz - 1],
            zr_rs.at[lot, nz - 1 + slot],
            mate,
        )

    def z_start(lot):
        for copy in z_copies(lot):
            copy.start()
        to_owner = lax.rem(owner_z[lot] - z + nz, nz)

        @pl.when(to_owner != 0)
        def _():
            d_copy(lot, to_owner - 1, lax.rem(net + 4 * to_owner, n_net)).start()

    def x_copy(lot):
        return remote(xs.at[lot], xr.at[lot], x_ss.at[lot], x_rs.at[lot], x_mate)

    def z_sum(lot):
        for copy in z_copies(lot):
            copy.wait_recv()
        mine = pl.ds(pl.multiple_of(z * chunk, chunk), chunk)
        total = acc_t[lot, mine]
        for step in range(1, nz):
            total = total + zr_t[lot, step - 1]
        xs[lot, 0:chunk] = total
        xs[lot, chunk : chunk + 8] = acc_d[lot]

        @pl.when(z == owner_z[lot])
        def _():
            total_d = acc_d[lot]
            for slot in range(nz - 1):
                d_copy(lot, slot, z_mate(slot + 1)).wait_recv()
            for slot in range(nz - 1):
                total_d = total_d + zr_d[lot, slot]
            xs[lot, chunk : chunk + 8] = total_d

        x_copy(lot).start()

    def full_rows(index):
        return pl.ds(pl.multiple_of(core * half + index * chunk, chunk), chunk)

    def ag_copies(lot, received):
        out = []
        for step in order:
            owner = lax.rem(z + nz - step, nz) if received else z
            out.append(
                remote(
                    t_out.at[lot, full_rows(owner)],
                    t_out.at[lot, full_rows(owner)],
                    ag_ss.at[lot, step - 1],
                    ag_rs.at[lot, step - 1],
                    z_mate(step),
                )
            )
        return out

    def agd_copy(lot, step):
        return remote(
            d_out.at[lot],
            d_out.at[lot],
            ag_ss.at[lot, nz - 1 + step - 1],
            ag_rs.at[lot, nz - 1],
            z_mate(step),
        )

    def x_sum(lot):
        x_copy(lot).wait_recv()
        t_out[lot, full_rows(z)] = xs[lot, 0:chunk] + xr[lot, 0:chunk]

        @pl.when(z == owner_z[lot])
        def _():
            d_out[lot] = xs[lot, chunk : chunk + 8] + xr[lot, chunk : chunk + 8]
            for step in order:
                agd_copy(lot, step).start()

        for copy in ag_copies(lot, False):
            copy.start()

    def fin_copy(lot, whose):
        rows = pl.ds(pl.multiple_of(whose * half, half), half)
        return remote(
            t_out.at[lot, rows], t_out.at[lot, rows], fin_ss.at[lot], fin_rs.at[lot], core_mate
        )

    def ag_finish(lot):
        for copy in ag_copies(lot, True):
            copy.wait_recv()
        fin_copy(lot, core).start()

        @pl.when(z != owner_z[lot])
        def _():
            agd_copy(lot, 1).wait_recv()

    def finish(lot):
        fin_copy(lot, 1 - core).wait_recv()

    def drain(lot):
        for copy in core_copies(lot):
            copy.wait_send()
        for copy in z_copies(lot):
            copy.wait_send()
        x_copy(lot).wait_send()
        for copy in ag_copies(lot, False):
            copy.wait_send()
        fin_copy(lot, core).wait_send()

        @pl.when(z != owner_z[lot])
        def _():
            d_copy(lot, 0, z_mate(1)).wait_send()

        @pl.when(z == owner_z[lot])
        def _():
            for step in order:
                agd_copy(lot, step).wait_send()

    pack(0, m0, dot_pieces(r_parts, q_parts, TN))
    for copy in core_copies(0):
        copy.start()
    part_w = local(q_parts)
    for copy in core_copies(0):
        copy.wait_recv()
    core_sum(0)
    z_start(0)
    m2 = dot_pieces(q_parts, q_parts, TN)
    for copy in halos[2]:
        copy.wait_recv()
    m3 = dot_pieces(q_parts, pieces(part_w - coupled(2), 3), TN)
    pack(1, m2, m3)
    for copy in core_copies(1):
        copy.start()
    for copy in core_copies(1):
        copy.wait_recv()
    core_sum(1)
    z_start(1)
    z_sum(0)
    x_sum(0)
    z_sum(1)
    x_sum(1)
    ag_finish(0)
    ag_finish(1)
    finish(0)
    finish(1)
    for stage in halos:
        for copy in stage:
            copy.wait_send()
    drain(0)
    drain(1)


def moments(diagonal, edge_ends, edge_cond, bnd_nodes, bnd_cond, hyd_ids, warm_start, n_net):
    nz = n_net // 4
    nodes, cols = warm_start.shape
    rim = bnd_nodes.shape[2]
    chunk = cols // 2 // nz
    dma = pltpu.SemaphoreType.DMA
    vmem = pl.BlockSpec(memory_space=pltpu.VMEM)
    return pl.pallas_call(
        functools.partial(moments_kernel, nz),
        name="moments",
        out_shape=[
            jax.ShapeDtypeStruct((nodes, cols), F32),
            jax.ShapeDtypeStruct((nodes, cols), F32),
            jax.ShapeDtypeStruct((2, cols, cols), F32),
            jax.ShapeDtypeStruct((2, 8, cols), F32),
        ],
        in_specs=[vmem] * 7,
        out_specs=[vmem] * 4,
        scratch_shapes=[
            pltpu.VMEM((nodes, nodes), F32),
            pltpu.VMEM((3, 2 * rim, cols), F32),
            pltpu.VMEM((3, 2 * rim, cols), F32),
            pltpu.VMEM((2, cols, cols), F32),
            pltpu.VMEM((2, 8, cols), F32),
            pltpu.VMEM((2, cols // 2, cols), F32),
            pltpu.VMEM((2, 8, cols), F32),
            pltpu.VMEM((2, cols // 2, cols), F32),
            pltpu.VMEM((2, 8, cols), F32),
            pltpu.VMEM((2, nz - 1, chunk, cols), F32),
            pltpu.VMEM((2, nz - 1, 8, cols), F32),
            pltpu.VMEM((2, chunk + 8, cols), F32),
            pltpu.VMEM((2, chunk + 8, cols), F32),
            dma((6,)),
            dma((6,)),
            dma((4,)),
            dma((4,)),
            dma((2, nz)),
            dma((2, 2 * nz - 2)),
            dma((2,)),
            dma((2,)),
            dma((2, 2 * nz - 2)),
            dma((2, nz)),
            dma((2,)),
            dma((2,)),
        ],
        compiler_params=pltpu.CompilerParams(
            collective_id=0, has_side_effects=True, vmem_limit_bytes=48 << 20
        ),
    )(
        diagonal[None, :],
        edge_ends.T,
        edge_cond[None, :],
        bnd_nodes[0],
        bnd_cond[0],
        hyd_ids[None, :],
        warm_start,
    )


def update_kernel(x_ref, r_ref, q_ref, t_ref, d_ref, out_ref, inv_ref):
    size = t_ref.shape[1]
    row = lax.broadcasted_iota(jnp.int32, (size, size), 0)
    col = lax.broadcasted_iota(jnp.int32, (size, size), 1)
    eye = (row == col).astype(F32)

    def unpack(lot):
        packed = t_ref[lot]
        upper = jnp.where(row < col, packed, 0.0)
        lower = jnp.where(row > col, packed, 0.0)
        first = jnp.where(row <= col, packed, 0.0) + upper.T
        second = lower + lower.T + eye * d_ref[lot, 0:1, :]
        return first, second

    def inverse(matrix):
        diag = eye * matrix
        by_row = lax.rsqrt(jnp.sum(diag, axis=1, keepdims=True))
        by_col = lax.rsqrt(jnp.sum(diag, axis=0, keepdims=True))
        scaled = matrix * by_row * by_col
        bound = jnp.max(jnp.sum(jnp.abs(scaled), axis=0, keepdims=True), axis=1, keepdims=True)
        gain = 2.0 / bound
        start = eye * gain
        error = eye - scaled * gain
        approx = start + error * gain
        for _ in range(5):
            error = dot_one(error, error)
            approx = approx + dot_one(approx, error)
        rest = eye - dot_full(scaled, approx)
        size_of = jnp.sum(rest * rest)
        good = size_of < 0.25
        inv_ref[...] = jnp.where(good, approx + dot_full(approx, rest), start)

        def unfinished(state):
            step, size_of = state
            return jnp.logical_and(step < 64, jnp.logical_not(size_of < 1e-6))

        def improve(state):
            approx = inv_ref[...]
            rest = eye - dot_full(scaled, approx)
            inv_ref[...] = approx + dot_full(approx, rest)
            return state[0] + 1, jnp.sum(rest * rest)

        lax.while_loop(unfinished, improve, (jnp.int32(0), size_of))
        return inv_ref[...] * by_row * by_col

    m0, m1 = unpack(0)
    m2, m3 = unpack(1)
    inv1 = inverse(m1)
    alpha = dot_full(inv1, m0)
    cross = dot_full(inv1, m2)
    schur = m3 - dot_full(m2, cross)
    rhs = m1 - dot_full(m2, alpha)
    weight_q = dot_full(inverse(schur), rhs)
    weight_r = alpha - dot_full(cross, weight_q)
    out_ref[...] = (
        x_ref[...]
        + dot_pieces(pieces(r_ref[...], 3), pieces(weight_r, 3), NN)
        + dot_pieces(pieces(q_ref[...], 3), pieces(weight_q, 3), NN)
    )


def update(warm_start, residual, image, packed, diagonals):
    cols = warm_start.shape[1]
    vmem = pl.BlockSpec(memory_space=pltpu.VMEM)
    return pl.pallas_call(
        update_kernel,
        name="update",
        out_shape=jax.ShapeDtypeStruct(warm_start.shape, F32),
        in_specs=[vmem] * 5,
        out_specs=vmem,
        scratch_shapes=[pltpu.VMEM((cols, cols), F32)],
        compiler_params=pltpu.CompilerParams(vmem_limit_bytes=48 << 20),
    )(warm_start, residual, image, packed, diagonals)


def heads_kernel(
    groups, x_ref, picks_in, flows_in, out_ref, src, dst, ss, rs, picks_ref, flows_ref, in_sem
):
    nodes, cols = x_ref.shape
    scen = out_ref.shape[0]
    hyd = lax.axis_index("hyd")
    order = sorted(range(1, groups), key=lambda s: -min(s % 4, 4 - s % 4) - 2 * (s >= 4))
    order = order[: groups - 1]

    def mate(step):
        return lax.rem(hyd + step, groups)

    barrier = pltpu.get_barrier_semaphore()
    for step in order:
        pl.semaphore_signal(barrier, inc=1, device_id={"hyd": mate(step)}, device_id_type=MESH)

    loads = [
        pltpu.make_async_copy(picks_in, picks_ref, in_sem.at[0]),
        pltpu.make_async_copy(flows_in, flows_ref, in_sem.at[1]),
    ]
    for load in loads:
        load.start()
    x_parts = pieces(x_ref[...], 3)
    column = lax.broadcasted_iota(jnp.int32, (cols, scen), 0) + hyd * cols
    for load in loads:
        load.wait()

    def scenario(owner):
        lanes = pl.ds(pl.multiple_of(owner * scen, scen), scen)
        picks, flows = picks_ref[:, lanes], flows_ref[:, lanes]
        total = jnp.zeros((cols, scen), F32)
        for slot in range(PICK):
            total = total + jnp.where(
                column == picks[slot : slot + 1, :], flows[slot : slot + 1, :], 0.0
            )
        return total

    def copy(step):
        return pltpu.make_async_remote_copy(
            src_ref=src.at[step],
            dst_ref=dst.at[step],
            send_sem=ss.at[step],
            recv_sem=rs.at[step],
            device_id={"hyd": mate(step)},
            device_id_type=MESH,
        )

    every = order + [0]
    waited = False
    for at in range(0, len(every), 2):
        pair = every[at : at + 2]
        block = jnp.concatenate([scenario(mate(step)) for step in pair], axis=1)
        both = dot_pieces(x_parts, pieces(block, 3), NN)
        for i, step in enumerate(pair):
            src[step] = both[:, i * scen : (i + 1) * scen]
        if not waited:
            pl.semaphore_wait(barrier, len(order))
            waited = True
        for step in pair:
            if step:
                copy(step).start()
    total = src[0]
    for step in order:
        copy(step).wait_recv()
    for step in order:
        total = total + dst[step]
    out_ref[...] = total.T
    for step in order:
        copy(step).wait_send()


def heads_of(responses, picks, flows, groups):
    nodes, cols = responses.shape
    scen = picks.shape[0] // groups
    dma = pltpu.SemaphoreType.DMA
    vmem = pl.BlockSpec(memory_space=pltpu.VMEM)
    return pl.pallas_call(
        functools.partial(heads_kernel, groups),
        name="heads",
        out_shape=jax.ShapeDtypeStruct((scen, nodes), F32),
        in_specs=[vmem] + [pl.BlockSpec(memory_space=pltpu.HBM)] * 2,
        out_specs=vmem,
        scratch_shapes=[
            pltpu.VMEM((groups, nodes, scen), F32),
            pltpu.VMEM((groups, nodes, scen), F32),
            dma((groups,)),
            dma((groups,)),
            pltpu.VMEM((PICK, scen * groups), jnp.int32),
            pltpu.VMEM((PICK, scen * groups), F32),
            dma((2,)),
        ],
        compiler_params=pltpu.CompilerParams(
            collective_id=1, has_side_effects=True, vmem_limit_bytes=48 << 20
        ),
    )(responses, picks.T, flows.T)


def fused_kernel(
    nz,
    groups,
    diag_in,
    ends_in,
    cond_in,
    bn_in,
    bc_in,
    hid_in,
    x_in,
    picks_in,
    flows_in,
    resp_ref,
    heads_ref,
    flag_ref,
    diag_ref,
    ends_ref,
    cond_ref,
    bn_ref,
    bc_ref,
    hid_ref,
    x_ref,
    picks_ref,
    flows_ref,
    r_ref,
    q_ref,
    a_ref,
    halo_src,
    halo_dst,
    t_buf,
    d_buf,
    core_t,
    core_d,
    cross_t,
    acc_t,
    acc_d,
    share_t,
    share_dd,
    t_all,
    d_all,
    part,
    mid_a,
    fin_a,
    mid_b,
    fin_b,
    in_sem,
    know,
    halo_ss,
    halo_rs,
    core_ss,
    core_rs,
    cd_ss,
    cd_rs,
    sh_ss,
    sh_rs,
    sd_ss,
    sd_rs,
    ag_ss,
    ag_rs,
    ad_ss,
    ad_rs,
    last_ss,
    last_rs,
    cr_ss,
    cr_rs,
    ca_ss,
    ca_rs,
    a1_ss,
    a1_rs,
    a2_ss,
    a2_rs,
    b1_ss,
    b1_rs,
    b2_ss,
    b2_rs,
):
    nodes, cols = x_ref.shape
    edges = ends_ref.shape[1]
    rim = bn_ref.shape[1]
    scen = heads_ref.shape[0]
    ny = groups // 2
    n_net = 4 * nz
    net = lax.axis_index("net")
    hyd = lax.axis_index("hyd")
    z = net // 4
    x_lo = lax.rem(net // 2, 2)
    core = lax.rem(net, 2)
    x_hi = hyd // ny
    y = lax.rem(hyd, ny)
    up, down = lax.rem(net + 1, n_net), lax.rem(net + n_net - 1, n_net)
    core_mate = net + 1 - 2 * core
    half = cols // 2

    def net_mate(key):
        return lax.rem(net + 4 * (key // 2) + (key % 2) * (2 - 4 * x_lo) + n_net, n_net)

    def z_mate(step):
        return lax.rem(net + 4 * step + n_net, n_net)

    def y_mate(step):
        return x_hi * ny + lax.rem(y + step, ny)

    hi_mate = (1 - x_hi) * ny + y

    keys = sorted(range(1, 2 * nz), key=lambda k: -min(k // 2, nz - k // 2))
    steps = sorted(range(nz), key=lambda s: -min(s, nz - s))
    near = [1] + ([2, 3, 2 * nz - 2, 2 * nz - 1] if nz > 2 else [2, 3])
    rounds = []
    reach = 1
    while 2 * reach <= nz // 2:
        rounds.append(reach)
        reach *= 2

    barrier = pltpu.get_barrier_semaphore()
    mates = [{"net": net_mate(k)} for k in near] + [{"net": up}, {"net": down}]
    mates += [{"hyd": hi_mate}] + [{"hyd": y_mate(s)} for s in range(1, ny)]
    for mate in mates:
        pl.semaphore_signal(barrier, inc=1, device_id=mate, device_id_type=MESH)

    loads = [
        pltpu.make_async_copy(whole, place, in_sem.at[at])
        for at, (whole, place) in enumerate(
            [
                (x_in, x_ref),
                (bn_in, bn_ref),
                (bc_in, bc_ref),
                (ends_in, ends_ref),
                (cond_in, cond_ref),
                (diag_in, diag_ref),
                (hid_in, hid_ref),
                (picks_in, picks_ref),
                (flows_in, flows_ref),
            ]
        )
    ]
    for load in loads:
        load.start()

    def learn(at):
        for step in (rounds[at], nz - rounds[at]):
            pl.semaphore_signal(
                know.at[at], inc=1, device_id={"net": z_mate(step)}, device_id_type=MESH
            )

    def learned(at):
        pl.semaphore_wait(know.at[at], 2)

    def remote(src, dst, ss, rs, mate):
        return pltpu.make_async_remote_copy(
            src_ref=src,
            dst_ref=dst,
            send_sem=ss,
            recv_sem=rs,
            device_id=mate if isinstance(mate, dict) else {"net": mate},
            device_id_type=MESH,
        )

    def gather(parts, stage):
        halo_src[stage] = dot_pieces(pick_b, parts, TN)

    for load in loads[:3]:
        load.wait()
    ids = jnp.concatenate([bn_ref[0:1, :], bn_ref[1:2, :]], axis=1)
    conds = jnp.concatenate([bc_ref[0:1, :], bc_ref[1:2, :]], axis=1)
    pick = (lax.broadcasted_iota(jnp.int32, (nodes, 2 * rim), 0) == ids).astype(F32)
    pick_b = [pick.astype(BF16)]
    couple = pieces(pick * conds, 3)
    x_parts = pieces(x_ref[...], 3)
    gather(x_parts, 0)
    for load in loads[3:]:
        load.wait()

    pl.semaphore_wait(barrier, len(mates))

    def build():
        node_iota = lax.broadcasted_iota(jnp.int32, (nodes, edges), 0)
        first = node_iota == ends_ref[0:1, :]
        second = node_iota == ends_ref[1:2, :]
        incidence = first.astype(F32) - second.astype(F32)
        incidence_b = incidence.astype(BF16)
        weights = jnp.concatenate(
            [cond_ref[i : i + 1, :] for i in range(cond_ref.shape[0])], axis=1
        )
        total = None
        for part_c in reversed(pieces(weights, 3)):
            term = lax.dot_general(
                (incidence * part_c.astype(F32)).astype(BF16),
                incidence_b,
                NT,
                preferred_element_type=F32,
            )
            total = term if total is None else total + term
        for part_c in reversed(pieces(conds, 3)):
            total = total + lax.dot_general(
                (pick * part_c.astype(F32)).astype(BF16),
                pick_b[0],
                NT,
                preferred_element_type=F32,
            )
        square = lax.broadcasted_iota(jnp.int32, (nodes, nodes), 0) == lax.broadcasted_iota(
            jnp.int32, (nodes, nodes), 1
        )
        a_ref[...] = total + jnp.where(square, diag_ref[...], 0.0)

    def halo(stage):
        upper, lower = pl.ds(rim, rim), pl.ds(0, rim)
        at = 2 * stage
        return [
            remote(
                halo_src.at[stage, upper],
                halo_dst.at[stage, lower],
                halo_ss.at[at],
                halo_rs.at[at],
                up,
            ),
            remote(
                halo_src.at[stage, lower],
                halo_dst.at[stage, upper],
                halo_ss.at[at + 1],
                halo_rs.at[at + 1],
                down,
            ),
        ]

    def local(parts):
        return dot_pieces(pieces(a_ref[...], 3), parts, NN)

    def coupled(stage):
        return dot_pieces(couple, pieces(halo_dst[stage], 3), NN)

    tri_row = lax.broadcasted_iota(jnp.int32, (half, half), 0)
    tri_col = lax.broadcasted_iota(jnp.int32, (half, half), 1)
    half_eye = (tri_row == tri_col).astype(F32)
    base = [half * lot for lot in range(4)]
    rows_of = [half // 2] * 4
    spot_rows = [2 * rows // nz for rows in rows_of]

    def pack(place, matrix):
        folded = jnp.where(tri_row <= tri_col, matrix[:half, :half], matrix[half:, half:])
        t_buf[place : place + half, 0:half] = folded
        t_buf[place : place + half, half:cols] = matrix[:half, half:]
        return jnp.sum(half_eye * matrix[half:, half:], axis=0, keepdims=True)

    def unpack(place, diagonal):
        folded, cross = t_all[place : place + half, 0:half], t_all[place : place + half, half:cols]
        upper = jnp.where(tri_row < tri_col, folded, 0.0)
        lower = jnp.where(tri_row > tri_col, folded, 0.0)
        first = jnp.where(tri_row <= tri_col, folded, 0.0) + upper.T
        second = lower + lower.T + half_eye * diagonal
        return jnp.concatenate(
            [
                jnp.concatenate([first, cross], axis=1),
                jnp.concatenate([cross.T, second], axis=1),
            ],
            axis=0,
        )

    def lot_rows(lot, whose):
        rows = rows_of[lot]
        return pl.ds(pl.multiple_of(base[lot] + whose * rows, rows), rows)

    def own_rows(lot):
        return pl.ds(base[lot] // 2, rows_of[lot])

    def core_copy(lot):
        return remote(
            t_buf.at[lot_rows(lot, 1 - core)],
            core_t.at[own_rows(lot)],
            core_ss.at[lot],
            core_rs.at[lot],
            core_mate,
        )

    def core_sum(lot):
        core_copy(lot).wait_recv()
        acc_t[own_rows(lot)] = t_buf[lot_rows(lot, core)] + core_t[own_rows(lot)]

    def core_d_copy(at):
        return remote(d_buf.at[at], core_d.at[at], cd_ss.at[at], cd_rs.at[at], core_mate)

    def core_d_sum(at):
        core_d_copy(at).wait_recv()
        acc_d[at] = d_buf[at] + core_d[at]

    mine = x_lo == lax.rem(z, 2)

    def spot(lot, zc, start):
        rows = spot_rows[lot]
        return (
            pl.ds(pl.multiple_of(start + (zc // 2) * rows, rows), rows),
            pl.ds(pl.multiple_of(lax.rem(zc, 2) * half, half), half),
        )

    x_mate = net + 2 - 4 * x_lo
    own_lanes = pl.ds(pl.multiple_of(x_lo * half, half), half)
    far_lanes = pl.ds(pl.multiple_of((1 - x_lo) * half, half), half)
    odd = lax.rem(x_lo + z, 2)

    def cross_copy(lot):
        return remote(
            acc_t.at[own_rows(lot), far_lanes],
            cross_t.at[own_rows(lot)],
            cr_ss.at[lot],
            cr_rs.at[lot],
            x_mate,
        )

    def cross_start(lot):
        if lot in CROSS_FIRST:
            cross_copy(lot).start()

    def cross_sum(lot):
        if lot in CROSS_FIRST:
            cross_copy(lot).wait_recv()
            acc_t[own_rows(lot), own_lanes] = (
                acc_t[own_rows(lot), own_lanes] + cross_t[own_rows(lot)]
            )

    def share_copy(lot, step):
        zc = lax.rem(z + step, nz)
        if lot in CROSS_FIRST:
            slot = step - 1
        else:
            slot = 2 * step - 1 + (lax.rem(x_lo + zc, 2) if step else 1)
        rows, lanes = spot(lot, zc, base[lot] // 2)
        return remote(
            acc_t.at[rows, lanes],
            share_t.at[lot, slot, pl.ds(0, spot_rows[lot])],
            sh_ss.at[lot, step],
            sh_rs.at[lot, slot],
            4 * zc + 2 * lax.rem(zc, 2) + core,
        )

    def share_slots(lot):
        return nz - 1 if lot in CROSS_FIRST else 2 * nz - 1

    def share_arrival(lot, slot):
        rows, lanes = spot(lot, z, base[lot] // 2)
        return remote(
            acc_t.at[rows, lanes],
            share_t.at[lot, slot, pl.ds(0, spot_rows[lot])],
            sh_ss.at[lot, 0],
            sh_rs.at[lot, slot],
            core_mate,
        )

    def share_each(lot, act):
        if lot in CROSS_FIRST:
            for step in sorted(range(2, nz, 2), key=lambda s: -min(s, nz - s)):
                act(share_copy(lot, step + odd))
        else:
            for step in steps:
                if step:
                    act(share_copy(lot, step))

        @pl.when(jnp.logical_not(mine))
        def _():
            act(share_copy(lot, 1 if lot in CROSS_FIRST else 0))

    def share_start(lot):
        share_each(lot, lambda copy: copy.start())

    def all_spot(lot, zc):
        return spot(lot, zc, base[lot] + core * rows_of[lot])

    def all_copy(lot, zc, key):
        rows, lanes = all_spot(lot, zc)
        return remote(
            t_all.at[rows, lanes],
            t_all.at[rows, lanes],
            ag_ss.at[lot, key - 1],
            ag_rs.at[lot, zc],
            net_mate(key),
        )

    def all_keys(lot):
        return [key for key in keys if key % 2 == 0 or lot not in CROSS_LAST]

    def share_sum(lot):
        @pl.when(mine)
        def _():
            for slot in range(share_slots(lot)):
                share_arrival(lot, slot).wait_recv()
            rows, lanes = spot(lot, z, base[lot] // 2)
            total = acc_t[rows, lanes]
            for slot in range(share_slots(lot)):
                total = total + share_t[lot, slot, 0 : spot_rows[lot]]
            rows, lanes = all_spot(lot, z)
            t_all[rows, lanes] = total
            for key in all_keys(lot):
                all_copy(lot, z, key).start()

    owner_z = [nz // 4, (3 * nz) // 4]

    def is_owner(at):
        return jnp.logical_and(z == owner_z[at], x_lo == 0)

    def share_d(at, slot, mate):
        return remote(
            acc_d.at[at], share_dd.at[at, slot], sd_ss.at[at], sd_rs.at[at, slot], mate
        )

    def all_d(at, key):
        return remote(
            d_all.at[at], d_all.at[at], ad_ss.at[at, key - 1], ad_rs.at[at], net_mate(key)
        )

    def share_d_start(at):
        @pl.when(jnp.logical_not(is_owner(at)))
        def _():
            slot = 2 * lax.rem(owner_z[at] - z + nz, nz) + x_lo - 1
            share_d(at, slot, 4 * owner_z[at] + core).start()

    def share_d_sum(at):
        @pl.when(is_owner(at))
        def _():
            total_d = acc_d[at]
            for slot in range(2 * nz - 1):
                share_d(at, slot, core_mate).wait_recv()
            for slot in range(2 * nz - 1):
                total_d = total_d + share_dd[at, slot]
            d_all[at] = total_d
            for key in keys:
                all_d(at, key).start()

    def all_d_finish(at):
        @pl.when(jnp.logical_not(is_owner(at)))
        def _():
            all_d(at, 1).wait_recv()

    def last_copy(lot, whose):
        return remote(
            t_all.at[lot_rows(lot, whose)],
            t_all.at[lot_rows(lot, whose)],
            last_ss.at[lot],
            last_rs.at[lot],
            core_mate,
        )

    def level_copy(lot, lanes):
        rows = lot_rows(lot, core)
        return remote(
            t_all.at[rows, lanes], t_all.at[rows, lanes], ca_ss.at[lot], ca_rs.at[lot], x_mate
        )

    def all_finish(lot):
        if lot in CROSS_LAST:
            for step in range(2, nz, 2):
                all_copy(lot, lax.rem(z + step + odd, nz), 1).wait_recv()
        else:
            for step in range(1, nz):
                all_copy(lot, lax.rem(z + step, nz), 1).wait_recv()

        @pl.when(jnp.logical_not(mine))
        def _():
            zc = lax.rem(z + 1, nz) if lot in CROSS_LAST else z
            all_copy(lot, zc, 1).wait_recv()

        if lot in CROSS_LAST:
            level_copy(lot, own_lanes).start()
        else:
            last_copy(lot, core).start()

    def level(lot):
        if lot in CROSS_LAST:
            level_copy(lot, far_lanes).wait_recv()
            last_copy(lot, core).start()

    def drain(lot):
        core_copy(lot).wait_send()
        share_each(lot, lambda copy: copy.wait_send())
        if lot in CROSS_FIRST:
            cross_copy(lot).wait_send()
        if lot in CROSS_LAST:
            level_copy(lot, own_lanes).wait_send()

        @pl.when(mine)
        def _():
            for key in all_keys(lot):
                all_copy(lot, z, key).wait_send()

        last_copy(lot, core).wait_send()

    def drain_d(at):
        core_d_copy(at).wait_send()

        @pl.when(jnp.logical_not(is_owner(at)))
        def _():
            share_d(at, 0, core_mate).wait_send()

        @pl.when(is_owner(at))
        def _():
            for key in keys:
                all_d(at, key).wait_send()

    halos = [halo(stage) for stage in range(3)]
    for copy in halos[0]:
        copy.start()
    if rounds:
        learn(0)
    build()
    hyd_local = hid_ref[...] - net * nodes
    demand = (lax.broadcasted_iota(jnp.int32, (nodes, cols), 0) == hyd_local).astype(F32)
    part_r = demand - local(x_parts)
    if rounds:
        learned(0)
        if len(rounds) > 1:
            learn(1)
    for copy in halos[0]:
        copy.wait_recv()
    residual = part_r + coupled(0)
    r_parts = pieces(residual, 3)
    gather(r_parts, 1)
    for copy in halos[1]:
        copy.start()
    r_ref[...] = residual
    d0 = pack(base[0], dot_pieces(r_parts, r_parts, TN))
    core_copy(0).start()
    if len(rounds) > 1:
        learned(1)
        if len(rounds) > 2:
            learn(2)
    part_q = local(r_parts)
    core_sum(0)
    cross_start(0)
    for copy in halos[1]:
        copy.wait_recv()
    image = part_q - coupled(1)
    q_parts = pieces(image, 3)
    gather(q_parts, 2)
    for copy in halos[2]:
        copy.start()
    q_ref[...] = image
    for at in range(2, len(rounds)):
        learned(at)
        if at + 1 < len(rounds):
            learn(at + 1)
    cross_sum(0)
    share_start(0)
    d1 = pack(base[1], dot_pieces(r_parts, q_parts, TN))
    core_copy(1).start()
    d2 = pack(base[2], dot_pieces(q_parts, q_parts, TN))
    d_buf[0] = jnp.concatenate([d0, d1, d2, jnp.zeros((5, half), F32)], axis=0)
    core_copy(2).start()
    core_d_copy(0).start()
    core_sum(1)
    share_start(1)
    part_w = local(q_parts)
    core_sum(2)
    cross_start(2)
    if 2 not in CROSS_FIRST:
        share_start(2)
    core_d_sum(0)
    share_d_start(0)
    for copy in halos[2]:
        copy.wait_recv()
    d3 = pack(base[3], dot_pieces(q_parts, pieces(part_w - coupled(2), 3), TN))
    d_buf[1] = jnp.broadcast_to(d3, (8, half))
    core_copy(3).start()
    core_d_copy(1).start()
    if 2 in CROSS_FIRST:
        cross_sum(2)
        share_start(2)
    core_sum(3)
    share_start(3)
    core_d_sum(1)
    share_d_start(1)
    share_sum(0)
    share_sum(1)
    share_d_sum(0)
    share_sum(2)
    share_sum(3)
    share_d_sum(1)
    all_finish(0)
    level(0)
    all_finish(1)
    all_d_finish(0)
    last_copy(0, 1 - core).wait_recv()
    last_copy(1, 1 - core).wait_recv()

    row = lax.broadcasted_iota(jnp.int32, (cols, cols), 0)
    col = lax.broadcasted_iota(jnp.int32, (cols, cols), 1)
    eye = (row == col).astype(F32)

    def inverse(matrix):
        diag = eye * matrix
        by_row = lax.rsqrt(jnp.sum(diag, axis=1, keepdims=True))
        by_col = lax.rsqrt(jnp.sum(diag, axis=0, keepdims=True))
        scaled = matrix * by_row * by_col
        bound = jnp.max(jnp.sum(jnp.abs(scaled), axis=0, keepdims=True), axis=1, keepdims=True)
        gain = 2.0 / bound
        error = eye - scaled * gain
        approx = eye * gain + error * gain
        for _ in range(5):
            error = dot_one(error, error)
            approx = approx + dot_one(approx, error)
        approx = approx + dot_one(approx, eye - dot_full(scaled, approx))
        rest = eye - dot_full(scaled, approx)
        approx = approx + dot_one(approx, rest)
        left = jnp.sum(jnp.sum(rest * rest, axis=0, keepdims=True), axis=1, keepdims=True)
        return approx * by_row * by_col, left

    m0 = unpack(base[0], d_all[0, 0:1, :])
    m1 = unpack(base[1], d_all[0, 1:2, :])
    inv1, left1 = inverse(m1)
    all_finish(2)
    alpha = dot_full(inv1, m0)
    level(2)
    all_finish(3)
    last_copy(2, 1 - core).wait_recv()
    m2 = unpack(base[2], d_all[0, 2:3, :])
    cross = dot_full(inv1, m2)
    rhs = m1 - dot_full(m2, alpha)
    fill = dot_full(m2, cross)
    all_d_finish(1)
    last_copy(3, 1 - core).wait_recv()
    inv2, left2 = inverse(unpack(base[3], d_all[1, 0:1, :]) - fill)
    weight_q = dot_full(inv2, rhs)
    weight_r = alpha - dot_full(cross, weight_q)
    converged = jnp.logical_and(left1 < 2e-5, left2 < 2e-5)
    flag = jnp.broadcast_to(jnp.where(converged, 0.0, 1.0), (8, scen))
    answer = (
        x_ref[...]
        + dot_pieces(pieces(r_ref[...], 2), pieces(weight_r, 2), NN)
        + dot_pieces(pieces(q_ref[...], 2), pieces(weight_q, 2), NN)
    )
    resp_ref[...] = answer
    a_parts = pieces(answer, 2)
    column = lax.broadcasted_iota(jnp.int32, (cols, scen), 0) + hyd * cols

    def scenario(owner):
        lanes = pl.ds(pl.multiple_of(owner * scen, scen), scen)
        picks, flows = picks_ref[:, lanes], flows_ref[:, lanes]
        total = jnp.zeros((cols, scen), F32)
        for slot in range(PICK):
            total = total + jnp.where(
                column == picks[slot : slot + 1, :], flows[slot : slot + 1, :], 0.0
            )
        return total

    deep = mid_a.shape[1]
    rows_a, rows_b = pl.ds(0, deep), pl.ds(deep, part.shape[1] - deep)

    def a1_copy(dy):
        return remote(
            part.at[ny + dy, rows_a], mid_a.at[dy], a1_ss.at[dy], a1_rs.at[dy], {"hyd": hi_mate}
        )

    def a2_copy(dy):
        return remote(
            part.at[dy, rows_a],
            fin_a.at[dy - 1],
            a2_ss.at[dy - 1],
            a2_rs.at[dy - 1],
            {"hyd": y_mate(dy)},
        )

    def b1_copy(fx, dy):
        return remote(
            part.at[fx * ny + dy, rows_b],
            mid_b.at[fx, dy - 1],
            b1_ss.at[fx, dy - 1],
            b1_rs.at[fx, dy - 1],
            {"hyd": y_mate(dy)},
        )

    def b2_copy():
        return remote(part.at[ny, rows_b], fin_b, b2_ss.at[0], b2_rs.at[0], {"hyd": hi_mate})

    order = sorted(range(1, ny), key=lambda s: -min(s, ny - s)) + [0]
    every = [(1, dy) for dy in order] + [(0, dy) for dy in order]
    for at in range(0, groups, 2):
        pair = every[at : at + 2]
        block = jnp.concatenate(
            [scenario((x_hi if fx == 0 else 1 - x_hi) * ny + lax.rem(y + dy, ny)) for fx, dy in pair],
            axis=1,
        )
        both = dot_pieces(a_parts, pieces(block, 2), NN)
        for i, (fx, dy) in enumerate(pair):
            part[fx * ny + dy, 0:8] = flag
            part[fx * ny + dy, 8 : nodes + 8] = both[:, i * scen : (i + 1) * scen]
            if fx:
                a1_copy(dy).start()
            if dy:
                b1_copy(fx, dy).start()

    def a_step(dy):
        a1_copy(dy).wait_recv()
        part[dy, rows_a] = part[dy, rows_a] + mid_a[dy]
        if dy:
            a2_copy(dy).start()

    half_way = (len(order) - 1) // 2 + 1
    for dy in order[:half_way]:
        a_step(dy)
    total_b = part[ny, rows_b]
    for dy in range(1, ny):
        b1_copy(1, dy).wait_recv()
        total_b = total_b + mid_b[1, dy - 1]
    part[ny, rows_b] = total_b
    b2_copy().start()
    for dy in order[half_way:]:
        a_step(dy)
    for stage in halos:
        for copy in stage:
            copy.wait_send()
    for lot in range(4):
        drain(lot)
    drain_d(0)
    drain_d(1)
    total_b = part[0, rows_b]
    for dy in range(1, ny):
        b1_copy(0, dy).wait_recv()
        total_b = total_b + mid_b[0, dy - 1]
    b2_copy().wait_recv()
    total_b = total_b + fin_b[...]
    total_a = part[0, rows_a]
    for dy in order[:-1]:
        a2_copy(dy).wait_recv()
        total_a = total_a + fin_a[dy - 1]
    flag_ref[0, 0] = jnp.where(jnp.max(total_a[0:8]) > 0.0, 1, 0).astype(jnp.int32)
    heads_ref[...] = jnp.concatenate([total_a[8:], total_b], axis=0).T
    for dy in range(ny):
        a1_copy(dy).wait_send()
        if dy:
            a2_copy(dy).wait_send()
            b1_copy(0, dy).wait_send()
            b1_copy(1, dy).wait_send()
    b2_copy().wait_send()


def fused(
    diagonal,
    edge_ends,
    edge_cond,
    bnd_nodes,
    bnd_cond,
    hyd_ids,
    warm_start,
    picks,
    flows,
    n_net,
    groups,
):
    nz = n_net // 4
    ny = groups // 2
    nodes, cols = warm_start.shape
    rim = bnd_nodes.shape[2]
    edges = edge_cond.shape[0]
    scen = picks.shape[0] // groups
    half = cols // 2
    peers = 2 * nz - 1
    spot = half // nz
    deep = 8 + (nodes * SPLIT // 64) // 8 * 8
    dma = pltpu.SemaphoreType.DMA
    vmem = pl.BlockSpec(memory_space=pltpu.VMEM)
    return pl.pallas_call(
        functools.partial(fused_kernel, nz, groups),
        name="fused",
        out_shape=[
            jax.ShapeDtypeStruct((nodes, cols), F32),
            jax.ShapeDtypeStruct((scen, nodes), F32),
            jax.ShapeDtypeStruct((1, 1), jnp.int32),
        ],
        in_specs=[pl.BlockSpec(memory_space=pltpu.HBM)] * 9,
        out_specs=[vmem] * 2 + [pl.BlockSpec(memory_space=pltpu.SMEM)],
        scratch_shapes=[
            pltpu.VMEM((1, nodes), F32),
            pltpu.VMEM((2, edges), jnp.int32),
            pltpu.VMEM((edges // 128, 128), F32),
            pltpu.VMEM((2, rim), jnp.int32),
            pltpu.VMEM((2, rim), F32),
            pltpu.VMEM((1, cols), jnp.int32),
            pltpu.VMEM((nodes, cols), F32),
            pltpu.VMEM((PICK, scen * groups), jnp.int32),
            pltpu.VMEM((PICK, scen * groups), F32),
            pltpu.VMEM((nodes, cols), F32),
            pltpu.VMEM((nodes, cols), F32),
            pltpu.VMEM((nodes, nodes), F32),
            pltpu.VMEM((3, 2 * rim, cols), F32),
            pltpu.VMEM((3, 2 * rim, cols), F32),
            pltpu.VMEM((2 * cols, cols), F32),
            pltpu.VMEM((2, 8, half), F32),
            pltpu.VMEM((cols, cols), F32),
            pltpu.VMEM((2, 8, half), F32),
            pltpu.VMEM((cols, half), F32),
            pltpu.VMEM((cols, cols), F32),
            pltpu.VMEM((2, 8, half), F32),
            pltpu.VMEM((4, peers, spot, half), F32),
            pltpu.VMEM((2, peers, 8, half), F32),
            pltpu.VMEM((2 * cols, cols), F32),
            pltpu.VMEM((2, 8, half), F32),
            pltpu.VMEM((groups, nodes + 8, scen), F32),
            pltpu.VMEM((ny, deep, scen), F32),
            pltpu.VMEM((ny - 1, deep, scen), F32),
            pltpu.VMEM((2, ny - 1, nodes + 8 - deep, scen), F32),
            pltpu.VMEM((nodes + 8 - deep, scen), F32),
            dma((9,)),
            pltpu.SemaphoreType.REGULAR((3,)),
            dma((6,)),
            dma((6,)),
            dma((4,)),
            dma((4,)),
            dma((2,)),
            dma((2,)),
            dma((4, nz)),
            dma((4, peers)),
            dma((2,)),
            dma((2, peers)),
            dma((4, peers)),
            dma((4, nz)),
            dma((2, peers)),
            dma((2,)),
            dma((4,)),
            dma((4,)),
            dma((4,)),
            dma((4,)),
            dma((4,)),
            dma((4,)),
            dma((ny,)),
            dma((ny,)),
            dma((ny - 1,)),
            dma((ny - 1,)),
            dma((2, ny - 1)),
            dma((2, ny - 1)),
            dma((1,)),
            dma((1,)),
        ],
        compiler_params=pltpu.CompilerParams(
            collective_id=2, has_side_effects=True, vmem_limit_bytes=48 << 20
        ),
    )(
        diagonal[None, :],
        edge_ends.T,
        edge_cond.reshape(edges // 128, 128),
        bnd_nodes[0],
        bnd_cond[0],
        hyd_ids[None, :],
        warm_start,
        picks.T,
        flows.T,
    )


def settle_kernel(resp_in, heads_in, resp_out, heads_out, sems):
    copies = [
        pltpu.make_async_copy(resp_in, resp_out, sems.at[0]),
        pltpu.make_async_copy(heads_in, heads_out, sems.at[1]),
    ]
    for copy in copies:
        copy.start()
    for copy in copies:
        copy.wait()


def settle(responses, heads):
    anywhere = pl.BlockSpec(memory_space=pl.ANY)
    return pl.pallas_call(
        settle_kernel,
        name="settle",
        out_shape=[jax.ShapeDtypeStruct(a.shape, a.dtype) for a in (responses, heads)],
        in_specs=[anywhere] * 2,
        out_specs=[anywhere] * 2,
        scratch_shapes=[pltpu.SemaphoreType.DMA((2,))],
    )(responses, heads)


def per_device(
    diagonal, edge_ends, edge_cond, bnd_nodes, bnd_cond, hyd_ids, warm_start, scen_picks, scen_flows
):
    n_net, groups = lax.axis_size("net"), lax.axis_size("hyd")
    local = (diagonal, edge_ends, edge_cond, bnd_nodes, bnd_cond, hyd_ids, warm_start)
    responses, heads, flag = fused(*local, scen_picks, scen_flows, n_net, groups)

    def keep(responses, heads):
        return settle(responses, heads)

    def redo(responses, heads):
        residual, image, packed, diagonals = moments(*local, n_net)
        responses = update(warm_start, residual, image, packed, diagonals)
        return settle(responses, heads_of(responses, scen_picks, scen_flows, groups))

    return lax.switch(flag[0, 0], [keep, redo], responses, heads)


def solution(mesh):
    placed = (
        P("net"),
        P("net", None),
        P("net"),
        P("net", None, None),
        P("net", None, None),
        P("hyd"),
        P("net", "hyd"),
        P(),
        P(),
    )
    return jax.shard_map(
        per_device,
        mesh=mesh,
        in_specs=placed,
        out_specs=(P("net", "hyd"), P("hyd", "net")),
        check_vma=False,
    )
```
